32 devices in a mesh: parts: 2 (over y), row: 4 (over z), col: 4 (over x, core).
Axes of the slice: x: 2, y: 2, z: 4, core: 2. Of those that a mesh axis runs over, the one named last changes fastest.
Arguments:
- tokens: bfloat16 [3072, 4096], P(('parts', 'row'), 'col'), parts along dimension 0, may hold values from -6 to 6
- gate_weight: bfloat16 [4096, 14336], P('row', 'col'), may hold values from -0.09375 to 0.09375
- up_weight: bfloat16 [4096, 14336], P('row', 'col'), may hold values from -0.09375 to 0.09375
Outputs:
- hidden: bfloat16 [3072, 14336], P(('parts', 'row'), 'col'), parts along dimension 0
The draws below stay inside these ranges and needn't reach their ends.
There are 2 independent parts, one for each index of `parts`. The reference program is written for one: setup_inputs(seed, part) draws one part's arguments, and reference() takes and returns one part's arrays. A program takes and returns all parts, laid end to end along the dimension named above; an argument that names none is the same for every part. Nothing has to cross between parts.
All inputs are finite; a program needn't handle non-finite values.
Results may differ from the reference program's by a relative error of at most 0.001.
Values may be sent and summed in bfloat16 or wider, within the bound.
No kernel may reach another device: no remote copies, remote signals or barrier semaphores. Data moves between devices by JAX's collectives and lax.ppermute only.
A program may use at most 192 MiB of HBM per device.

```python
import jax
import jax.numpy as jnp

D = 4096
FF = 14336
TOKENS = 1536


def levels(rng, extent, cuts, smallest, high):
    def one(axis_at, parts):
        draws = jax.random.uniform(jax.random.fold_in(jax.random.fold_in(rng, 6), axis_at), (parts,), jnp.float32, smallest / len(cuts), high / len(cuts))
        return jnp.repeat(jnp.exp(draws), extent[axis_at] // parts).reshape((-1,) + (1,) * (len(extent) - axis_at - 1))

    level = one(*cuts[0])
    for cut in cuts[1:]:
        level = level * one(*cut)
    return level


def bell_draw(own_key, dims, scale, bound, shards=(), dtype=jnp.bfloat16):
    result = scale * jax.random.normal(own_key, dims, jnp.float32)
    if shards:
        result = result * levels(own_key, dims, shards, -0.22, 0.18)
    return jnp.clip(result, -bound, bound).astype(dtype)


def setup_inputs(seed: int = 0, part: int = 0) -> dict:
    seeds = jax.random.split(jax.random.key(seed), 4)
    part_splits = jax.random.split(jax.random.fold_in(seeds[3], part), 4)
    return {
        "tokens": bell_draw(part_splits[0], (TOKENS, D), 1.0, 6.0, ((0, 4), (1, 4))),
        "gate_weight": bell_draw(seeds[1], (D, FF), D ** -0.5, 0.09375, ((0, 4), (1, 4))),
        "up_weight": bell_draw(seeds[2], (D, FF), D ** -0.5, 0.09375, ((0, 4), (1, 4))),
    }


def reference(tokens, gate_weight, up_weight):
    gate = jnp.dot(tokens, gate_weight, preferred_element_type=jnp.float32)
    up = jnp.dot(tokens, up_weight, preferred_element_type=jnp.float32)
    return (jax.nn.silu(gate) * up).astype(jnp.bfloat16)
```

```python
import jax
import jax.numpy as jnp
from jax import lax
from jax.sharding import PartitionSpec as P

CHUNKS = 1


def cut(width, pieces):
    unit = 128 if width % 128 == 0 else width
    units = width // unit
    pieces = min(pieces, units)
    edges = [unit * (units * i // pieces) for i in range(pieces + 1)]
    return list(zip(edges[:-1], edges[1:]))


def on_device(tokens, gate_weight, up_weight):
    rows = lax.axis_size("row")
    parts = lax.axis_size("parts")
    z = lax.axis_index("row")
    y = lax.axis_index("parts")
    mine, ff = tokens.shape[0], gate_weight.shape[1]
    depth = gate_weight.shape[0]
    share = depth // parts
    width = ff // rows

    whole = lax.all_gather(lax.all_gather(tokens, "row", axis=0, tiled=True), "col", axis=1, tiled=True)

    def rotated(value, shift):
        return lax.ppermute(value, "row", [(i, (i + shift) % rows) for i in range(rows)])

    hidden = jnp.zeros((mine, ff), jnp.bfloat16)
    for low, high in cut(width, CHUNKS):
        wide = high - low
        gate = up = 0.0
        for shift in range(rows):
            to, came = (z + shift) % rows, (z - shift) % rows
            if shift == 0:
                both = [lax.dynamic_slice(w, (0, z * width + low), (depth, wide)) for w in (gate_weight, up_weight)]
            else:
                sent = jnp.stack([
                    lax.dynamic_slice(w, (y * share, to * width + low), (share, wide))
                    for w in (gate_weight, up_weight)
                ])
                both = lax.all_gather(rotated(sent, shift), "parts", axis=1, tiled=True)
            features = lax.dynamic_slice(whole, (0, came * depth), (whole.shape[0], depth))
            gate += jnp.dot(features, both[0], preferred_element_type=jnp.float32)
            up += jnp.dot(features, both[1], preferred_element_type=jnp.float32)
        done = (jax.nn.silu(gate) * up).astype(jnp.bfloat16)
        for shift in range(rows):
            to, came = (z + shift) % rows, (z - shift) % rows
            block = lax.dynamic_slice(done, (to * mine, 0), (mine, wide))
            if shift:
                block = rotated(block, shift)
            hidden = lax.dynamic_update_slice(hidden, block, (0, came * width + low))
    return hidden


def solution(mesh):
    placed = (P(("parts", "row"), "col"), P("row", "col"), P("row", "col"))
    return jax.shard_map(
        on_device, mesh=mesh, in_specs=placed, out_specs=P(("parts", "row"), "col"), check_vma=False
    )
```

```python
import jax
import jax.numpy as jnp
from jax import lax
from jax.sharding import PartitionSpec as P

PIECES = 4


def cut(width, pieces):
    unit = 128 if width % 128 == 0 else width
    units = width // unit
    pieces = min(pieces, units)
    edges = [unit * (-(-units * i // pieces)) for i in range(pieces + 1)]
    return list(zip(edges[:-1], edges[1:]))


def on_device(tokens, gate_weight, up_weight):
    rows = lax.axis_size("row")
    parts = lax.axis_size("parts")
    y = lax.axis_index("parts")
    mine, ff = tokens.shape[0], gate_weight.shape[1]
    depth = gate_weight.shape[0]
    share = depth // parts
    width = ff // rows

    whole = lax.all_gather(lax.all_gather(tokens, "row", axis=0, tiled=True), "col", axis=1, tiled=True)
    everyone = whole.shape[0]
    by_share = whole.reshape(everyone, rows, parts, share)
    features = [
        lax.dynamic_index_in_dim(by_share, (y + turn) % parts, 2, keepdims=False).reshape(everyone, rows * share)
        for turn in range(parts)
    ]
    halves = [
        lax.dynamic_slice(w, (y * share, 0), (share, ff)).reshape(share, rows, width)
        for w in (gate_weight, up_weight)
    ]

    hidden = []
    for low, high in cut(width, PIECES):
        wide = high - low
        sent = jnp.stack([h[:, :, low:high].transpose(1, 0, 2) for h in halves])
        held = lax.all_to_all(sent, "row", 1, 1, tiled=True)
        gate = up = 0.0
        for turn in range(parts):
            block = held if turn == 0 else lax.ppermute(
                held, "parts", [(i, (i - turn) % parts) for i in range(parts)]
            )
            block = block.reshape(2, rows * share, wide)
            gate += jnp.dot(features[turn], block[0], preferred_element_type=jnp.float32)
            up += jnp.dot(features[turn], block[1], preferred_element_type=jnp.float32)
        done = (jax.nn.silu(gate) * up).astype(jnp.bfloat16)
        back = lax.all_to_all(done.reshape(rows, mine, wide), "row", 0, 0, tiled=True)
        hidden.append(back)
    hidden = jnp.concatenate(hidden, axis=2)
    return hidden.transpose(1, 0, 2).reshape(mine, ff)


def solution(mesh):
    placed = (P(("parts", "row"), "col"), P("row", "col"), P("row", "col"))
    return jax.shard_map(
        on_device, mesh=mesh, in_specs=placed, out_specs=P(("parts", "row"), "col"), check_vma=False
    )
```

```python
import jax
import jax.numpy as jnp
from jax import lax
from jax.experimental import pallas as pl
from jax.experimental.pallas import tpu as pltpu
from jax.sharding import PartitionSpec as P

PIECES = (4, 3)
LANES = 128
ANY = pl.BlockSpec(memory_space=pl.ANY)


def around(size, shift):
    return [(i, (i + shift) % size) for i in range(size)]


def run_all(copies):
    for copy in copies:
        copy.start()
    for copy in copies:
        copy.wait()


def pack(gate_weight, up_weight, shift, low, wide, after):
    depth, ff = gate_weight.shape
    rows, parts = lax.axis_size("row"), lax.axis_size("parts")
    share, width, tiles = depth // parts, ff // rows, wide // LANES

    def body(*refs):
        weights, sent, sems = refs[:2], refs[-2], refs[-1]
        to = lax.rem(lax.axis_index("row") + shift, rows)
        first = pl.multiple_of(lax.axis_index("parts") * share, share)
        copies = []
        for j in range(tiles):
            start = pl.multiple_of(to * width + low + j * LANES, LANES)
            for g, weight in enumerate(weights):
                copies.append(pltpu.make_async_copy(
                    weight.at[pl.ds(first, share), pl.ds(start, LANES)],
                    sent.at[:, pl.ds((2 * j + g) * LANES, LANES)],
                    sems.at[2 * j + g],
                ))
        run_all(copies)

    size = share * 2 * wide * 2
    return pl.pallas_call(
        body,
        out_shape=jax.ShapeDtypeStruct((share, 2 * wide), gate_weight.dtype),
        in_specs=[ANY] * (2 + len(after)),
        out_specs=ANY,
        scratch_shapes=[pltpu.SemaphoreType.DMA((2 * tiles,))],
        cost_estimate=pl.CostEstimate(flops=0, bytes_accessed=2 * size, transcendentals=0),
        name="pack",
    )(gate_weight, up_weight, *after)


def hold(value, after):
    def body(*refs):
        pass

    return pl.pallas_call(
        body,
        out_shape=jax.ShapeDtypeStruct(value.shape, value.dtype),
        in_specs=[ANY] * (1 + len(after)),
        out_specs=ANY,
        input_output_aliases={0: 0},
        name="hold",
    )(value, *after)


def product(tokens, gate_weight, up_weight, held, low, wide, mine, after):
    depth, ff = gate_weight.shape
    rows, parts = lax.axis_size("row"), lax.axis_size("parts")
    share, width, tiles = depth // parts, ff // rows, wide // LANES
    features = rows * depth
    order = list(range(1, rows)) + [0]
    pieces = [(shift, turn) for shift in range(1, rows) for turn in range(parts)]

    def body(tokens_ref, gate_ref, up_ref, *refs):
        held_refs = refs[:len(pieces)]
        outs = refs[len(pieces) + len(after):][:rows]
        stack, block, sems, block_sems = refs[-4:]
        z, y = lax.axis_index("row"), lax.axis_index("parts")

        def fetch(step):
            to = lax.rem(z + order[step], rows)
            return pltpu.make_async_copy(
                tokens_ref.at[pl.ds(pl.multiple_of(to * mine, mine), mine), :],
                block.at[step % 2],
                block_sems.at[step % 2],
            )

        copies = []
        for ref, (shift, turn) in zip(held_refs, pieces):
            came = lax.rem(z + rows - shift, rows)
            half = lax.rem(y + turn, parts)
            start = pl.multiple_of(came * depth + half * share, share)
            copies.append(pltpu.make_async_copy(ref, stack.at[pl.ds(start, share), :], sems.at[len(copies)]))
        own = pl.multiple_of(z * depth, depth)
        for j in range(tiles):
            start = pl.multiple_of(z * width + low + j * LANES, LANES)
            for g, weight in enumerate((gate_ref, up_ref)):
                copies.append(pltpu.make_async_copy(
                    weight.at[:, pl.ds(start, LANES)],
                    stack.at[pl.ds(own, depth), pl.ds((2 * j + g) * LANES, LANES)],
                    sems.at[len(copies)],
                ))
        fetch(0).start()
        run_all(copies)
        for step, shift in enumerate(order):
            fetch(step).wait()
            if step + 1 < rows:
                fetch(step + 1).start()

            def tile(j, carry, step=step, shift=shift):
                both = jnp.dot(
                    block[step % 2],
                    stack[:, pl.ds(pl.multiple_of(j * 2 * LANES, 2 * LANES), 2 * LANES)],
                    preferred_element_type=jnp.float32,
                )
                gate, up = both[:, :LANES], both[:, LANES:]
                outs[shift][:, pl.ds(pl.multiple_of(j * LANES, LANES), LANES)] = (
                    jax.nn.silu(gate) * up
                ).astype(jnp.bfloat16)
                return carry

            lax.fori_loop(0, tiles, tile, 0)

    moved = 2 * (rows * mine * features + features * 2 * wide + rows * mine * wide)
    return pl.pallas_call(
        body,
        out_shape=[jax.ShapeDtypeStruct((mine, wide), jnp.bfloat16)] * rows,
        in_specs=[ANY] * (3 + len(pieces) + len(after)),
        out_specs=[pl.BlockSpec(memory_space=pltpu.VMEM)] * rows,
        scratch_shapes=[
            pltpu.VMEM((features, 2 * wide), gate_weight.dtype),
            pltpu.VMEM((2, mine, features), tokens.dtype),
            pltpu.SemaphoreType.DMA((len(pieces) + 2 * tiles,)),
            pltpu.SemaphoreType.DMA((2,)),
        ],
        compiler_params=pltpu.CompilerParams(vmem_limit_bytes=32 * 2**20),
        cost_estimate=pl.CostEstimate(
            flops=4 * rows * mine * features * wide, bytes_accessed=moved, transcendentals=rows * mine * wide
        ),
        name="product",
    )(tokens, gate_weight, up_weight, *held, *after)


def place(blocks, mine, ff):
    rows = lax.axis_size("row")
    width = ff // rows

    def body(*refs):
        out, sems = refs[-2], refs[-1]
        z = lax.axis_index("row")
        copies = []
        for ref, (shift, low, value) in zip(refs, blocks):
            came = lax.rem(z + rows - shift, rows)
            start = pl.multiple_of(came * width + low, LANES)
            copies.append(pltpu.make_async_copy(
                ref, out.at[:, pl.ds(start, value.shape[1])], sems.at[len(copies)]
            ))
        run_all(copies)

    return pl.pallas_call(
        body,
        out_shape=jax.ShapeDtypeStruct((mine, ff), jnp.bfloat16),
        in_specs=[ANY] * len(blocks),
        out_specs=ANY,
        scratch_shapes=[pltpu.SemaphoreType.DMA((len(blocks),))],
        cost_estimate=pl.CostEstimate(flops=0, bytes_accessed=4 * mine * ff, transcendentals=0),
        name="place",
    )(*[value for _, _, value in blocks])


def in_tiles(tokens, gate_weight, up_weight):
    rows, parts = lax.axis_size("row"), lax.axis_size("parts")
    mine, ff = tokens.shape[0], gate_weight.shape[1]
    width = ff // rows
    units = width // LANES

    block_rows = lax.all_gather(tokens, "row", axis=0, tiled=True)

    edges, total = [0], sum(PIECES)
    for piece in range(len(PIECES)):
        edge = units * sum(PIECES[:piece + 1]) // total * LANES
        if edge > edges[-1]:
            edges.append(edge)
    spans = list(zip(edges[:-1], edges[1:]))

    sent, arrived, swapped, held = [], [], [], []
    for low, high in spans:
        pieces = []
        for shift in range(1, rows):
            sent.append(pack(gate_weight, up_weight, shift, low, high - low, arrived[-2:-1] + swapped[-3:-2]))
            came = lax.ppermute(sent[-1], "row", around(rows, shift))
            arrived.append(came)
            pieces.append(came)
            for turn in range(1, parts):
                swapped.append(lax.ppermute(came, "parts", around(parts, -turn)))
                pieces.append(swapped[-1])
        held.append(pieces)

    whole = lax.all_gather(hold(block_rows, sent[2:3]), "col", axis=1, tiled=True)
    blocks, after = [], sent[-1:]
    for pieces, (low, high) in zip(held, spans):
        outs = product(whole, gate_weight, up_weight, pieces, low, high - low, mine, after)
        after = outs[:1]
        for shift in range(rows):
            value = lax.ppermute(outs[shift], "row", around(rows, shift)) if shift else outs[shift]
            blocks.append((shift, low, value))
    return place(blocks, mine, ff)


def at_once(tokens, gate_weight, up_weight):
    rows, parts = lax.axis_size("row"), lax.axis_size("parts")
    y = lax.axis_index("parts")
    mine, ff = tokens.shape[0], gate_weight.shape[1]
    depth = gate_weight.shape[0]
    share, width = depth // parts, ff // rows

    whole = lax.all_gather(lax.all_gather(tokens, "row", axis=0, tiled=True), "col", axis=1, tiled=True)
    everyone = whole.shape[0]
    by_share = whole.reshape(everyone, rows, parts, share)
    sent = jnp.stack([
        lax.dynamic_slice(w, (y * share, 0), (share, ff)).reshape(share, rows, width).transpose(1, 0, 2)
        for w in (gate_weight, up_weight)
    ])
    held = lax.all_to_all(sent, "row", 1, 1, tiled=True)
    gate = up = 0.0
    for turn in range(parts):
        features = lax.dynamic_index_in_dim(by_share, (y + turn) % parts, 2, keepdims=False)
        features = features.reshape(everyone, rows * share)
        block = lax.ppermute(held, "parts", around(parts, -turn)) if turn else held
        block = block.reshape(2, rows * share, width)
        gate += jnp.dot(features, block[0], preferred_element_type=jnp.float32)
        up += jnp.dot(features, block[1], preferred_element_type=jnp.float32)
    done = (jax.nn.silu(gate) * up).astype(jnp.bfloat16)
    back = lax.all_to_all(done.reshape(rows, mine, width), "row", 0, 0, tiled=True)
    return back.transpose(1, 0, 2).reshape(mine, ff)


def on_device(tokens, gate_weight, up_weight):
    rows, parts = lax.axis_size("row"), lax.axis_size("parts")
    aligned = (
        gate_weight.shape[1] % (rows * LANES) == 0
        and gate_weight.shape[0] % (parts * 16) == 0
        and tokens.shape[0] % 16 == 0
    )
    return (in_tiles if aligned else at_once)(tokens, gate_weight, up_weight)


def solution(mesh):
    placed = (P(("parts", "row"), "col"), P("row", "col"), P("row", "col"))
    return jax.shard_map(
        on_device, mesh=mesh, in_specs=placed, out_specs=P(("parts", "row"), "col"), check_vma=False
    )
```

```python
import jax
import jax.numpy as jnp
from jax import lax
from jax.experimental import pallas as pl
from jax.experimental.pallas import tpu as pltpu
from jax.sharding import PartitionSpec as P

PIECES = (3, 2, 2)
GRANT = 60 * 2**20
LANES = 128
ANY = pl.BlockSpec(memory_space=pl.ANY)


def around(size, shift):
    return [(i, (i + shift) % size) for i in range(size)]


def run_all(copies):
    for copy in copies:
        copy.start()
    for copy in copies:
        copy.wait()


def pack(gate_weight, up_weight, shift, low, wide, after):
    depth, ff = gate_weight.shape
    rows, parts = lax.axis_size("row"), lax.axis_size("parts")
    share, width, tiles = depth // parts, ff // rows, wide // LANES

    def body(*refs):
        weights, sent, sems = refs[:2], refs[-2], refs[-1]
        to = lax.rem(lax.axis_index("row") + shift, rows)
        first = pl.multiple_of(lax.axis_index("parts") * share, share)
        copies = []
        for j in range(tiles):
            start = pl.multiple_of(to * width + low + j * LANES, LANES)
            for g, weight in enumerate(weights):
                copies.append(pltpu.make_async_copy(
                    weight.at[pl.ds(first, share), pl.ds(start, LANES)],
                    sent.at[:, pl.ds((2 * j + g) * LANES, LANES)],
                    sems.at[2 * j + g],
                ))
        run_all(copies)

    size = share * 2 * wide * 2
    return pl.pallas_call(
        body,
        out_shape=jax.ShapeDtypeStruct((share, 2 * wide), gate_weight.dtype),
        in_specs=[ANY] * (2 + len(after)),
        out_specs=pl.BlockSpec(memory_space=pltpu.VMEM),
        scratch_shapes=[pltpu.SemaphoreType.DMA((2 * tiles,))],
        compiler_params=pltpu.CompilerParams(vmem_limit_bytes=GRANT),
        cost_estimate=pl.CostEstimate(flops=0, bytes_accessed=2 * size, transcendentals=0),
        name="pack",
    )(gate_weight, up_weight, *after)


def hold(value, after):
    def body(*refs):
        pass

    return pl.pallas_call(
        body,
        out_shape=jax.ShapeDtypeStruct(value.shape, value.dtype),
        in_specs=[ANY] * (1 + len(after)),
        out_specs=ANY,
        input_output_aliases={0: 0},
        name="hold",
    )(value, *after)


def product(tokens, gate_weight, up_weight, held, low, wide, mine, after):
    depth, ff = gate_weight.shape
    rows, parts = lax.axis_size("row"), lax.axis_size("parts")
    share, width, tiles = depth // parts, ff // rows, wide // LANES
    features = rows * depth
    order = list(range(1, rows)) + [0]
    pieces = [(shift, turn) for shift in range(1, rows) for turn in range(parts)]

    def body(tokens_ref, gate_ref, up_ref, *refs):
        held_refs = refs[:len(pieces)]
        outs = refs[len(pieces) + len(after):][:rows]
        stack, block, sems, block_sems = refs[-4:]
        z, y = lax.axis_index("row"), lax.axis_index("parts")

        def fetch(step):
            to = lax.rem(z + order[step], rows)
            return pltpu.make_async_copy(
                tokens_ref.at[pl.ds(pl.multiple_of(to * mine, mine), mine), :],
                block.at[step % 2],
                block_sems.at[step % 2],
            )

        copies = []
        for ref, (shift, turn) in zip(held_refs, pieces):
            came = lax.rem(z + rows - shift, rows)
            half = lax.rem(y + turn, parts)
            start = pl.multiple_of(came * depth + half * share, share)
            copies.append(pltpu.make_async_copy(ref, stack.at[pl.ds(start, share), :], sems.at[len(copies)]))
        own = pl.multiple_of(z * depth, depth)
        for j in range(tiles):
            start = pl.multiple_of(z * width + low + j * LANES, LANES)
            for g, weight in enumerate((gate_ref, up_ref)):
                copies.append(pltpu.make_async_copy(
                    weight.at[:, pl.ds(start, LANES)],
                    stack.at[pl.ds(own, depth), pl.ds((2 * j + g) * LANES, LANES)],
                    sems.at[len(copies)],
                ))
        fetch(0).start()
        run_all(copies)
        for step, shift in enumerate(order):
            fetch(step).wait()
            if step + 1 < rows:
                fetch(step + 1).start()

            def tile(j, carry, step=step, shift=shift):
                both = jnp.dot(
                    block[step % 2],
                    stack[:, pl.ds(pl.multiple_of(j * 2 * LANES, 2 * LANES), 2 * LANES)],
                    preferred_element_type=jnp.float32,
                )
                gate, up = both[:, :LANES], both[:, LANES:]
                outs[shift][:, pl.ds(pl.multiple_of(j * LANES, LANES), LANES)] = (
                    jax.nn.silu(gate) * up
                ).astype(jnp.bfloat16)
                return carry

            lax.fori_loop(0, tiles, tile, 0)

    moved = 2 * (rows * mine * features + features * 2 * wide + rows * mine * wide)
    return pl.pallas_call(
        body,
        out_shape=[jax.ShapeDtypeStruct((mine, wide), jnp.bfloat16)] * rows,
        in_specs=[ANY] * (3 + len(pieces) + len(after)),
        out_specs=[pl.BlockSpec(memory_space=pltpu.VMEM)] * rows,
        scratch_shapes=[
            pltpu.VMEM((features, 2 * wide), gate_weight.dtype),
            pltpu.VMEM((2, mine, features), tokens.dtype),
            pltpu.SemaphoreType.DMA((len(pieces) + 2 * tiles,)),
            pltpu.SemaphoreType.DMA((2,)),
        ],
        compiler_params=pltpu.CompilerParams(vmem_limit_bytes=GRANT),
        cost_estimate=pl.CostEstimate(
            flops=4 * rows * mine * features * wide, bytes_accessed=moved, transcendentals=rows * mine * wide
        ),
        name="product",
    )(tokens, gate_weight, up_weight, *held, *after)


def place(blocks, mine, ff):
    rows = lax.axis_size("row")
    width = ff // rows

    def body(*refs):
        out, sems = refs[-2], refs[-1]
        z = lax.axis_index("row")
        copies = []
        for ref, (shift, low, value) in zip(refs, blocks):
            came = lax.rem(z + rows - shift, rows)
            start = pl.multiple_of(came * width + low, LANES)
            copies.append(pltpu.make_async_copy(
                ref, out.at[:, pl.ds(start, value.shape[1])], sems.at[len(copies)]
            ))
        run_all(copies)

    return pl.pallas_call(
        body,
        out_shape=jax.ShapeDtypeStruct((mine, ff), jnp.bfloat16),
        in_specs=[ANY] * len(blocks),
        out_specs=pl.BlockSpec(memory_space=pltpu.VMEM),
        scratch_shapes=[pltpu.SemaphoreType.DMA((len(blocks),))],
        compiler_params=pltpu.CompilerParams(vmem_limit_bytes=GRANT),
        cost_estimate=pl.CostEstimate(flops=0, bytes_accessed=4 * mine * ff, transcendentals=0),
        name="place",
    )(*[value for _, _, value in blocks])


def in_tiles(tokens, gate_weight, up_weight):
    rows, parts = lax.axis_size("row"), lax.axis_size("parts")
    mine, ff = tokens.shape[0], gate_weight.shape[1]
    width = ff // rows
    units = width // LANES

    block_rows = lax.all_gather(tokens, "row", axis=0, tiled=True)

    edges, total = [0], sum(PIECES)
    for piece in range(len(PIECES)):
        edge = units * sum(PIECES[:piece + 1]) // total * LANES
        if edge > edges[-1]:
            edges.append(edge)
    spans = list(zip(edges[:-1], edges[1:]))

    sent, arrived, swapped, held = [], [], [], []
    for low, high in spans:
        pieces = []
        for shift in range(1, rows):
            sent.append(pack(gate_weight, up_weight, shift, low, high - low, sent[-1:] + arrived[-2:-1] + swapped[-3:-2]))
            came = lax.ppermute(sent[-1], "row", around(rows, shift))
            arrived.append(came)
            pieces.append(came)
            for turn in range(1, parts):
                swapped.append(lax.ppermute(came, "parts", around(parts, -turn)))
                pieces.append(swapped[-1])
        held.append(pieces)

    whole = lax.all_gather(hold(block_rows, arrived[1:2]), "col", axis=1, tiled=True)
    blocks, done, returned = [], [], [[]]
    for pieces, (low, high) in zip(held, spans):
        outs = product(whole, gate_weight, up_weight, pieces, low, high - low, mine, done[-1:] + returned[-2:][0])
        done.append(outs[0])
        back = [lax.ppermute(outs[shift], "row", around(rows, shift)) for shift in range(1, rows)]
        returned.append(back)
        blocks += [(shift, low, value) for shift, value in enumerate([outs[0]] + back)]
    return place(blocks, mine, ff)


def at_once(tokens, gate_weight, up_weight):
    rows, parts = lax.axis_size("row"), lax.axis_size("parts")
    y = lax.axis_index("parts")
    mine, ff = tokens.shape[0], gate_weight.shape[1]
    depth = gate_weight.shape[0]
    share, width = depth // parts, ff // rows

    whole = lax.all_gather(lax.all_gather(tokens, "row", axis=0, tiled=True), "col", axis=1, tiled=True)
    everyone = whole.shape[0]
    by_share = whole.reshape(everyone, rows, parts, share)
    sent = jnp.stack([
        lax.dynamic_slice(w, (y * share, 0), (share, ff)).reshape(share, rows, width).transpose(1, 0, 2)
        for w in (gate_weight, up_weight)
    ])
    held = lax.all_to_all(sent, "row", 1, 1, tiled=True)
    gate = up = 0.0
    for turn in range(parts):
        features = lax.dynamic_index_in_dim(by_share, (y + turn) % parts, 2, keepdims=False)
        features = features.reshape(everyone, rows * share)
        block = lax.ppermute(held, "parts", around(parts, -turn)) if turn else held
        block = block.reshape(2, rows * share, width)
        gate += jnp.dot(features, block[0], preferred_element_type=jnp.float32)
        up += jnp.dot(features, block[1], preferred_element_type=jnp.float32)
    done = (jax.nn.silu(gate) * up).astype(jnp.bfloat16)
    back = lax.all_to_all(done.reshape(rows, mine, width), "row", 0, 0, tiled=True)
    return back.transpose(1, 0, 2).reshape(mine, ff)


def on_device(tokens, gate_weight, up_weight):
    rows, parts = lax.axis_size("row"), lax.axis_size("parts")
    aligned = (
        gate_weight.shape[1] % (rows * LANES) == 0
        and gate_weight.shape[0] % (parts * 16) == 0
        and tokens.shape[0] % 16 == 0
    )
    return (in_tiles if aligned else at_once)(tokens, gate_weight, up_weight)


def solution(mesh):
    placed = (P(("parts", "row"), "col"), P("row", "col"), P("row", "col"))
    return jax.shard_map(
        on_device, mesh=mesh, in_specs=placed, out_specs=P(("parts", "row"), "col"), check_vma=False
    )
```

```python
import jax
import jax.numpy as jnp
from jax import lax
from jax.experimental import pallas as pl
from jax.experimental.pallas import tpu as pltpu
from jax.sharding import PartitionSpec as P

PIECES = (3, 2, 2)
GRANT = 60 * 2**20
LANES = 128
ANY = pl.BlockSpec(memory_space=pl.ANY)


def around(size, shift):
    return [(i, (i + shift) % size) for i in range(size)]


def run_all(copies):
    for copy in copies:
        copy.start()
    for copy in copies:
        copy.wait()


def pack(gate_weight, up_weight, shift, low, wide, after):
    depth, ff = gate_weight.shape
    rows, parts = lax.axis_size("row"), lax.axis_size("parts")
    share, width, tiles = depth // parts, ff // rows, wide // LANES

    def body(*refs):
        weights, sent, sems = refs[:2], refs[-2], refs[-1]
        to = lax.rem(lax.axis_index("row") + shift, rows)
        first = pl.multiple_of(lax.axis_index("parts") * share, share)
        copies = []
        for j in range(tiles):
            start = pl.multiple_of(to * width + low + j * LANES, LANES)
            for g, weight in enumerate(weights):
                copies.append(pltpu.make_async_copy(
                    weight.at[pl.ds(first, share), pl.ds(start, LANES)],
                    sent.at[:, pl.ds((2 * j + g) * LANES, LANES)],
                    sems.at[2 * j + g],
                ))
        run_all(copies)

    size = share * 2 * wide * 2
    return pl.pallas_call(
        body,
        out_shape=jax.ShapeDtypeStruct((share, 2 * wide), gate_weight.dtype),
        in_specs=[ANY] * (2 + len(after)),
        out_specs=pl.BlockSpec(memory_space=pltpu.VMEM),
        scratch_shapes=[pltpu.SemaphoreType.DMA((2 * tiles,))],
        compiler_params=pltpu.CompilerParams(vmem_limit_bytes=GRANT),
        cost_estimate=pl.CostEstimate(flops=0, bytes_accessed=2 * size, transcendentals=0),
        name="pack",
    )(gate_weight, up_weight, *after)


def hold(value, after):
    def body(*refs):
        pass

    return pl.pallas_call(
        body,
        out_shape=jax.ShapeDtypeStruct(value.shape, value.dtype),
        in_specs=[ANY] * (1 + len(after)),
        out_specs=ANY,
        input_output_aliases={0: 0},
        name="hold",
    )(value, *after)


def product(tokens, gate_weight, up_weight, held, low, wide, mine, after):
    depth, ff = gate_weight.shape
    rows, parts = lax.axis_size("row"), lax.axis_size("parts")
    share, width, tiles = depth // parts, ff // rows, wide // LANES
    features = rows * depth
    order = list(range(1, rows)) + [0]
    pieces = [(shift, turn) for shift in range(1, rows) for turn in range(parts)]

    def body(tokens_ref, gate_ref, up_ref, *refs):
        held_refs = refs[:len(pieces)]
        outs = refs[len(pieces) + len(after):][:rows]
        stack, block, sems, block_sems = refs[-4:]
        z, y = lax.axis_index("row"), lax.axis_index("parts")

        def fetch(step):
            to = lax.rem(z + order[step], rows)
            return pltpu.make_async_copy(
                tokens_ref.at[pl.ds(pl.multiple_of(to * mine, mine), mine), :],
                block.at[step % 2],
                block_sems.at[step % 2],
            )

        copies = []
        for ref, (shift, turn) in zip(held_refs, pieces):
            came = lax.rem(z + rows - shift, rows)
            half = lax.rem(y + turn, parts)
            start = pl.multiple_of(came * depth + half * share, share)
            copies.append(pltpu.make_async_copy(ref, stack.at[pl.ds(start, share), :], sems.at[len(copies)]))
        own = pl.multiple_of(z * depth, depth)
        for j in range(tiles):
            start = pl.multiple_of(z * width + low + j * LANES, LANES)
            for g, weight in enumerate((gate_ref, up_ref)):
                copies.append(pltpu.make_async_copy(
                    weight.at[:, pl.ds(start, LANES)],
                    stack.at[pl.ds(own, depth), pl.ds((2 * j + g) * LANES, LANES)],
                    sems.at[len(copies)],
                ))
        fetch(0).start()
        run_all(copies)
        for step, shift in enumerate(order):
            fetch(step).wait()
            if step + 1 < rows:
                fetch(step + 1).start()

            def tile(j, carry, step=step, shift=shift):
                both = jnp.dot(
                    block[step % 2],
                    stack[:, pl.ds(pl.multiple_of(j * 2 * LANES, 2 * LANES), 2 * LANES)],
                    preferred_element_type=jnp.float32,
                )
                gate, up = both[:, :LANES], both[:, LANES:]
                outs[shift][:, pl.ds(pl.multiple_of(j * LANES, LANES), LANES)] = (
                    jax.nn.silu(gate) * up
                ).astype(jnp.bfloat16)
                return carry

            lax.fori_loop(0, tiles, tile, 0)

    moved = 2 * (rows * mine * features + features * 2 * wide + rows * mine * wide)
    return pl.pallas_call(
        body,
        out_shape=[jax.ShapeDtypeStruct((mine, wide), jnp.bfloat16)] * rows,
        in_specs=[ANY] * (3 + len(pieces) + len(after)),
        out_specs=[pl.BlockSpec(memory_space=pltpu.VMEM)] * rows,
        scratch_shapes=[
            pltpu.VMEM((features, 2 * wide), gate_weight.dtype),
            pltpu.VMEM((2, mine, features), tokens.dtype),
            pltpu.SemaphoreType.DMA((len(pieces) + 2 * tiles,)),
            pltpu.SemaphoreType.DMA((2,)),
        ],
        compiler_params=pltpu.CompilerParams(vmem_limit_bytes=GRANT),
        cost_estimate=pl.CostEstimate(
            flops=4 * rows * mine * features * wide, bytes_accessed=moved, transcendentals=rows * mine * wide
        ),
        name="product",
    )(tokens, gate_weight, up_weight, *held, *after)


def place(blocks, mine, ff):
    rows = lax.axis_size("row")
    width = ff // rows

    def body(*refs):
        out, sems = refs[-2], refs[-1]
        z = lax.axis_index("row")
        copies = []
        for ref, (shift, low, value) in zip(refs, blocks):
            came = lax.rem(z + rows - shift, rows)
            start = pl.multiple_of(came * width + low, LANES)
            copies.append(pltpu.make_async_copy(
                ref, out.at[:, pl.ds(start, value.shape[1])], sems.at[len(copies)]
            ))
        run_all(copies)

    return pl.pallas_call(
        body,
        out_shape=jax.ShapeDtypeStruct((mine, ff), jnp.bfloat16),
        in_specs=[ANY] * len(blocks),
        out_specs=pl.BlockSpec(memory_space=pltpu.VMEM),
        scratch_shapes=[pltpu.SemaphoreType.DMA((len(blocks),))],
        compiler_params=pltpu.CompilerParams(vmem_limit_bytes=GRANT),
        cost_estimate=pl.CostEstimate(flops=0, bytes_accessed=4 * mine * ff, transcendentals=0),
        name="place",
    )(*[value for _, _, value in blocks])


def in_tiles(tokens, gate_weight, up_weight):
    rows, parts = lax.axis_size("row"), lax.axis_size("parts")
    mine, ff = tokens.shape[0], gate_weight.shape[1]
    width = ff // rows
    units = width // LANES

    block_rows = lax.all_gather(tokens, "row", axis=0, tiled=True)

    edges, total = [0], sum(PIECES)
    for piece in range(len(PIECES)):
        edge = units * sum(PIECES[:piece + 1]) // total * LANES
        if edge > edges[-1]:
            edges.append(edge)
    spans = list(zip(edges[:-1], edges[1:]))

    def weights_of(n):
        low, high = spans[n]
        for shift in range(1, rows):
            after = sent[-1:] + arrived[-2:-1] + swapped[-3:-2]
            sent.append(pack(gate_weight, up_weight, shift, low, high - low, after))
            arrived.append(lax.ppermute(sent[-1], "row", around(rows, shift)))
            came = arrived[-1]
            if done and shift == rows - 1:
                came = hold(came, done)
            held[n].append(came)
            for turn in range(1, parts):
                swapped.append(lax.ppermute(came, "parts", around(parts, -turn)))
                held[n].append(swapped[-1])

    def hidden_of(n, after):
        low, high = spans[n]
        outs = product(whole, gate_weight, up_weight, held[n], low, high - low, mine, after)
        back = [lax.ppermute(outs[shift], "row", around(rows, shift)) for shift in range(1, rows)]
        blocks.extend((shift, low, value) for shift, value in enumerate([outs[0]] + back))
        done.append(outs[0])
        returned.append(back)

    last = len(spans) - 1
    sent, arrived, swapped, done, returned, blocks = [], [], [], [], [], []
    held = [[] for _ in spans]
    for n in range(last):
        weights_of(n)
    whole = lax.all_gather(hold(block_rows, arrived[1:3] + sent[3:4]), "col", axis=1, tiled=True)
    if last:
        hidden_of(0, [])
    weights_of(last)
    for n in range(min(last, 1), last + 1):
        hidden_of(n, done[-1:] + (returned[n - 2] if n > 1 else []))
    return place(blocks, mine, ff)


def at_once(tokens, gate_weight, up_weight):
    rows, parts = lax.axis_size("row"), lax.axis_size("parts")
    y = lax.axis_index("parts")
    mine, ff = tokens.shape[0], gate_weight.shape[1]
    depth = gate_weight.shape[0]
    share, width = depth // parts, ff // rows

    whole = lax.all_gather(lax.all_gather(tokens, "row", axis=0, tiled=True), "col", axis=1, tiled=True)
    everyone = whole.shape[0]
    by_share = whole.reshape(everyone, rows, parts, share)
    sent = jnp.stack([
        lax.dynamic_slice(w, (y * share, 0), (share, ff)).reshape(share, rows, width).transpose(1, 0, 2)
        for w in (gate_weight, up_weight)
    ])
    held = lax.all_to_all(sent, "row", 1, 1, tiled=True)
    gate = up = 0.0
    for turn in range(parts):
        features = lax.dynamic_index_in_dim(by_share, (y + turn) % parts, 2, keepdims=False)
        features = features.reshape(everyone, rows * share)
        block = lax.ppermute(held, "parts", around(parts, -turn)) if turn else held
        block = block.reshape(2, rows * share, width)
        gate += jnp.dot(features, block[0], preferred_element_type=jnp.float32)
        up += jnp.dot(features, block[1], preferred_element_type=jnp.float32)
    done = (jax.nn.silu(gate) * up).astype(jnp.bfloat16)
    back = lax.all_to_all(done.reshape(rows, mine, width), "row", 0, 0, tiled=True)
    return back.transpose(1, 0, 2).reshape(mine, ff)


def on_device(tokens, gate_weight, up_weight):
    rows, parts = lax.axis_size("row"), lax.axis_size("parts")
    aligned = (
        gate_weight.shape[1] % (rows * LANES) == 0
        and gate_weight.shape[0] % (parts * 16) == 0
        and tokens.shape[0] % 16 == 0
    )
    return (in_tiles if aligned else at_once)(tokens, gate_weight, up_weight)


def solution(mesh):
    placed = (P(("parts", "row"), "col"), P("row", "col"), P("row", "col"))
    return jax.shard_map(
        on_device, mesh=mesh, in_specs=placed, out_specs=P(("parts", "row"), "col"), check_vma=False
    )
```

```python
import jax
import jax.numpy as jnp
from jax import lax
from jax.experimental import pallas as pl
from jax.experimental.pallas import tpu as pltpu
from jax.sharding import PartitionSpec as P

PIECES = (3, 2, 2)
GRANT = 60 * 2**20
LANES = 128
ANY = pl.BlockSpec(memory_space=pl.ANY)


def around(size, shift):
    return [(i, (i + shift) % size) for i in range(size)]


def by_distance(size):
    return sorted(range(1, size), key=lambda shift: -min(shift, size - shift))


def run_all(copies):
    for copy in copies:
        copy.start()
    for copy in copies:
        copy.wait()


def pack(gate_weight, up_weight, shift, low, wide, after):
    depth, ff = gate_weight.shape
    rows, parts = lax.axis_size("row"), lax.axis_size("parts")
    share, width, tiles = depth // parts, ff // rows, wide // LANES

    def body(*refs):
        weights, sent, sems = refs[:2], refs[-2], refs[-1]
        to = lax.rem(lax.axis_index("row") + shift, rows)
        first = pl.multiple_of(lax.axis_index("parts") * share, share)
        copies = []
        for j in range(tiles):
            start = pl.multiple_of(to * width + low + j * LANES, LANES)
            for g, weight in enumerate(weights):
                copies.append(pltpu.make_async_copy(
                    weight.at[pl.ds(first, share), pl.ds(start, LANES)],
                    sent.at[:, pl.ds((2 * j + g) * LANES, LANES)],
                    sems.at[2 * j + g],
                ))
        run_all(copies)

    size = share * 2 * wide * 2
    return pl.pallas_call(
        body,
        out_shape=jax.ShapeDtypeStruct((share, 2 * wide), gate_weight.dtype),
        in_specs=[ANY] * (2 + len(after)),
        out_specs=pl.BlockSpec(memory_space=pltpu.VMEM),
        scratch_shapes=[pltpu.SemaphoreType.DMA((2 * tiles,))],
        compiler_params=pltpu.CompilerParams(vmem_limit_bytes=GRANT),
        cost_estimate=pl.CostEstimate(flops=0, bytes_accessed=2 * size, transcendentals=0),
        name="pack",
    )(gate_weight, up_weight, *after)


def hold(value, after):
    def body(*refs):
        pass

    return pl.pallas_call(
        body,
        out_shape=jax.ShapeDtypeStruct(value.shape, value.dtype),
        in_specs=[ANY] * (1 + len(after)),
        out_specs=ANY,
        input_output_aliases={0: 0},
        name="hold",
    )(value, *after)


def product(tokens, gate_weight, up_weight, held, low, wide, mine, after):
    depth, ff = gate_weight.shape
    rows, parts = lax.axis_size("row"), lax.axis_size("parts")
    share, width, tiles = depth // parts, ff // rows, wide // LANES
    features = rows * depth
    columns, near = tokens.shape[1], tokens.shape[3]
    order = by_distance(rows) + [0]
    pieces = [(shift, turn) for shift in by_distance(rows) for turn in range(parts)]

    def body(tokens_ref, gate_ref, up_ref, *refs):
        held_refs = refs[:len(pieces)]
        outs = refs[len(pieces) + len(after):][:rows]
        stack, block, sems, block_sems = refs[-4:]
        z, y = lax.axis_index("row"), lax.axis_index("parts")

        def fetch(step):
            to = lax.rem(z + order[step], rows)
            return [
                pltpu.make_async_copy(
                    tokens_ref.at[to, j], block.at[step % 2, :, pl.ds(j * near, near)], block_sems.at[step % 2, j]
                )
                for j in range(columns)
            ]

        copies = []
        for ref, (shift, turn) in zip(held_refs, pieces):
            came = lax.rem(z + rows - shift, rows)
            half = lax.rem(y + turn, parts)
            start = pl.multiple_of(came * depth + half * share, share)
            copies.append(pltpu.make_async_copy(ref, stack.at[pl.ds(start, share), :], sems.at[len(copies)]))
        own = pl.multiple_of(z * depth, depth)
        for j in range(tiles):
            start = pl.multiple_of(z * width + low + j * LANES, LANES)
            for g, weight in enumerate((gate_ref, up_ref)):
                copies.append(pltpu.make_async_copy(
                    weight.at[:, pl.ds(start, LANES)],
                    stack.at[pl.ds(own, depth), pl.ds((2 * j + g) * LANES, LANES)],
                    sems.at[len(copies)],
                ))
        for copy in fetch(0):
            copy.start()
        run_all(copies)
        for step, shift in enumerate(order):
            for copy in fetch(step):
                copy.wait()
            if step + 1 < rows:
                for copy in fetch(step + 1):
                    copy.start()

            def tile(j, carry, step=step, shift=shift):
                both = jnp.dot(
                    block[step % 2],
                    stack[:, pl.ds(pl.multiple_of(j * 2 * LANES, 2 * LANES), 2 * LANES)],
                    preferred_element_type=jnp.float32,
                )
                gate, up = both[:, :LANES], both[:, LANES:]
                outs[shift][:, pl.ds(pl.multiple_of(j * LANES, LANES), LANES)] = (
                    jax.nn.silu(gate) * up
                ).astype(jnp.bfloat16)
                return carry

            lax.fori_loop(0, tiles, tile, 0)

    moved = 2 * (rows * mine * features + features * 2 * wide + rows * mine * wide)
    return pl.pallas_call(
        body,
        out_shape=[jax.ShapeDtypeStruct((mine, wide), jnp.bfloat16)] * rows,
        in_specs=[ANY] * (3 + len(pieces) + len(after)),
        out_specs=[pl.BlockSpec(memory_space=pltpu.VMEM)] * rows,
        scratch_shapes=[
            pltpu.VMEM((features, 2 * wide), gate_weight.dtype),
            pltpu.VMEM((2, mine, features), tokens.dtype),
            pltpu.SemaphoreType.DMA((len(pieces) + 2 * tiles,)),
            pltpu.SemaphoreType.DMA((2, columns)),
        ],
        compiler_params=pltpu.CompilerParams(vmem_limit_bytes=GRANT),
        cost_estimate=pl.CostEstimate(
            flops=4 * rows * mine * features * wide, bytes_accessed=moved, transcendentals=rows * mine * wide
        ),
        name="product",
    )(tokens, gate_weight, up_weight, *held, *after)


def place(blocks, mine, ff):
    rows = lax.axis_size("row")
    width = ff // rows

    def body(*refs):
        out, sems = refs[-2], refs[-1]
        z = lax.axis_index("row")
        copies = []
        for ref, (shift, low, value) in zip(refs, blocks):
            came = lax.rem(z + rows - shift, rows)
            start = pl.multiple_of(came * width + low, LANES)
            copies.append(pltpu.make_async_copy(
                ref, out.at[:, pl.ds(start, value.shape[1])], sems.at[len(copies)]
            ))
        run_all(copies)

    return pl.pallas_call(
        body,
        out_shape=jax.ShapeDtypeStruct((mine, ff), jnp.bfloat16),
        in_specs=[ANY] * len(blocks),
        out_specs=pl.BlockSpec(memory_space=pltpu.VMEM),
        scratch_shapes=[pltpu.SemaphoreType.DMA((len(blocks),))],
        compiler_params=pltpu.CompilerParams(vmem_limit_bytes=GRANT),
        cost_estimate=pl.CostEstimate(flops=0, bytes_accessed=4 * mine * ff, transcendentals=0),
        name="place",
    )(*[value for _, _, value in blocks])


def in_tiles(tokens, gate_weight, up_weight):
    rows, parts = lax.axis_size("row"), lax.axis_size("parts")
    mine, ff = tokens.shape[0], gate_weight.shape[1]
    width = ff // rows
    units = width // LANES

    whole = lax.all_gather(tokens, ("row", "col")).reshape(rows, -1, *tokens.shape)

    edges, total = [0], sum(PIECES)
    for piece in range(len(PIECES)):
        edge = units * sum(PIECES[:piece + 1]) // total * LANES
        if edge > edges[-1]:
            edges.append(edge)
    spans = list(zip(edges[:-1], edges[1:]))

    def weights_of(n):
        low, high = spans[n]
        for shift in by_distance(rows):
            after = sent[-1:] + arrived[-2:-1] + swapped[-3:-2]
            sent.append(pack(gate_weight, up_weight, shift, low, high - low, after))
            arrived.append(lax.ppermute(sent[-1], "row", around(rows, shift)))
            came = arrived[-1]
            if done and len(sent) > len(spans) * (rows - 1) - 2:
                came = hold(came, done)
            held[n].append(came)
            for turn in range(1, parts):
                swapped.append(lax.ppermute(came, "parts", around(parts, -turn)))
                held[n].append(swapped[-1])

    def hidden_of(n, after):
        low, high = spans[n]
        outs = product(whole, gate_weight, up_weight, held[n], low, high - low, mine, after)
        back = [lax.ppermute(outs[shift], "row", around(rows, shift)) for shift in range(1, rows)]
        blocks.extend((shift, low, value) for shift, value in enumerate([outs[0]] + back))
        done.append(outs[0])
        returned.append(back)

    last = len(spans) - 1
    sent, arrived, swapped, done, returned, blocks = [], [], [], [], [], []
    held = [[] for _ in spans]
    for n in range(last):
        weights_of(n)
    if last:
        hidden_of(0, [])
    weights_of(last)
    for n in range(min(last, 1), last + 1):
        hidden_of(n, done[-1:] + (returned[n - 2] if n > 1 else []))
    return place(blocks, mine, ff)


def at_once(tokens, gate_weight, up_weight):
    rows, parts = lax.axis_size("row"), lax.axis_size("parts")
    y = lax.axis_index("parts")
    mine, ff = tokens.shape[0], gate_weight.shape[1]
    depth = gate_weight.shape[0]
    share, width = depth // parts, ff // rows

    whole = lax.all_gather(lax.all_gather(tokens, "row", axis=0, tiled=True), "col", axis=1, tiled=True)
    everyone = whole.shape[0]
    by_share = whole.reshape(everyone, rows, parts, share)
    sent = jnp.stack([
        lax.dynamic_slice(w, (y * share, 0), (share, ff)).reshape(share, rows, width).transpose(1, 0, 2)
        for w in (gate_weight, up_weight)
    ])
    held = lax.all_to_all(sent, "row", 1, 1, tiled=True)
    gate = up = 0.0
    for turn in range(parts):
        features = lax.dynamic_index_in_dim(by_share, (y + turn) % parts, 2, keepdims=False)
        features = features.reshape(everyone, rows * share)
        block = lax.ppermute(held, "parts", around(parts, -turn)) if turn else held
        block = block.reshape(2, rows * share, width)
        gate += jnp.dot(features, block[0], preferred_element_type=jnp.float32)
        up += jnp.dot(features, block[1], preferred_element_type=jnp.float32)
    done = (jax.nn.silu(gate) * up).astype(jnp.bfloat16)
    back = lax.all_to_all(done.reshape(rows, mine, width), "row", 0, 0, tiled=True)
    return back.transpose(1, 0, 2).reshape(mine, ff)


def on_device(tokens, gate_weight, up_weight):
    rows, parts = lax.axis_size("row"), lax.axis_size("parts")
    aligned = (
        gate_weight.shape[1] % (rows * LANES) == 0
        and gate_weight.shape[0] % (parts * 16) == 0
        and tokens.shape[0] % 16 == 0
    )
    return (in_tiles if aligned else at_once)(tokens, gate_weight, up_weight)


def solution(mesh):
    placed = (P(("parts", "row"), "col"), P("row", "col"), P("row", "col"))
    return jax.shard_map(
        on_device, mesh=mesh, in_specs=placed, out_specs=P(("parts", "row"), "col"), check_vma=False
    )
```

```python
import jax
import jax.numpy as jnp
from jax import lax
from jax.experimental import pallas as pl
from jax.experimental.pallas import tpu as pltpu
from jax.sharding import PartitionSpec as P

PIECES = (3, 2, 2)
GRANT = 60 * 2**20
LANES = 128
ANY = pl.BlockSpec(memory_space=pl.ANY)


def around(size, shift):
    return [(i, (i + shift) % size) for i in range(size)]


def by_distance(size):
    return sorted(range(1, size), key=lambda shift: -min(shift, size - shift))


def run_all(copies):
    for copy in copies:
        copy.start()
    for copy in copies:
        copy.wait()


def pack(gate_weight, up_weight, shift, low, wide, after):
    depth, ff = gate_weight.shape
    rows, parts = lax.axis_size("row"), lax.axis_size("parts")
    share, width, tiles = depth // parts, ff // rows, wide // LANES

    def body(*refs):
        weights, sent, sems = refs[:2], refs[-2], refs[-1]
        to = lax.rem(lax.axis_index("row") + shift, rows)
        first = pl.multiple_of(lax.axis_index("parts") * share, share)
        copies = []
        for j in range(tiles):
            start = pl.multiple_of(to * width + low + j * LANES, LANES)
            for g, weight in enumerate(weights):
                copies.append(pltpu.make_async_copy(
                    weight.at[pl.ds(first, share), pl.ds(start, LANES)],
                    sent.at[:, pl.ds((2 * j + g) * LANES, LANES)],
                    sems.at[2 * j + g],
                ))
        run_all(copies)

    size = share * 2 * wide * 2
    return pl.pallas_call(
        body,
        out_shape=jax.ShapeDtypeStruct((share, 2 * wide), gate_weight.dtype),
        in_specs=[ANY] * (2 + len(after)),
        out_specs=pl.BlockSpec(memory_space=pltpu.VMEM),
        scratch_shapes=[pltpu.SemaphoreType.DMA((2 * tiles,))],
        compiler_params=pltpu.CompilerParams(vmem_limit_bytes=GRANT),
        cost_estimate=pl.CostEstimate(flops=0, bytes_accessed=2 * size, transcendentals=0),
        name="pack",
    )(gate_weight, up_weight, *after)


def hold(value, after):
    def body(*refs):
        pass

    return pl.pallas_call(
        body,
        out_shape=jax.ShapeDtypeStruct(value.shape, value.dtype),
        in_specs=[ANY] * (1 + len(after)),
        out_specs=ANY,
        input_output_aliases={0: 0},
        name="hold",
    )(value, *after)


def product(tokens, gate_weight, up_weight, held, low, wide, mine, after):
    depth, ff = gate_weight.shape
    rows, parts = lax.axis_size("row"), lax.axis_size("parts")
    share, width, tiles = depth // parts, ff // rows, wide // LANES
    features = rows * depth
    order = by_distance(rows) + [0]
    pieces = [(shift, turn) for shift in by_distance(rows) for turn in range(parts)]

    def body(tokens_ref, gate_ref, up_ref, *refs):
        held_refs = refs[:len(pieces)]
        outs = refs[len(pieces) + len(after):][:rows]
        stack, block, sems, block_sems = refs[-4:]
        z, y = lax.axis_index("row"), lax.axis_index("parts")

        def fetch(step):
            to = lax.rem(z + order[step], rows)
            return pltpu.make_async_copy(
                tokens_ref.at[pl.ds(pl.multiple_of(to * mine, mine), mine), :],
                block.at[step % 2],
                block_sems.at[step % 2],
            )

        copies = []
        for ref, (shift, turn) in zip(held_refs, pieces):
            came = lax.rem(z + rows - shift, rows)
            half = lax.rem(y + turn, parts)
            start = pl.multiple_of(came * depth + half * share, share)
            copies.append(pltpu.make_async_copy(ref, stack.at[pl.ds(start, share), :], sems.at[len(copies)]))
        own = pl.multiple_of(z * depth, depth)
        for j in range(tiles):
            start = pl.multiple_of(z * width + low + j * LANES, LANES)
            for g, weight in enumerate((gate_ref, up_ref)):
                copies.append(pltpu.make_async_copy(
                    weight.at[:, pl.ds(start, LANES)],
                    stack.at[pl.ds(own, depth), pl.ds((2 * j + g) * LANES, LANES)],
                    sems.at[len(copies)],
                ))
        fetch(0).start()
        run_all(copies)
        for step, shift in enumerate(order):
            fetch(step).wait()
            if step + 1 < rows:
                fetch(step + 1).start()

            def tile(j, carry, step=step, shift=shift):
                both = jnp.dot(
                    block[step % 2],
                    stack[:, pl.ds(pl.multiple_of(j * 2 * LANES, 2 * LANES), 2 * LANES)],
                    preferred_element_type=jnp.float32,
                )
                gate, up = both[:, :LANES], both[:, LANES:]
                outs[shift][:, pl.ds(pl.multiple_of(j * LANES, LANES), LANES)] = (
                    jax.nn.silu(gate) * up
                ).astype(jnp.bfloat16)
                return carry

            lax.fori_loop(0, tiles, tile, 0)

    moved = 2 * (rows * mine * features + features * 2 * wide + rows * mine * wide)
    return pl.pallas_call(
        body,
        out_shape=[jax.ShapeDtypeStruct((mine, wide), jnp.bfloat16)] * rows,
        in_specs=[ANY] * (3 + len(pieces) + len(after)),
        out_specs=[pl.BlockSpec(memory_space=pltpu.VMEM)] * rows,
        scratch_shapes=[
            pltpu.VMEM((features, 2 * wide), gate_weight.dtype),
            pltpu.VMEM((2, mine, features), tokens.dtype),
            pltpu.SemaphoreType.DMA((len(pieces) + 2 * tiles,)),
            pltpu.SemaphoreType.DMA((2,)),
        ],
        compiler_params=pltpu.CompilerParams(vmem_limit_bytes=GRANT),
        cost_estimate=pl.CostEstimate(
            flops=4 * rows * mine * features * wide, bytes_accessed=moved, transcendentals=rows * mine * wide
        ),
        name="product",
    )(tokens, gate_weight, up_weight, *held, *after)


def place(blocks, mine, ff):
    rows = lax.axis_size("row")
    width = ff // rows

    def body(*refs):
        out, sems = refs[-2], refs[-1]
        z = lax.axis_index("row")
        copies = []
        for ref, (shift, low, value) in zip(refs, blocks):
            came = lax.rem(z + rows - shift, rows)
            start = pl.multiple_of(came * width + low, LANES)
            copies.append(pltpu.make_async_copy(
                ref, out.at[:, pl.ds(start, value.shape[1])], sems.at[len(copies)]
            ))
        run_all(copies)

    return pl.pallas_call(
        body,
        out_shape=jax.ShapeDtypeStruct((mine, ff), jnp.bfloat16),
        in_specs=[ANY] * len(blocks),
        out_specs=pl.BlockSpec(memory_space=pltpu.VMEM),
        scratch_shapes=[pltpu.SemaphoreType.DMA((len(blocks),))],
        compiler_params=pltpu.CompilerParams(vmem_limit_bytes=GRANT),
        cost_estimate=pl.CostEstimate(flops=0, bytes_accessed=4 * mine * ff, transcendentals=0),
        name="place",
    )(*[value for _, _, value in blocks])


def in_tiles(tokens, gate_weight, up_weight):
    rows, parts = lax.axis_size("row"), lax.axis_size("parts")
    mine, ff = tokens.shape[0], gate_weight.shape[1]
    width = ff // rows
    units = width // LANES

    block_rows = lax.all_gather(tokens, "row", axis=0, tiled=True)

    edges, total = [0], sum(PIECES)
    for piece in range(len(PIECES)):
        edge = units * sum(PIECES[:piece + 1]) // total * LANES
        if edge > edges[-1]:
            edges.append(edge)
    spans = list(zip(edges[:-1], edges[1:]))

    def weights_of(n):
        low, high = spans[n]
        for shift in by_distance(rows):
            after = sent[-1:] + arrived[-2:-1] + swapped[-3:-2]
            sent.append(pack(gate_weight, up_weight, shift, low, high - low, after))
            arrived.append(lax.ppermute(sent[-1], "row", around(rows, shift)))
            came = arrived[-1]
            if done and len(sent) > len(spans) * (rows - 1) - 2:
                came = hold(came, done)
            held[n].append(came)
            for turn in range(1, parts):
                swapped.append(lax.ppermute(came, "parts", around(parts, -turn)))
                held[n].append(swapped[-1])

    def hidden_of(n, after):
        low, high = spans[n]
        outs = product(whole, gate_weight, up_weight, held[n], low, high - low, mine, after)
        back = [lax.ppermute(outs[shift], "row", around(rows, shift)) for shift in range(1, rows)]
        blocks.extend((shift, low, value) for shift, value in enumerate([outs[0]] + back))
        done.append(outs[0])
        returned.append(back)

    last = len(spans) - 1
    sent, arrived, swapped, done, returned, blocks = [], [], [], [], [], []
    held = [[] for _ in spans]
    for n in range(last):
        weights_of(n)
    whole = lax.all_gather(hold(block_rows, arrived[1:3] + sent[3:4]), "col", axis=1, tiled=True)
    if last:
        hidden_of(0, [])
    weights_of(last)
    for n in range(min(last, 1), last + 1):
        hidden_of(n, done[-1:] + (returned[n - 2] if n > 1 else []))
    return place(blocks, mine, ff)


def at_once(tokens, gate_weight, up_weight):
    rows, parts = lax.axis_size("row"), lax.axis_size("parts")
    y = lax.axis_index("parts")
    mine, ff = tokens.shape[0], gate_weight.shape[1]
    depth = gate_weight.shape[0]
    share, width = depth // parts, ff // rows

    whole = lax.all_gather(lax.all_gather(tokens, "row", axis=0, tiled=True), "col", axis=1, tiled=True)
    everyone = whole.shape[0]
    by_share = whole.reshape(everyone, rows, parts, share)
    sent = jnp.stack([
        lax.dynamic_slice(w, (y * share, 0), (share, ff)).reshape(share, rows, width).transpose(1, 0, 2)
        for w in (gate_weight, up_weight)
    ])
    held = lax.all_to_all(sent, "row", 1, 1, tiled=True)
    gate = up = 0.0
    for turn in range(parts):
        features = lax.dynamic_index_in_dim(by_share, (y + turn) % parts, 2, keepdims=False)
        features = features.reshape(everyone, rows * share)
        block = lax.ppermute(held, "parts", around(parts, -turn)) if turn else held
        block = block.reshape(2, rows * share, width)
        gate += jnp.dot(features, block[0], preferred_element_type=jnp.float32)
        up += jnp.dot(features, block[1], preferred_element_type=jnp.float32)
    done = (jax.nn.silu(gate) * up).astype(jnp.bfloat16)
    back = lax.all_to_all(done.reshape(rows, mine, width), "row", 0, 0, tiled=True)
    return back.transpose(1, 0, 2).reshape(mine, ff)


def on_device(tokens, gate_weight, up_weight):
    rows, parts = lax.axis_size("row"), lax.axis_size("parts")
    aligned = (
        gate_weight.shape[1] % (rows * LANES) == 0
        and gate_weight.shape[0] % (parts * 16) == 0
        and tokens.shape[0] % 16 == 0
    )
    return (in_tiles if aligned else at_once)(tokens, gate_weight, up_weight)


def solution(mesh):
    placed = (P(("parts", "row"), "col"), P("row", "col"), P("row", "col"))
    return jax.shard_map(
        on_device, mesh=mesh, in_specs=placed, out_specs=P(("parts", "row"), "col"), check_vma=False
    )
```

```python
import jax
import jax.numpy as jnp
from jax import lax
from jax.experimental import pallas as pl
from jax.experimental.pallas import tpu as pltpu
from jax.sharding import PartitionSpec as P

PIECES = (3, 2, 2)
GRANT = 60 * 2**20
LANES = 128
ANY = pl.BlockSpec(memory_space=pl.ANY)


def around(size, shift):
    return [(i, (i + shift) % size) for i in range(size)]


def by_distance(size):
    return sorted(range(1, size), key=lambda shift: -min(shift, size - shift))


def run_all(copies):
    for copy in copies:
        copy.start()
    for copy in copies:
        copy.wait()


def pack(gate_weight, up_weight, shift, low, wide, after):
    depth, ff = gate_weight.shape
    rows, parts = lax.axis_size("row"), lax.axis_size("parts")
    share, width, tiles = depth // parts, ff // rows, wide // LANES

    def body(*refs):
        weights, sent, sems = refs[:2], refs[-2], refs[-1]
        to = lax.rem(lax.axis_index("row") + shift, rows)
        first = pl.multiple_of(lax.axis_index("parts") * share, share)
        copies = []
        for j in range(tiles):
            start = pl.multiple_of(to * width + low + j * LANES, LANES)
            for g, weight in enumerate(weights):
                copies.append(pltpu.make_async_copy(
                    weight.at[pl.ds(first, share), pl.ds(start, LANES)],
                    sent.at[:, pl.ds((2 * j + g) * LANES, LANES)],
                    sems.at[2 * j + g],
                ))
        run_all(copies)

    size = share * 2 * wide * 2
    return pl.pallas_call(
        body,
        out_shape=jax.ShapeDtypeStruct((share, 2 * wide), gate_weight.dtype),
        in_specs=[ANY] * (2 + len(after)),
        out_specs=pl.BlockSpec(memory_space=pltpu.VMEM),
        scratch_shapes=[pltpu.SemaphoreType.DMA((2 * tiles,))],
        compiler_params=pltpu.CompilerParams(vmem_limit_bytes=GRANT),
        cost_estimate=pl.CostEstimate(flops=0, bytes_accessed=2 * size, transcendentals=0),
        name="pack",
    )(gate_weight, up_weight, *after)


def hold(value, after):
    def body(*refs):
        pass

    return pl.pallas_call(
        body,
        out_shape=jax.ShapeDtypeStruct(value.shape, value.dtype),
        in_specs=[ANY] * (1 + len(after)),
        out_specs=ANY,
        input_output_aliases={0: 0},
        name="hold",
    )(value, *after)


def product(tokens, gate_weight, up_weight, held, low, wide, mine, after):
    depth, ff = gate_weight.shape
    rows, parts = lax.axis_size("row"), lax.axis_size("parts")
    share, width, tiles = depth // parts, ff // rows, wide // LANES
    features = rows * depth
    order = by_distance(rows) + [0]

    def body(tokens_ref, gate_ref, up_ref, *refs):
        held_refs = refs[:len(held)]
        outs = refs[len(held) + len(after):][:rows]
        stack, block, sems, block_sems = refs[-4:]
        z, y = lax.axis_index("row"), lax.axis_index("parts")

        def fetch(step):
            to = lax.rem(z + order[step], rows)
            return pltpu.make_async_copy(
                tokens_ref.at[pl.ds(pl.multiple_of(to * mine, mine), mine), :],
                block.at[step % 2],
                block_sems.at[step % 2],
            )

        copies = []
        for ref, (shift, turn, begin, _) in zip(held_refs, held):
            came = lax.rem(z + rows - shift, rows)
            half = lax.rem(y + turn, parts)
            start = pl.multiple_of(came * depth + half * share, share)
            copies.append(pltpu.make_async_copy(
                ref.at[:, pl.ds(2 * (low - begin), 2 * wide)], stack.at[pl.ds(start, share), :], sems.at[len(copies)]
            ))
        own = pl.multiple_of(z * depth, depth)
        for j in range(tiles):
            start = pl.multiple_of(z * width + low + j * LANES, LANES)
            for g, weight in enumerate((gate_ref, up_ref)):
                copies.append(pltpu.make_async_copy(
                    weight.at[:, pl.ds(start, LANES)],
                    stack.at[pl.ds(own, depth), pl.ds((2 * j + g) * LANES, LANES)],
                    sems.at[len(copies)],
                ))
        fetch(0).start()
        run_all(copies)
        for step, shift in enumerate(order):
            fetch(step).wait()
            if step + 1 < rows:
                fetch(step + 1).start()

            def tile(j, carry, step=step, shift=shift):
                both = jnp.dot(
                    block[step % 2],
                    stack[:, pl.ds(pl.multiple_of(j * 2 * LANES, 2 * LANES), 2 * LANES)],
                    preferred_element_type=jnp.float32,
                )
                gate, up = both[:, :LANES], both[:, LANES:]
                outs[shift][:, pl.ds(pl.multiple_of(j * LANES, LANES), LANES)] = (
                    jax.nn.silu(gate) * up
                ).astype(jnp.bfloat16)
                return carry

            lax.fori_loop(0, tiles, tile, 0)

    moved = 2 * (rows * mine * features + features * 2 * wide + rows * mine * wide)
    return pl.pallas_call(
        body,
        out_shape=[jax.ShapeDtypeStruct((mine, wide), jnp.bfloat16)] * rows,
        in_specs=[ANY] * (3 + len(held) + len(after)),
        out_specs=[pl.BlockSpec(memory_space=pltpu.VMEM)] * rows,
        scratch_shapes=[
            pltpu.VMEM((features, 2 * wide), gate_weight.dtype),
            pltpu.VMEM((2, mine, features), tokens.dtype),
            pltpu.SemaphoreType.DMA((len(held) + 2 * tiles,)),
            pltpu.SemaphoreType.DMA((2,)),
        ],
        compiler_params=pltpu.CompilerParams(vmem_limit_bytes=GRANT),
        cost_estimate=pl.CostEstimate(
            flops=4 * rows * mine * features * wide, bytes_accessed=moved, transcendentals=rows * mine * wide
        ),
        name="product",
    )(tokens, gate_weight, up_weight, *[value for *_, value in held], *after)


def place(blocks, mine, ff):
    rows = lax.axis_size("row")
    width = ff // rows

    def body(*refs):
        out, sems = refs[-2], refs[-1]
        z = lax.axis_index("row")
        copies = []
        for ref, (shift, low, value) in zip(refs, blocks):
            came = lax.rem(z + rows - shift, rows)
            start = pl.multiple_of(came * width + low, LANES)
            copies.append(pltpu.make_async_copy(
                ref, out.at[:, pl.ds(start, value.shape[1])], sems.at[len(copies)]
            ))
        run_all(copies)

    return pl.pallas_call(
        body,
        out_shape=jax.ShapeDtypeStruct((mine, ff), jnp.bfloat16),
        in_specs=[ANY] * len(blocks),
        out_specs=pl.BlockSpec(memory_space=pltpu.VMEM),
        scratch_shapes=[pltpu.SemaphoreType.DMA((len(blocks),))],
        compiler_params=pltpu.CompilerParams(vmem_limit_bytes=GRANT),
        cost_estimate=pl.CostEstimate(flops=0, bytes_accessed=4 * mine * ff, transcendentals=0),
        name="place",
    )(*[value for _, _, value in blocks])


def in_tiles(tokens, gate_weight, up_weight):
    rows, parts = lax.axis_size("row"), lax.axis_size("parts")
    mine, ff = tokens.shape[0], gate_weight.shape[1]
    width = ff // rows
    units = width // LANES

    block_rows = lax.all_gather(tokens, "row", axis=0, tiled=True)

    edges = [0]
    for piece in range(len(PIECES)):
        edge = units * sum(PIECES[:piece + 1]) // sum(PIECES) * LANES
        if edge > edges[-1]:
            edges.append(edge)
    spans = list(zip(edges[:-1], edges[1:]))

    def weights(shift, low, high, users):
        after = sent[-1:] + arrived[:len(sent) - 2][-1:] * (len(sent) > 2) + swapped[:len(sent) - 3][-1:] * (len(sent) > 3)
        sent.append(pack(gate_weight, up_weight, shift, low, high - low, after))
        arrived.append(lax.ppermute(sent[-1], "row", around(rows, shift)))
        came = hold(arrived[-1], done) if done else arrived[-1]
        for turn in range(parts):
            if turn:
                swapped.append(lax.ppermute(came, "parts", around(parts, -turn)))
            for n in users:
                held[n].append((shift, turn, low, swapped[-1] if turn else came))

    def hidden_of(n, after):
        low, high = spans[n]
        outs = product(whole, gate_weight, up_weight, held[n], low, high - low, mine, after)
        back = [lax.ppermute(outs[shift], "row", around(rows, shift)) for shift in range(1, rows)]
        blocks.extend((shift, low, value) for shift, value in enumerate([outs[0]] + back))
        done.append(outs[0])
        returned.append(back)

    last = len(spans) - 1
    far, *near = by_distance(rows)
    plan = [(far, 0, spans[max(last - 1, 0)][1], range(max(last, 1)))]
    for n, (low, high) in enumerate(spans):
        plan += [(shift, low, high, [n]) for shift in ([far] if 0 < n == last else []) + near]
    sent, arrived, swapped, done, returned, blocks = [], [], [], [], [], []
    held = [[] for _ in spans]
    for step in plan:
        if last and len(sent) == len(plan) - 2:
            hidden_of(0, [])
        weights(*step)
        if len(sent) == min(3, len(plan)):
            whole = lax.all_gather(hold(block_rows, arrived[:1] + sent[1:3]), "col", axis=1, tiled=True)
    for n in range(min(last, 1), last + 1):
        hidden_of(n, done[-1:] + (returned[n - 2] if n > 1 else []))
    return place(blocks, mine, ff)


def at_once(tokens, gate_weight, up_weight):
    rows, parts = lax.axis_size("row"), lax.axis_size("parts")
    y = lax.axis_index("parts")
    mine, ff = tokens.shape[0], gate_weight.shape[1]
    depth = gate_weight.shape[0]
    share, width = depth // parts, ff // rows

    whole = lax.all_gather(lax.all_gather(tokens, "row", axis=0, tiled=True), "col", axis=1, tiled=True)
    everyone = whole.shape[0]
    by_share = whole.reshape(everyone, rows, parts, share)
    sent = jnp.stack([
        lax.dynamic_slice(w, (y * share, 0), (share, ff)).reshape(share, rows, width).transpose(1, 0, 2)
        for w in (gate_weight, up_weight)
    ])
    held = lax.all_to_all(sent, "row", 1, 1, tiled=True)
    gate = up = 0.0
    for turn in range(parts):
        features = lax.dynamic_index_in_dim(by_share, (y + turn) % parts, 2, keepdims=False)
        features = features.reshape(everyone, rows * share)
        block = lax.ppermute(held, "parts", around(parts, -turn)) if turn else held
        block = block.reshape(2, rows * share, width)
        gate += jnp.dot(features, block[0], preferred_element_type=jnp.float32)
        up += jnp.dot(features, block[1], preferred_element_type=jnp.float32)
    done = (jax.nn.silu(gate) * up).astype(jnp.bfloat16)
    back = lax.all_to_all(done.reshape(rows, mine, width), "row", 0, 0, tiled=True)
    return back.transpose(1, 0, 2).reshape(mine, ff)


def on_device(tokens, gate_weight, up_weight):
    rows, parts = lax.axis_size("row"), lax.axis_size("parts")
    aligned = (
        gate_weight.shape[1] % (rows * LANES) == 0
        and gate_weight.shape[0] % (parts * 16) == 0
        and tokens.shape[0] % 16 == 0
    )
    return (in_tiles if aligned else at_once)(tokens, gate_weight, up_weight)


def solution(mesh):
    placed = (P(("parts", "row"), "col"), P("row", "col"), P("row", "col"))
    return jax.shard_map(
        on_device, mesh=mesh, in_specs=placed, out_specs=P(("parts", "row"), "col"), check_vma=False
    )
```

```python
import jax
import jax.numpy as jnp
from jax import lax
from jax.experimental import pallas as pl
from jax.experimental.pallas import tpu as pltpu
from jax.sharding import PartitionSpec as P

PIECES = (3, 2, 2)
GRANT = 60 * 2**20
LANES = 128
ANY = pl.BlockSpec(memory_space=pl.ANY)


def around(size, shift):
    return [(i, (i + shift) % size) for i in range(size)]


def by_distance(size):
    return sorted(range(1, size), key=lambda shift: -min(shift, size - shift))


def run_all(copies):
    for copy in copies:
        copy.start()
    for copy in copies:
        copy.wait()


def pack(gate_weight, up_weight, shift, low, wide, after):
    depth, ff = gate_weight.shape
    rows, parts = lax.axis_size("row"), lax.axis_size("parts")
    share, width, tiles = depth // parts, ff // rows, wide // LANES

    def body(*refs):
        weights, sent, sems = refs[:2], refs[-2], refs[-1]
        to = lax.rem(lax.axis_index("row") + shift, rows)
        first = pl.multiple_of(lax.axis_index("parts") * share, share)
        copies = []
        for j in range(tiles):
            start = pl.multiple_of(to * width + low + j * LANES, LANES)
            for g, weight in enumerate(weights):
                copies.append(pltpu.make_async_copy(
                    weight.at[pl.ds(first, share), pl.ds(start, LANES)],
                    sent.at[:, pl.ds((2 * j + g) * LANES, LANES)],
                    sems.at[2 * j + g],
                ))
        run_all(copies)

    size = share * 2 * wide * 2
    return pl.pallas_call(
        body,
        out_shape=jax.ShapeDtypeStruct((share, 2 * wide), gate_weight.dtype),
        in_specs=[ANY] * (2 + len(after)),
        out_specs=pl.BlockSpec(memory_space=pltpu.VMEM),
        scratch_shapes=[pltpu.SemaphoreType.DMA((2 * tiles,))],
        compiler_params=pltpu.CompilerParams(vmem_limit_bytes=GRANT),
        cost_estimate=pl.CostEstimate(flops=0, bytes_accessed=2 * size, transcendentals=0),
        name="pack",
    )(gate_weight, up_weight, *after)


def hold(value, after):
    def body(*refs):
        pass

    return pl.pallas_call(
        body,
        out_shape=jax.ShapeDtypeStruct(value.shape, value.dtype),
        in_specs=[ANY] * (1 + len(after)),
        out_specs=ANY,
        input_output_aliases={0: 0},
        name="hold",
    )(value, *after)


def product(tokens, gate_weight, up_weight, held, low, wide, mine, after):
    depth, ff = gate_weight.shape
    rows, parts = lax.axis_size("row"), lax.axis_size("parts")
    share, width, tiles = depth // parts, ff // rows, wide // LANES
    features = rows * depth
    order = by_distance(rows) + [0]

    def body(tokens_ref, gate_ref, up_ref, *refs):
        held_refs = refs[:len(held)]
        outs = refs[len(held) + len(after):][:rows]
        stack, block, sems, block_sems = refs[-4:]
        z, y = lax.axis_index("row"), lax.axis_index("parts")

        def fetch(step):
            to = lax.rem(z + order[step], rows)
            return pltpu.make_async_copy(
                tokens_ref.at[pl.ds(pl.multiple_of(to * mine, mine), mine), :],
                block.at[step % 2],
                block_sems.at[step % 2],
            )

        copies = [[] for _ in range(tiles)]
        own = pl.multiple_of(z * depth, depth)
        for j in range(tiles):
            for ref, (shift, turn, begin, _) in zip(held_refs, held):
                came = lax.rem(z + rows - shift, rows)
                half = lax.rem(y + turn, parts)
                start = pl.multiple_of(came * depth + half * share, share)
                copies[j].append(pltpu.make_async_copy(
                    ref.at[:, pl.ds(2 * (low - begin + j * LANES), 2 * LANES)],
                    stack.at[pl.ds(start, share), pl.ds(2 * j * LANES, 2 * LANES)],
                    sems.at[j, len(copies[j])],
                ))
            start = pl.multiple_of(z * width + low + j * LANES, LANES)
            for g, weight in enumerate((gate_ref, up_ref)):
                copies[j].append(pltpu.make_async_copy(
                    weight.at[:, pl.ds(start, LANES)],
                    stack.at[pl.ds(own, depth), pl.ds((2 * j + g) * LANES, LANES)],
                    sems.at[j, len(copies[j])],
                ))

        def tile(step, j):
            both = jnp.dot(
                block[step % 2],
                stack[:, pl.ds(pl.multiple_of(j * 2 * LANES, 2 * LANES), 2 * LANES)],
                preferred_element_type=jnp.float32,
            )
            gate, up = both[:, :LANES], both[:, LANES:]
            outs[order[step]][:, pl.ds(pl.multiple_of(j * LANES, LANES), LANES)] = (
                jax.nn.silu(gate) * up
            ).astype(jnp.bfloat16)

        def first_tiles():
            for j in range(tiles):
                for copy in copies[j]:
                    copy.wait()
                tile(0, j)

        fetch(0).start()
        for copy in sum(copies, []):
            copy.start()
        for step in range(rows):
            fetch(step).wait()
            if step + 1 < rows:
                fetch(step + 1).start()
            if step:
                lax.fori_loop(0, tiles, lambda j, carry, step=step: (tile(step, j), carry)[1], 0)
            else:
                first_tiles()

    moved = 2 * (rows * mine * features + features * 2 * wide + rows * mine * wide)
    return pl.pallas_call(
        body,
        out_shape=[jax.ShapeDtypeStruct((mine, wide), jnp.bfloat16)] * rows,
        in_specs=[ANY] * (3 + len(held) + len(after)),
        out_specs=[pl.BlockSpec(memory_space=pltpu.VMEM)] * rows,
        scratch_shapes=[
            pltpu.VMEM((features, 2 * wide), gate_weight.dtype),
            pltpu.VMEM((2, mine, features), tokens.dtype),
            pltpu.SemaphoreType.DMA((tiles, len(held) + 2)),
            pltpu.SemaphoreType.DMA((2,)),
        ],
        compiler_params=pltpu.CompilerParams(vmem_limit_bytes=GRANT),
        cost_estimate=pl.CostEstimate(
            flops=4 * rows * mine * features * wide, bytes_accessed=moved, transcendentals=rows * mine * wide
        ),
        name="product",
    )(tokens, gate_weight, up_weight, *[value for *_, value in held], *after)


def place(blocks, mine, ff, onto=None):
    rows = lax.axis_size("row")
    width = ff // rows
    known = [] if onto is None else [onto]

    def body(*refs):
        refs, out, slots, sems = refs[len(known):], refs[len(known) + len(blocks)], refs[-2 - len(blocks):-2], refs[-2:]
        z = lax.axis_index("row")
        loads, stores = [], []
        for n, (ref, slot, (shift, low, value)) in enumerate(zip(refs, slots, blocks)):
            came = lax.rem(z + rows - shift, rows)
            start = pl.multiple_of(came * width + low, LANES)
            loads.append(pltpu.make_async_copy(ref, slot, sems[0].at[n]))
            stores.append(pltpu.make_async_copy(slot, out.at[:, pl.ds(start, value.shape[1])], sems[1].at[n]))
        for load in loads:
            load.start()
        for load, store in zip(loads, stores):
            load.wait()
            store.start()
        for store in stores:
            store.wait()

    values = [value for _, _, value in blocks]
    return pl.pallas_call(
        body,
        out_shape=jax.ShapeDtypeStruct((mine, ff), jnp.bfloat16),
        in_specs=[ANY] * (len(known) + len(blocks)),
        out_specs=ANY,
        scratch_shapes=[pltpu.VMEM(value.shape, value.dtype) for value in values]
        + [pltpu.SemaphoreType.DMA((len(blocks),))] * 2,
        input_output_aliases={0: 0} if known else {},
        compiler_params=pltpu.CompilerParams(vmem_limit_bytes=GRANT),
        cost_estimate=pl.CostEstimate(
            flops=0, bytes_accessed=4 * sum(value.size for value in values), transcendentals=0
        ),
        name="place",
    )(*known, *values)


def in_tiles(tokens, gate_weight, up_weight):
    rows, parts = lax.axis_size("row"), lax.axis_size("parts")
    mine, ff = tokens.shape[0], gate_weight.shape[1]
    width = ff // rows
    units = width // LANES

    block_rows = lax.all_gather(tokens, "row", axis=0, tiled=True)

    edges = [0]
    for piece in range(len(PIECES)):
        edge = units * sum(PIECES[:piece + 1]) // sum(PIECES) * LANES
        if edge > edges[-1]:
            edges.append(edge)
    spans = list(zip(edges[:-1], edges[1:]))

    def weights(shift, low, high, users):
        after = sent[-1:] + arrived[:len(sent) - 2][-1:] * (len(sent) > 2) + swapped[:len(sent) - 3][-1:] * (len(sent) > 3)
        sent.append(pack(gate_weight, up_weight, shift, low, high - low, after))
        arrived.append(lax.ppermute(sent[-1], "row", around(rows, shift)))
        came = hold(arrived[-1], done) if done else arrived[-1]
        for turn in range(parts):
            if turn:
                swapped.append(lax.ppermute(came, "parts", around(parts, -turn)))
            for n in users:
                held[n].append((shift, turn, low, swapped[-1] if turn else came))

    def hidden_of(n, after):
        low, high = spans[n]
        outs = product(whole, gate_weight, up_weight, held[n], low, high - low, mine, after)
        back = [lax.ppermute(outs[shift], "row", around(rows, shift)) for shift in range(1, rows)]
        blocks.extend((shift, low, value) for shift, value in enumerate([outs[0]] + back))
        done.append(outs[0])
        returned.append(back)

    last = len(spans) - 1
    far, *near = by_distance(rows)
    plan = [(far, 0, spans[max(last - 1, 0)][1], range(max(last, 1)))]
    for n, (low, high) in enumerate(spans):
        plan += [(shift, low, high, [n]) for shift in near]
        if n == 0 < last:
            plan.append((far, *spans[last], [last]))
    sent, arrived, swapped, done, returned, blocks = [], [], [], [], [], []
    held = [[] for _ in spans]
    for step in plan:
        if last and len(sent) == len(plan) - 2:
            hidden_of(0, [])
        weights(*step)
        if len(sent) == min(3, len(plan)):
            whole = lax.all_gather(hold(block_rows, arrived[:1] + sent[1:3]), "col", axis=1, tiled=True)
    for n in range(min(last, 1), last + 1):
        hidden_of(n, done[-1:] + (returned[n - 2] if n > 1 else []))
    early = len(blocks) - rows if last else len(blocks)
    out = place(blocks[:early], mine, ff)
    return place(blocks[early:], mine, ff, out) if last else out


def at_once(tokens, gate_weight, up_weight):
    rows, parts = lax.axis_size("row"), lax.axis_size("parts")
    y = lax.axis_index("parts")
    mine, ff = tokens.shape[0], gate_weight.shape[1]
    depth = gate_weight.shape[0]
    share, width = depth // parts, ff // rows

    whole = lax.all_gather(lax.all_gather(tokens, "row", axis=0, tiled=True), "col", axis=1, tiled=True)
    everyone = whole.shape[0]
    by_share = whole.reshape(everyone, rows, parts, share)
    sent = jnp.stack([
        lax.dynamic_slice(w, (y * share, 0), (share, ff)).reshape(share, rows, width).transpose(1, 0, 2)
        for w in (gate_weight, up_weight)
    ])
    held = lax.all_to_all(sent, "row", 1, 1, tiled=True)
    gate = up = 0.0
    for turn in range(parts):
        features = lax.dynamic_index_in_dim(by_share, (y + turn) % parts, 2, keepdims=False)
        features = features.reshape(everyone, rows * share)
        block = lax.ppermute(held, "parts", around(parts, -turn)) if turn else held
        block = block.reshape(2, rows * share, width)
        gate += jnp.dot(features, block[0], preferred_element_type=jnp.float32)
        up += jnp.dot(features, block[1], preferred_element_type=jnp.float32)
    done = (jax.nn.silu(gate) * up).astype(jnp.bfloat16)
    back = lax.all_to_all(done.reshape(rows, mine, width), "row", 0, 0, tiled=True)
    return back.transpose(1, 0, 2).reshape(mine, ff)


def on_device(tokens, gate_weight, up_weight):
    rows, parts = lax.axis_size("row"), lax.axis_size("parts")
    aligned = (
        gate_weight.shape[1] % (rows * LANES) == 0
        and gate_weight.shape[0] % (parts * 16) == 0
        and tokens.shape[0] % 16 == 0
    )
    return (in_tiles if aligned else at_once)(tokens, gate_weight, up_weight)


def solution(mesh):
    placed = (P(("parts", "row"), "col"), P("row", "col"), P("row", "col"))
    return jax.shard_map(
        on_device, mesh=mesh, in_specs=placed, out_specs=P(("parts", "row"), "col"), check_vma=False
    )
```

```python
import jax
import jax.numpy as jnp
from jax import lax
from jax.experimental import pallas as pl
from jax.experimental.pallas import tpu as pltpu
from jax.sharding import PartitionSpec as P

PIECES = (3, 2, 2)
GRANT = 60 * 2**20
LANES = 128
ANY = pl.BlockSpec(memory_space=pl.ANY)


def around(size, shift):
    return [(i, (i + shift) % size) for i in range(size)]


def by_distance(size):
    return sorted(range(1, size), key=lambda shift: -min(shift, size - shift))


def run_all(copies):
    for copy in copies:
        copy.start()
    for copy in copies:
        copy.wait()


def pack(gate_weight, up_weight, shift, low, wide, after):
    depth, ff = gate_weight.shape
    rows, parts = lax.axis_size("row"), lax.axis_size("parts")
    share, width, tiles = depth // parts, ff // rows, wide // LANES

    def body(*refs):
        weights, sent, sems = refs[:2], refs[-2], refs[-1]
        to = lax.rem(lax.axis_index("row") + shift, rows)
        first = pl.multiple_of(lax.axis_index("parts") * share, share)
        copies = []
        for j in range(tiles):
            start = pl.multiple_of(to * width + low + j * LANES, LANES)
            for g, weight in enumerate(weights):
                copies.append(pltpu.make_async_copy(
                    weight.at[pl.ds(first, share), pl.ds(start, LANES)],
                    sent.at[:, pl.ds((2 * j + g) * LANES, LANES)],
                    sems.at[2 * j + g],
                ))
        run_all(copies)

    size = share * 2 * wide * 2
    return pl.pallas_call(
        body,
        out_shape=jax.ShapeDtypeStruct((share, 2 * wide), gate_weight.dtype),
        in_specs=[ANY] * (2 + len(after)),
        out_specs=pl.BlockSpec(memory_space=pltpu.VMEM),
        scratch_shapes=[pltpu.SemaphoreType.DMA((2 * tiles,))],
        compiler_params=pltpu.CompilerParams(vmem_limit_bytes=GRANT),
        cost_estimate=pl.CostEstimate(flops=0, bytes_accessed=2 * size, transcendentals=0),
        name="pack",
    )(gate_weight, up_weight, *after)


def hold(value, after):
    def body(*refs):
        pass

    return pl.pallas_call(
        body,
        out_shape=jax.ShapeDtypeStruct(value.shape, value.dtype),
        in_specs=[ANY] * (1 + len(after)),
        out_specs=ANY,
        input_output_aliases={0: 0},
        name="hold",
    )(value, *after)


def product(tokens, gate_weight, up_weight, held, low, wide, mine, after):
    depth, ff = gate_weight.shape
    rows, parts = lax.axis_size("row"), lax.axis_size("parts")
    share, width, tiles = depth // parts, ff // rows, wide // LANES
    features = rows * depth
    order = by_distance(rows) + [0]

    def body(tokens_ref, gate_ref, up_ref, *refs):
        held_refs = refs[:len(held)]
        outs = refs[len(held) + len(after):][:rows]
        stack, block, sems, block_sems = refs[-4:]
        z, y = lax.axis_index("row"), lax.axis_index("parts")

        def fetch(step):
            to = lax.rem(z + order[step], rows)
            return pltpu.make_async_copy(
                tokens_ref.at[pl.ds(pl.multiple_of(to * mine, mine), mine), :],
                block.at[step % 2],
                block_sems.at[step % 2],
            )

        copies = []
        for ref, (shift, turn, begin, _) in zip(held_refs, held):
            came = lax.rem(z + rows - shift, rows)
            half = lax.rem(y + turn, parts)
            start = pl.multiple_of(came * depth + half * share, share)
            copies.append(pltpu.make_async_copy(
                ref.at[:, pl.ds(2 * (low - begin), 2 * wide)], stack.at[pl.ds(start, share), :], sems.at[len(copies)]
            ))
        own = pl.multiple_of(z * depth, depth)
        for j in range(tiles):
            start = pl.multiple_of(z * width + low + j * LANES, LANES)
            for g, weight in enumerate((gate_ref, up_ref)):
                copies.append(pltpu.make_async_copy(
                    weight.at[:, pl.ds(start, LANES)],
                    stack.at[pl.ds(own, depth), pl.ds((2 * j + g) * LANES, LANES)],
                    sems.at[len(copies)],
                ))
        fetch(0).start()
        run_all(copies)
        for step, shift in enumerate(order):
            fetch(step).wait()
            if step + 1 < rows:
                fetch(step + 1).start()

            def tile(j, carry, step=step, shift=shift):
                both = jnp.dot(
                    block[step % 2],
                    stack[:, pl.ds(pl.multiple_of(j * 2 * LANES, 2 * LANES), 2 * LANES)],
                    preferred_element_type=jnp.float32,
                )
                gate, up = both[:, :LANES], both[:, LANES:]
                outs[shift][:, pl.ds(pl.multiple_of(j * LANES, LANES), LANES)] = (
                    jax.nn.silu(gate) * up
                ).astype(jnp.bfloat16)
                return carry

            lax.fori_loop(0, tiles, tile, 0)

    moved = 2 * (rows * mine * features + features * 2 * wide + rows * mine * wide)
    return pl.pallas_call(
        body,
        out_shape=[jax.ShapeDtypeStruct((mine, wide), jnp.bfloat16)] * rows,
        in_specs=[ANY] * (3 + len(held) + len(after)),
        out_specs=[pl.BlockSpec(memory_space=pltpu.VMEM)] * rows,
        scratch_shapes=[
            pltpu.VMEM((features, 2 * wide), gate_weight.dtype),
            pltpu.VMEM((2, mine, features), tokens.dtype),
            pltpu.SemaphoreType.DMA((len(held) + 2 * tiles,)),
            pltpu.SemaphoreType.DMA((2,)),
        ],
        compiler_params=pltpu.CompilerParams(vmem_limit_bytes=GRANT),
        cost_estimate=pl.CostEstimate(
            flops=4 * rows * mine * features * wide, bytes_accessed=moved, transcendentals=rows * mine * wide
        ),
        name="product",
    )(tokens, gate_weight, up_weight, *[value for *_, value in held], *after)


def ordered(lower, upper, after):
    rows = lax.axis_size("row")
    mine, near = lower[0].shape

    def body(*refs):
        lower_refs, upper_refs = refs[:rows], refs[rows:2 * rows - 1]
        out, slots, sems = refs[-3:]
        z = lax.axis_index("row")
        for here in range(rows):

            @pl.when(z == here)
            def _(here=here):
                loads, stores = [], []
                for row in range(rows):
                    source = lower_refs[here - row] if row <= here else upper_refs[row - here - 1]
                    loads.append(pltpu.make_async_copy(source, slots.at[row], sems.at[0, row]))
                    stores.append(pltpu.make_async_copy(
                        slots.at[row], out.at[pl.ds(row * mine, mine), :], sems.at[1, row]
                    ))
                for load in loads:
                    load.start()
                for load, store in zip(loads, stores):
                    load.wait()
                    store.start()
                for store in stores:
                    store.wait()

    values = lower + upper[1:] + after
    return pl.pallas_call(
        body,
        out_shape=jax.ShapeDtypeStruct((rows * mine, near), lower[0].dtype),
        in_specs=[ANY] * len(values),
        out_specs=ANY,
        scratch_shapes=[
            pltpu.VMEM((rows, mine, near), lower[0].dtype),
            pltpu.SemaphoreType.DMA((2, rows)),
        ],
        compiler_params=pltpu.CompilerParams(vmem_limit_bytes=GRANT),
        cost_estimate=pl.CostEstimate(flops=0, bytes_accessed=4 * rows * mine * near, transcendentals=0),
        name="ordered",
    )(*values)


def place(blocks, mine, ff, onto=None):
    rows = lax.axis_size("row")
    width = ff // rows
    known = [] if onto is None else [onto]

    def body(*refs):
        refs, out, slots, sems = refs[len(known):], refs[len(known) + len(blocks)], refs[-2 - len(blocks):-2], refs[-2:]
        z = lax.axis_index("row")
        loads, stores = [], []
        for n, (ref, slot, (shift, low, value)) in enumerate(zip(refs, slots, blocks)):
            came = lax.rem(z + rows - shift, rows)
            start = pl.multiple_of(came * width + low, LANES)
            loads.append(pltpu.make_async_copy(ref, slot, sems[0].at[n]))
            stores.append(pltpu.make_async_copy(slot, out.at[:, pl.ds(start, value.shape[1])], sems[1].at[n]))
        for load in loads:
            load.start()
        for load, store in zip(loads, stores):
            load.wait()
            store.start()
        for store in stores:
            store.wait()

    values = [value for _, _, value in blocks]
    return pl.pallas_call(
        body,
        out_shape=jax.ShapeDtypeStruct((mine, ff), jnp.bfloat16),
        in_specs=[ANY] * (len(known) + len(blocks)),
        out_specs=ANY,
        scratch_shapes=[pltpu.VMEM(value.shape, value.dtype) for value in values]
        + [pltpu.SemaphoreType.DMA((len(blocks),))] * 2,
        input_output_aliases={0: 0} if known else {},
        compiler_params=pltpu.CompilerParams(vmem_limit_bytes=GRANT),
        cost_estimate=pl.CostEstimate(
            flops=0, bytes_accessed=4 * sum(value.size for value in values), transcendentals=0
        ),
        name="place",
    )(*known, *values)


def in_tiles(tokens, gate_weight, up_weight):
    rows, parts = lax.axis_size("row"), lax.axis_size("parts")
    mine, ff = tokens.shape[0], gate_weight.shape[1]
    width = ff // rows
    units = width // LANES

    lower, upper = [tokens], [tokens]
    for step in range(1, rows):
        lower.append(lax.ppermute(lower[-1], "row", [(i, i + 1) for i in range(step - 1, rows - 1)]))
        upper.append(lax.ppermute(upper[-1], "row", [(i, i - 1) for i in range(1, rows - step + 1)]))

    edges = [0]
    for piece in range(len(PIECES)):
        edge = units * sum(PIECES[:piece + 1]) // sum(PIECES) * LANES
        if edge > edges[-1]:
            edges.append(edge)
    spans = list(zip(edges[:-1], edges[1:]))

    def weights(shift, low, high, users):
        after = sent[-1:] + arrived[:len(sent) - 2][-1:] * (len(sent) > 2) + swapped[:len(sent) - 3][-1:] * (len(sent) > 3)
        sent.append(pack(gate_weight, up_weight, shift, low, high - low, after))
        arrived.append(lax.ppermute(sent[-1], "row", around(rows, shift)))
        came = hold(arrived[-1], done) if done else arrived[-1]
        for turn in range(parts):
            if turn:
                swapped.append(lax.ppermute(came, "parts", around(parts, -turn)))
            for n in users:
                held[n].append((shift, turn, low, swapped[-1] if turn else came))

    def hidden_of(n, after):
        low, high = spans[n]
        outs = product(whole, gate_weight, up_weight, held[n], low, high - low, mine, after)
        back = [lax.ppermute(outs[shift], "row", around(rows, shift)) for shift in range(1, rows)]
        blocks.extend((shift, low, value) for shift, value in enumerate([outs[0]] + back))
        done.append(outs[0])
        returned.append(back)

    last = len(spans) - 1
    far, *near = by_distance(rows)
    plan = [(far, 0, spans[max(last - 1, 0)][1], range(max(last, 1)))]
    for n, (low, high) in enumerate(spans):
        plan += [(shift, low, high, [n]) for shift in near]
        if n == 0 < last:
            plan.append((far, *spans[last], [last]))
    sent, arrived, swapped, done, returned, blocks = [], [], [], [], [], []
    held = [[] for _ in spans]
    for step in plan:
        if last and len(sent) == max(len(plan) - 3, 3):
            hidden_of(0, [])
        weights(*step)
        if len(sent) == min(3, len(plan)):
            whole = lax.all_gather(ordered(lower, upper, arrived[:1] + sent[1:3]), "col", axis=1, tiled=True)
    for n in range(min(last, 1), last + 1):
        hidden_of(n, done[-1:] + (returned[n - 2] if n > 1 else []))
    early = len(blocks) - rows if last else len(blocks)
    out = place(blocks[:early], mine, ff)
    return place(blocks[early:], mine, ff, out) if last else out


def at_once(tokens, gate_weight, up_weight):
    rows, parts = lax.axis_size("row"), lax.axis_size("parts")
    y = lax.axis_index("parts")
    mine, ff = tokens.shape[0], gate_weight.shape[1]
    depth = gate_weight.shape[0]
    share, width = depth // parts, ff // rows

    whole = lax.all_gather(lax.all_gather(tokens, "row", axis=0, tiled=True), "col", axis=1, tiled=True)
    everyone = whole.shape[0]
    by_share = whole.reshape(everyone, rows, parts, share)
    sent = jnp.stack([
        lax.dynamic_slice(w, (y * share, 0), (share, ff)).reshape(share, rows, width).transpose(1, 0, 2)
        for w in (gate_weight, up_weight)
    ])
    held = lax.all_to_all(sent, "row", 1, 1, tiled=True)
    gate = up = 0.0
    for turn in range(parts):
        features = lax.dynamic_index_in_dim(by_share, (y + turn) % parts, 2, keepdims=False)
        features = features.reshape(everyone, rows * share)
        block = lax.ppermute(held, "parts", around(parts, -turn)) if turn else held
        block = block.reshape(2, rows * share, width)
        gate += jnp.dot(features, block[0], preferred_element_type=jnp.float32)
        up += jnp.dot(features, block[1], preferred_element_type=jnp.float32)
    done = (jax.nn.silu(gate) * up).astype(jnp.bfloat16)
    back = lax.all_to_all(done.reshape(rows, mine, width), "row", 0, 0, tiled=True)
    return back.transpose(1, 0, 2).reshape(mine, ff)


def on_device(tokens, gate_weight, up_weight):
    rows, parts = lax.axis_size("row"), lax.axis_size("parts")
    aligned = (
        gate_weight.shape[1] % (rows * LANES) == 0
        and gate_weight.shape[0] % (parts * 16) == 0
        and tokens.shape[0] % 16 == 0
    )
    return (in_tiles if aligned else at_once)(tokens, gate_weight, up_weight)


def solution(mesh):
    placed = (P(("parts", "row"), "col"), P("row", "col"), P("row", "col"))
    return jax.shard_map(
        on_device, mesh=mesh, in_specs=placed, out_specs=P(("parts", "row"), "col"), check_vma=False
    )
```

```python
import jax
import jax.numpy as jnp
from jax import lax
from jax.experimental import pallas as pl
from jax.experimental.pallas import tpu as pltpu
from jax.sharding import PartitionSpec as P

PIECES = (3, 2, 2)
GRANT = 60 * 2**20
LANES = 128
ANY = pl.BlockSpec(memory_space=pl.ANY)


def around(size, shift):
    return [(i, (i + shift) % size) for i in range(size)]


def by_distance(size):
    return sorted(range(1, size), key=lambda shift: -min(shift, size - shift))


def run_all(copies):
    for copy in copies:
        copy.start()
    for copy in copies:
        copy.wait()


def pack(gate_weight, up_weight, shift, low, wide, after):
    depth, ff = gate_weight.shape
    rows, parts = lax.axis_size("row"), lax.axis_size("parts")
    share, width, tiles = depth // parts, ff // rows, wide // LANES

    def body(*refs):
        weights, sent, sems = refs[:2], refs[-2], refs[-1]
        to = lax.rem(lax.axis_index("row") + shift, rows)
        first = pl.multiple_of(lax.axis_index("parts") * share, share)
        copies = []
        for j in range(tiles):
            start = pl.multiple_of(to * width + low + j * LANES, LANES)
            for g, weight in enumerate(weights):
                copies.append(pltpu.make_async_copy(
                    weight.at[pl.ds(first, share), pl.ds(start, LANES)],
                    sent.at[:, pl.ds((2 * j + g) * LANES, LANES)],
                    sems.at[2 * j + g],
                ))
        run_all(copies)

    size = share * 2 * wide * 2
    return pl.pallas_call(
        body,
        out_shape=jax.ShapeDtypeStruct((share, 2 * wide), gate_weight.dtype),
        in_specs=[ANY] * (2 + len(after)),
        out_specs=pl.BlockSpec(memory_space=pltpu.VMEM),
        scratch_shapes=[pltpu.SemaphoreType.DMA((2 * tiles,))],
        compiler_params=pltpu.CompilerParams(vmem_limit_bytes=GRANT),
        cost_estimate=pl.CostEstimate(flops=0, bytes_accessed=2 * size, transcendentals=0),
        name="pack",
    )(gate_weight, up_weight, *after)


def hold(value, after):
    def body(*refs):
        pass

    return pl.pallas_call(
        body,
        out_shape=jax.ShapeDtypeStruct(value.shape, value.dtype),
        in_specs=[ANY] * (1 + len(after)),
        out_specs=ANY,
        input_output_aliases={0: 0},
        name="hold",
    )(value, *after)


def product(tokens, gate_weight, up_weight, held, low, wide, mine, after):
    depth, ff = gate_weight.shape
    rows, parts = lax.axis_size("row"), lax.axis_size("parts")
    share, width, tiles = depth // parts, ff // rows, wide // LANES
    features = rows * depth
    sources = by_step(rows)
    order = by_distance(rows) + [0]

    def body(*refs):
        token_refs, (gate_ref, up_ref), refs = refs[:rows], refs[rows:rows + 2], refs[rows + 2:]
        held_refs = refs[:len(held)]
        outs = refs[len(held) + len(after):][:rows]
        stack, block, sems, block_sems = refs[-4:]
        z, y = lax.axis_index("row"), lax.axis_index("parts")

        def fetched(step, slot=0):
            return pltpu.make_async_copy(token_refs[slot], block.at[step % 2], block_sems.at[step % 2])

        def fetch(step):
            for here in range(rows):
                slot = sources[here].index((here + order[step]) % rows)
                pl.when(z == here)(lambda slot=slot: fetched(step, slot).start())

        copies = []
        for ref, (shift, turn, begin, _) in zip(held_refs, held):
            came = lax.rem(z + rows - shift, rows)
            half = lax.rem(y + turn, parts)
            start = pl.multiple_of(came * depth + half * share, share)
            copies.append(pltpu.make_async_copy(
                ref.at[:, pl.ds(2 * (low - begin), 2 * wide)], stack.at[pl.ds(start, share), :], sems.at[len(copies)]
            ))
        own = pl.multiple_of(z * depth, depth)
        for j in range(tiles):
            start = pl.multiple_of(z * width + low + j * LANES, LANES)
            for g, weight in enumerate((gate_ref, up_ref)):
                copies.append(pltpu.make_async_copy(
                    weight.at[:, pl.ds(start, LANES)],
                    stack.at[pl.ds(own, depth), pl.ds((2 * j + g) * LANES, LANES)],
                    sems.at[len(copies)],
                ))
        fetch(0)
        run_all(copies)
        for step, shift in enumerate(order):
            fetched(step).wait()
            if step + 1 < rows:
                fetch(step + 1)

            def tile(j, carry, step=step, shift=shift):
                both = jnp.dot(
                    block[step % 2],
                    stack[:, pl.ds(pl.multiple_of(j * 2 * LANES, 2 * LANES), 2 * LANES)],
                    preferred_element_type=jnp.float32,
                )
                gate, up = both[:, :LANES], both[:, LANES:]
                outs[shift][:, pl.ds(pl.multiple_of(j * LANES, LANES), LANES)] = (
                    jax.nn.silu(gate) * up
                ).astype(jnp.bfloat16)
                return carry

            lax.fori_loop(0, tiles, tile, 0)

    moved = 2 * (rows * mine * features + features * 2 * wide + rows * mine * wide)
    return pl.pallas_call(
        body,
        out_shape=[jax.ShapeDtypeStruct((mine, wide), jnp.bfloat16)] * rows,
        in_specs=[ANY] * (rows + 2 + len(held) + len(after)),
        out_specs=[pl.BlockSpec(memory_space=pltpu.VMEM)] * rows,
        scratch_shapes=[
            pltpu.VMEM((features, 2 * wide), gate_weight.dtype),
            pltpu.VMEM((2, mine, features), tokens[0].dtype),
            pltpu.SemaphoreType.DMA((len(held) + 2 * tiles,)),
            pltpu.SemaphoreType.DMA((2,)),
        ],
        compiler_params=pltpu.CompilerParams(vmem_limit_bytes=GRANT),
        cost_estimate=pl.CostEstimate(
            flops=4 * rows * mine * features * wide, bytes_accessed=moved, transcendentals=rows * mine * wide
        ),
        name="product",
    )(*tokens, gate_weight, up_weight, *[value for *_, value in held], *after)


def by_step(rows):
    sources = []
    for z in range(rows):
        above = [z + step for step in range(1, rows - z)]
        below = [z - step for step in range(1, z + 1)]
        sources.append([z] + (above + below if 2 * z < rows else below + above))
    return sources


def pick(choices, after):
    rows, like = lax.axis_size("row"), choices[0][1]

    def body(*refs):
        out, sem = refs[-2:]
        z = lax.axis_index("row")
        copies = [pltpu.make_async_copy(ref, out, sem) for ref, _ in zip(refs, choices)]
        for copy, (places, _) in zip(copies, choices):
            for place in places:
                pl.when(z == place)(copy.start)
        copies[0].wait()

    return pl.pallas_call(
        body,
        out_shape=jax.ShapeDtypeStruct(like.shape, like.dtype),
        in_specs=[ANY] * (len(choices) + len(after)),
        out_specs=pl.BlockSpec(memory_space=pltpu.VMEM),
        scratch_shapes=[pltpu.SemaphoreType.DMA],
        compiler_params=pltpu.CompilerParams(vmem_limit_bytes=GRANT),
        cost_estimate=pl.CostEstimate(flops=0, bytes_accessed=4 * like.size, transcendentals=0),
        name="pick",
    )(*[value for _, value in choices], *after)


def place(blocks, mine, ff, onto=None):
    rows = lax.axis_size("row")
    width = ff // rows
    known = [] if onto is None else [onto]

    def body(*refs):
        refs, out, slots, sems = refs[len(known):], refs[len(known) + len(blocks)], refs[-2 - len(blocks):-2], refs[-2:]
        z = lax.axis_index("row")
        loads, stores = [], []
        for n, (ref, slot, (shift, low, value)) in enumerate(zip(refs, slots, blocks)):
            came = lax.rem(z + rows - shift, rows)
            start = pl.multiple_of(came * width + low, LANES)
            loads.append(pltpu.make_async_copy(ref, slot, sems[0].at[n]))
            stores.append(pltpu.make_async_copy(slot, out.at[:, pl.ds(start, value.shape[1])], sems[1].at[n]))
        for load in loads:
            load.start()
        for load, store in zip(loads, stores):
            load.wait()
            store.start()
        for store in stores:
            store.wait()

    values = [value for _, _, value in blocks]
    return pl.pallas_call(
        body,
        out_shape=jax.ShapeDtypeStruct((mine, ff), jnp.bfloat16),
        in_specs=[ANY] * (len(known) + len(blocks)),
        out_specs=ANY,
        scratch_shapes=[pltpu.VMEM(value.shape, value.dtype) for value in values]
        + [pltpu.SemaphoreType.DMA((len(blocks),))] * 2,
        input_output_aliases={0: 0} if known else {},
        compiler_params=pltpu.CompilerParams(vmem_limit_bytes=GRANT),
        cost_estimate=pl.CostEstimate(
            flops=0, bytes_accessed=4 * sum(value.size for value in values), transcendentals=0
        ),
        name="place",
    )(*known, *values)


def in_tiles(tokens, gate_weight, up_weight):
    rows, parts = lax.axis_size("row"), lax.axis_size("parts")
    mine, ff = tokens.shape[0], gate_weight.shape[1]
    width = ff // rows
    units = width // LANES

    edges = [0]
    for piece in range(len(PIECES)):
        edge = units * sum(PIECES[:piece + 1]) // sum(PIECES) * LANES
        if edge > edges[-1]:
            edges.append(edge)
    spans = list(zip(edges[:-1], edges[1:]))

    def tokens_of(before_last_step, before_last_gather):
        lower, upper = [tokens], [tokens]
        for step in range(1, rows):
            if step > 1 and step == rows - 1:
                lower[-1], upper[-1] = hold(lower[-1], before_last_step), hold(upper[-1], before_last_step)
            lower.append(lax.ppermute(lower[-1], "row", [(i, i + 1) for i in range(step - 1, rows - 1)]))
            upper.append(lax.ppermute(upper[-1], "row", [(i, i - 1) for i in range(1, rows - step + 1)]))
        for slot in range(rows):
            chosen = {}
            for here, sources in enumerate(by_step(rows)):
                chosen.setdefault(sources[slot] - here, []).append(here)
            choices = [
                (places, upper[offset] if offset > 0 else lower[-offset]) for offset, places in chosen.items()
            ]
            value = pick(choices, before_last_gather if slot == rows - 1 else []) if slot else tokens
            whole.append(lax.all_gather(value, "col", axis=1, tiled=True))

    def weights(shift, low, high, users):
        after = sent[-1:] + arrived[:len(sent) - 2][-1:] * (len(sent) > 2) + swapped[:len(sent) - 3][-1:] * (len(sent) > 3)
        sent.append(pack(gate_weight, up_weight, shift, low, high - low, after))
        arrived.append(lax.ppermute(sent[-1], "row", around(rows, shift)))
        came = hold(arrived[-1], done) if done else arrived[-1]
        for turn in range(parts):
            if turn:
                swapped.append(lax.ppermute(came, "parts", around(parts, -turn)))
            for n in users:
                held[n].append((shift, turn, low, swapped[-1] if turn else came))

    def hidden_of(n, after):
        low, high = spans[n]
        outs = product(whole, gate_weight, up_weight, held[n], low, high - low, mine, after)
        back = [lax.ppermute(outs[shift], "row", around(rows, shift)) for shift in range(1, rows)]
        blocks.extend((shift, low, value) for shift, value in enumerate([outs[0]] + back))
        done.append(outs[0])
        returned.append(back)

    last = len(spans) - 1
    far, *near = by_distance(rows)
    plan = [(far, *spans[n], [n]) for n in range(max(last, 1))]
    ahead = len(plan)
    for n, (low, high) in enumerate(spans):
        plan += [(shift, low, high, [n]) for shift in near]
        if n == 0 < last:
            plan.append((far, *spans[last], [last]))
    sent, arrived, swapped, done, returned, blocks = [], [], [], [], [], []
    held = [[] for _ in spans]
    whole = []
    for step in plan:
        if last and len(sent) == max(len(plan) - 3, 3):
            hidden_of(0, [])
        weights(*step)
        if len(sent) == min(ahead + 2, len(plan)):
            tokens_of(arrived[:1], arrived[1:ahead] + sent[ahead:])
    for n in range(min(last, 1), last + 1):
        hidden_of(n, done[-1:] + (returned[n - 2] if n > 1 else []))
    early = len(blocks) - rows if last else len(blocks)
    out = place(blocks[:early], mine, ff)
    return place(blocks[early:], mine, ff, out) if last else out


def at_once(tokens, gate_weight, up_weight):
    rows, parts = lax.axis_size("row"), lax.axis_size("parts")
    y = lax.axis_index("parts")
    mine, ff = tokens.shape[0], gate_weight.shape[1]
    depth = gate_weight.shape[0]
    share, width = depth // parts, ff // rows

    whole = lax.all_gather(lax.all_gather(tokens, "row", axis=0, tiled=True), "col", axis=1, tiled=True)
    everyone = whole.shape[0]
    by_share = whole.reshape(everyone, rows, parts, share)
    sent = jnp.stack([
        lax.dynamic_slice(w, (y * share, 0), (share, ff)).reshape(share, rows, width).transpose(1, 0, 2)
        for w in (gate_weight, up_weight)
    ])
    held = lax.all_to_all(sent, "row", 1, 1, tiled=True)
    gate = up = 0.0
    for turn in range(parts):
        features = lax.dynamic_index_in_dim(by_share, (y + turn) % parts, 2, keepdims=False)
        features = features.reshape(everyone, rows * share)
        block = lax.ppermute(held, "parts", around(parts, -turn)) if turn else held
        block = block.reshape(2, rows * share, width)
        gate += jnp.dot(features, block[0], preferred_element_type=jnp.float32)
        up += jnp.dot(features, block[1], preferred_element_type=jnp.float32)
    done = (jax.nn.silu(gate) * up).astype(jnp.bfloat16)
    back = lax.all_to_all(done.reshape(rows, mine, width), "row", 0, 0, tiled=True)
    return back.transpose(1, 0, 2).reshape(mine, ff)


def on_device(tokens, gate_weight, up_weight):
    rows, parts = lax.axis_size("row"), lax.axis_size("parts")
    aligned = (
        gate_weight.shape[1] % (rows * LANES) == 0
        and gate_weight.shape[0] % (parts * 16) == 0
        and tokens.shape[0] % 16 == 0
    )
    return (in_tiles if aligned else at_once)(tokens, gate_weight, up_weight)


def solution(mesh):
    placed = (P(("parts", "row"), "col"), P("row", "col"), P("row", "col"))
    return jax.shard_map(
        on_device, mesh=mesh, in_specs=placed, out_specs=P(("parts", "row"), "col"), check_vma=False
    )
```

```python
import jax
import jax.numpy as jnp
from jax import lax
from jax.experimental import pallas as pl
from jax.experimental.pallas import tpu as pltpu
from jax.sharding import PartitionSpec as P

PIECES = (3, 2, 2)
GRANT = 60 * 2**20
LANES = 128
ANY = pl.BlockSpec(memory_space=pl.ANY)


def around(size, shift):
    return [(i, (i + shift) % size) for i in range(size)]


def by_distance(size):
    return sorted(range(1, size), key=lambda shift: -min(shift, size - shift))


def run_all(copies):
    for copy in copies:
        copy.start()
    for copy in copies:
        copy.wait()


def pack(gate_weight, up_weight, shift, low, wide, after):
    depth, ff = gate_weight.shape
    rows, parts = lax.axis_size("row"), lax.axis_size("parts")
    share, width, tiles = depth // parts, ff // rows, wide // LANES

    def body(*refs):
        weights, sent, sems = refs[:2], refs[-2], refs[-1]
        to = lax.rem(lax.axis_index("row") + shift, rows)
        first = pl.multiple_of(lax.axis_index("parts") * share, share)
        copies = []
        for j in range(tiles):
            start = pl.multiple_of(to * width + low + j * LANES, LANES)
            for g, weight in enumerate(weights):
                copies.append(pltpu.make_async_copy(
                    weight.at[pl.ds(first, share), pl.ds(start, LANES)],
                    sent.at[:, pl.ds((2 * j + g) * LANES, LANES)],
                    sems.at[2 * j + g],
                ))
        run_all(copies)

    size = share * 2 * wide * 2
    return pl.pallas_call(
        body,
        out_shape=jax.ShapeDtypeStruct((share, 2 * wide), gate_weight.dtype),
        in_specs=[ANY] * (2 + len(after)),
        out_specs=pl.BlockSpec(memory_space=pltpu.VMEM),
        scratch_shapes=[pltpu.SemaphoreType.DMA((2 * tiles,))],
        compiler_params=pltpu.CompilerParams(vmem_limit_bytes=GRANT),
        cost_estimate=pl.CostEstimate(flops=0, bytes_accessed=2 * size, transcendentals=0),
        name="pack",
    )(gate_weight, up_weight, *after)


def hold(value, after):
    def body(*refs):
        pass

    return pl.pallas_call(
        body,
        out_shape=jax.ShapeDtypeStruct(value.shape, value.dtype),
        in_specs=[ANY] * (1 + len(after)),
        out_specs=ANY,
        input_output_aliases={0: 0},
        name="hold",
    )(value, *after)


def product(tokens, gate_weight, up_weight, held, low, wide, mine, after):
    depth, ff = gate_weight.shape
    rows, parts = lax.axis_size("row"), lax.axis_size("parts")
    share, width, tiles = depth // parts, ff // rows, wide // LANES
    features = rows * depth
    sources = by_step(rows)
    order = by_distance(rows) + [0]

    def body(*refs):
        token_refs, (gate_ref, up_ref), refs = refs[:rows], refs[rows:rows + 2], refs[rows + 2:]
        held_refs = refs[:len(held)]
        outs = refs[len(held) + len(after):][:rows]
        stack, block, sems, block_sems = refs[-4:]
        z, y = lax.axis_index("row"), lax.axis_index("parts")

        def fetched(step, slot=0):
            return pltpu.make_async_copy(token_refs[slot], block.at[step % 2], block_sems.at[step % 2])

        def fetch(step):
            for here in range(rows):
                slot = sources[here].index((here + order[step]) % rows)
                pl.when(z == here)(lambda slot=slot: fetched(step, slot).start())

        copies = []
        for ref, (shift, turn, begin, _) in zip(held_refs, held):
            came = lax.rem(z + rows - shift, rows)
            half = lax.rem(y + turn, parts)
            start = pl.multiple_of(came * depth + half * share, share)
            copies.append(pltpu.make_async_copy(
                ref.at[:, pl.ds(2 * (low - begin), 2 * wide)], stack.at[pl.ds(start, share), :], sems.at[len(copies)]
            ))
        own = pl.multiple_of(z * depth, depth)
        for j in range(tiles):
            start = pl.multiple_of(z * width + low + j * LANES, LANES)
            for g, weight in enumerate((gate_ref, up_ref)):
                copies.append(pltpu.make_async_copy(
                    weight.at[:, pl.ds(start, LANES)],
                    stack.at[pl.ds(own, depth), pl.ds((2 * j + g) * LANES, LANES)],
                    sems.at[len(copies)],
                ))
        fetch(0)
        run_all(copies)
        for step, shift in enumerate(order):
            fetched(step).wait()
            if step + 1 < rows:
                fetch(step + 1)

            def tile(j, carry, step=step, shift=shift):
                both = jnp.dot(
                    block[step % 2],
                    stack[:, pl.ds(pl.multiple_of(j * 2 * LANES, 2 * LANES), 2 * LANES)],
                    preferred_element_type=jnp.float32,
                )
                gate, up = both[:, :LANES], both[:, LANES:]
                outs[shift][:, pl.ds(pl.multiple_of(j * LANES, LANES), LANES)] = (
                    jax.nn.silu(gate) * up
                ).astype(jnp.bfloat16)
                return carry

            lax.fori_loop(0, tiles, tile, 0)

    moved = 2 * (rows * mine * features + features * 2 * wide + rows * mine * wide)
    return pl.pallas_call(
        body,
        out_shape=[jax.ShapeDtypeStruct((mine, wide), jnp.bfloat16)] * rows,
        in_specs=[ANY] * (rows + 2 + len(held) + len(after)),
        out_specs=[pl.BlockSpec(memory_space=pltpu.VMEM)] * rows,
        scratch_shapes=[
            pltpu.VMEM((features, 2 * wide), gate_weight.dtype),
            pltpu.VMEM((2, mine, features), tokens[0].dtype),
            pltpu.SemaphoreType.DMA((len(held) + 2 * tiles,)),
            pltpu.SemaphoreType.DMA((2,)),
        ],
        compiler_params=pltpu.CompilerParams(vmem_limit_bytes=GRANT),
        cost_estimate=pl.CostEstimate(
            flops=4 * rows * mine * features * wide, bytes_accessed=moved, transcendentals=rows * mine * wide
        ),
        name="product",
    )(*tokens, gate_weight, up_weight, *[value for *_, value in held], *after)


def by_step(rows):
    sources = []
    for z in range(rows):
        above = [z + step for step in range(1, rows - z)]
        below = [z - step for step in range(1, z + 1)]
        sources.append([z] + (above + below if 2 * z < rows else below + above))
    return sources


def pick(choices, after):
    rows, like = lax.axis_size("row"), choices[0][1]

    def body(*refs):
        out, sem = refs[-2:]
        z = lax.axis_index("row")
        copies = [pltpu.make_async_copy(ref, out, sem) for ref, _ in zip(refs, choices)]
        for copy, (places, _) in zip(copies, choices):
            for place in places:
                pl.when(z == place)(copy.start)
        copies[0].wait()

    return pl.pallas_call(
        body,
        out_shape=jax.ShapeDtypeStruct(like.shape, like.dtype),
        in_specs=[ANY] * (len(choices) + len(after)),
        out_specs=pl.BlockSpec(memory_space=pltpu.VMEM),
        scratch_shapes=[pltpu.SemaphoreType.DMA],
        compiler_params=pltpu.CompilerParams(vmem_limit_bytes=GRANT),
        cost_estimate=pl.CostEstimate(flops=0, bytes_accessed=4 * like.size, transcendentals=0),
        name="pick",
    )(*[value for _, value in choices], *after)


def place(blocks, mine, ff, onto=None):
    rows = lax.axis_size("row")
    width = ff // rows
    known = [] if onto is None else [onto]

    def body(*refs):
        refs, out, slots, sems = refs[len(known):], refs[len(known) + len(blocks)], refs[-2 - len(blocks):-2], refs[-2:]
        z = lax.axis_index("row")
        loads, stores = [], []
        for n, (ref, slot, (shift, low, value)) in enumerate(zip(refs, slots, blocks)):
            came = lax.rem(z + rows - shift, rows)
            start = pl.multiple_of(came * width + low, LANES)
            loads.append(pltpu.make_async_copy(ref, slot, sems[0].at[n]))
            stores.append(pltpu.make_async_copy(slot, out.at[:, pl.ds(start, value.shape[1])], sems[1].at[n]))
        for load in loads:
            load.start()
        for load, store in zip(loads, stores):
            load.wait()
            store.start()
        for store in stores:
            store.wait()

    values = [value for _, _, value in blocks]
    return pl.pallas_call(
        body,
        out_shape=jax.ShapeDtypeStruct((mine, ff), jnp.bfloat16),
        in_specs=[ANY] * (len(known) + len(blocks)),
        out_specs=ANY,
        scratch_shapes=[pltpu.VMEM(value.shape, value.dtype) for value in values]
        + [pltpu.SemaphoreType.DMA((len(blocks),))] * 2,
        input_output_aliases={0: 0} if known else {},
        compiler_params=pltpu.CompilerParams(vmem_limit_bytes=GRANT),
        cost_estimate=pl.CostEstimate(
            flops=0, bytes_accessed=4 * sum(value.size for value in values), transcendentals=0
        ),
        name="place",
    )(*known, *values)


def in_tiles(tokens, gate_weight, up_weight):
    rows, parts = lax.axis_size("row"), lax.axis_size("parts")
    mine, ff = tokens.shape[0], gate_weight.shape[1]
    width = ff // rows
    units = width // LANES

    edges = [0]
    for piece in range(len(PIECES)):
        edge = units * sum(PIECES[:piece + 1]) // sum(PIECES) * LANES
        if edge > edges[-1]:
            edges.append(edge)
    spans = list(zip(edges[:-1], edges[1:]))

    def tokens_of(before_last_gather):
        lower, upper = [tokens], [tokens]
        for step in range(1, rows):
            if step > 1:
                before = arrived[step - 2:step - 1] + sent[step - 1:step] + swapped[:step - 2][-1:]
                lower[-1], upper[-1] = hold(lower[-1], before), hold(upper[-1], before)
            lower.append(lax.ppermute(lower[-1], "row", [(i, i + 1) for i in range(step - 1, rows - 1)]))
            upper.append(lax.ppermute(upper[-1], "row", [(i, i - 1) for i in range(1, rows - step + 1)]))
        for slot in range(rows):
            chosen = {}
            for here, sources in enumerate(by_step(rows)):
                chosen.setdefault(sources[slot] - here, []).append(here)
            choices = [
                (places, upper[offset] if offset > 0 else lower[-offset]) for offset, places in chosen.items()
            ]
            value = pick(choices, before_last_gather if slot == rows - 1 else []) if slot else tokens
            whole.append(lax.all_gather(value, "col", axis=1, tiled=True))

    def weights(shift, low, high, users):
        after = sent[-1:]
        sent.append(pack(gate_weight, up_weight, shift, low, high - low, after))
        arrived.append(lax.ppermute(sent[-1], "row", around(rows, shift)))
        came = hold(arrived[-1], done) if done else arrived[-1]
        for turn in range(parts):
            if turn:
                swapped.append(lax.ppermute(came, "parts", around(parts, -turn)))
            for n in users:
                held[n].append((shift, turn, low, swapped[-1] if turn else came))

    def hidden_of(n, after):
        low, high = spans[n]
        outs = product(whole, gate_weight, up_weight, held[n], low, high - low, mine, after)
        back = [lax.ppermute(outs[shift], "row", around(rows, shift)) for shift in range(1, rows)]
        blocks.extend((shift, low, value) for shift, value in enumerate([outs[0]] + back))
        done.append(outs[0])
        returned.append(back)

    last = len(spans) - 1
    far, *near = by_distance(rows)
    plan = [(far, low, high, [n]) for n, (low, high) in enumerate(spans)]
    plan += [(shift, low, high, [n]) for n, (low, high) in enumerate(spans) for shift in near]
    sent, arrived, swapped, done, returned, blocks = [], [], [], [], [], []
    held = [[] for _ in spans]
    whole = []
    for step in plan:
        if last and len(sent) == max(len(plan) - 2, 3):
            hidden_of(0, [])
        weights(*step)
        if len(sent) == min(rows + 2, max(len(plan) - 2, 3)):
            tokens_of(arrived[rows - 2:rows - 1] + sent[rows - 1:] + swapped[:rows - 2][-1:])
    for n in range(min(last, 1), last + 1):
        hidden_of(n, done[-1:] + (returned[n - 2] if n > 1 else []))
    early = len(blocks) - rows if last else len(blocks)
    out = place(blocks[:early], mine, ff)
    return place(blocks[early:], mine, ff, out) if last else out


def at_once(tokens, gate_weight, up_weight):
    rows, parts = lax.axis_size("row"), lax.axis_size("parts")
    y = lax.axis_index("parts")
    mine, ff = tokens.shape[0], gate_weight.shape[1]
    depth = gate_weight.shape[0]
    share, width = depth // parts, ff // rows

    whole = lax.all_gather(lax.all_gather(tokens, "row", axis=0, tiled=True), "col", axis=1, tiled=True)
    everyone = whole.shape[0]
    by_share = whole.reshape(everyone, rows, parts, share)
    sent = jnp.stack([
        lax.dynamic_slice(w, (y * share, 0), (share, ff)).reshape(share, rows, width).transpose(1, 0, 2)
        for w in (gate_weight, up_weight)
    ])
    held = lax.all_to_all(sent, "row", 1, 1, tiled=True)
    gate = up = 0.0
    for turn in range(parts):
        features = lax.dynamic_index_in_dim(by_share, (y + turn) % parts, 2, keepdims=False)
        features = features.reshape(everyone, rows * share)
        block = lax.ppermute(held, "parts", around(parts, -turn)) if turn else held
        block = block.reshape(2, rows * share, width)
        gate += jnp.dot(features, block[0], preferred_element_type=jnp.float32)
        up += jnp.dot(features, block[1], preferred_element_type=jnp.float32)
    done = (jax.nn.silu(gate) * up).astype(jnp.bfloat16)
    back = lax.all_to_all(done.reshape(rows, mine, width), "row", 0, 0, tiled=True)
    return back.transpose(1, 0, 2).reshape(mine, ff)


def on_device(tokens, gate_weight, up_weight):
    rows, parts = lax.axis_size("row"), lax.axis_size("parts")
    aligned = (
        gate_weight.shape[1] % (rows * LANES) == 0
        and gate_weight.shape[0] % (parts * 16) == 0
        and tokens.shape[0] % 16 == 0
    )
    return (in_tiles if aligned else at_once)(tokens, gate_weight, up_weight)


def solution(mesh):
    placed = (P(("parts", "row"), "col"), P("row", "col"), P("row", "col"))
    return jax.shard_map(
        on_device, mesh=mesh, in_specs=placed, out_specs=P(("parts", "row"), "col"), check_vma=False
    )
```

```python
import jax
import jax.numpy as jnp
from jax import lax
from jax.experimental import pallas as pl
from jax.experimental.pallas import tpu as pltpu
from jax.sharding import PartitionSpec as P

PIECES = (3, 2, 2)
GRANT = 60 * 2**20
LANES = 128
ANY = pl.BlockSpec(memory_space=pl.ANY)


def around(size, shift):
    return [(i, (i + shift) % size) for i in range(size)]


def by_distance(size):
    return sorted(range(1, size), key=lambda shift: -min(shift, size - shift))


def run_all(copies):
    for copy in copies:
        copy.start()
    for copy in copies:
        copy.wait()


def pack(gate_weight, up_weight, shift, low, wide, after):
    depth, ff = gate_weight.shape
    rows, parts = lax.axis_size("row"), lax.axis_size("parts")
    share, width, tiles = depth // parts, ff // rows, wide // LANES

    def body(*refs):
        weights, sent, sems = refs[:2], refs[-2], refs[-1]
        to = lax.rem(lax.axis_index("row") + shift, rows)
        first = pl.multiple_of(lax.axis_index("parts") * share, share)
        copies = []
        for j in range(tiles):
            start = pl.multiple_of(to * width + low + j * LANES, LANES)
            for g, weight in enumerate(weights):
                copies.append(pltpu.make_async_copy(
                    weight.at[pl.ds(first, share), pl.ds(start, LANES)],
                    sent.at[:, pl.ds((2 * j + g) * LANES, LANES)],
                    sems.at[2 * j + g],
                ))
        run_all(copies)

    size = share * 2 * wide * 2
    return pl.pallas_call(
        body,
        out_shape=jax.ShapeDtypeStruct((share, 2 * wide), gate_weight.dtype),
        in_specs=[ANY] * (2 + len(after)),
        out_specs=pl.BlockSpec(memory_space=pltpu.VMEM),
        scratch_shapes=[pltpu.SemaphoreType.DMA((2 * tiles,))],
        compiler_params=pltpu.CompilerParams(vmem_limit_bytes=GRANT),
        cost_estimate=pl.CostEstimate(flops=0, bytes_accessed=2 * size, transcendentals=0),
        name="pack",
    )(gate_weight, up_weight, *after)


def hold(value, after):
    def body(*refs):
        pass

    return pl.pallas_call(
        body,
        out_shape=jax.ShapeDtypeStruct(value.shape, value.dtype),
        in_specs=[ANY] * (1 + len(after)),
        out_specs=ANY,
        input_output_aliases={0: 0},
        name="hold",
    )(value, *after)


def product(tokens, gate_weight, up_weight, held, low, wide, mine, after):
    depth, ff = gate_weight.shape
    rows, parts = lax.axis_size("row"), lax.axis_size("parts")
    share, width, tiles = depth // parts, ff // rows, wide // LANES
    features = rows * depth
    order = by_distance(rows) + [0]

    def body(tokens_ref, gate_ref, up_ref, *refs):
        held_refs = refs[:len(held)]
        outs = refs[len(held) + len(after):][:rows]
        stack, block, sems, block_sems = refs[-4:]
        z, y = lax.axis_index("row"), lax.axis_index("parts")

        def fetch(step):
            to = lax.rem(z + order[step], rows)
            return pltpu.make_async_copy(
                tokens_ref.at[pl.ds(pl.multiple_of(to * mine, mine), mine), :],
                block.at[step % 2],
                block_sems.at[step % 2],
            )

        copies = []
        for ref, (shift, turn, begin, _) in zip(held_refs, held):
            came = lax.rem(z + rows - shift, rows)
            half = lax.rem(y + turn, parts)
            start = pl.multiple_of(came * depth + half * share, share)
            copies.append(pltpu.make_async_copy(
                ref.at[:, pl.ds(2 * (low - begin), 2 * wide)], stack.at[pl.ds(start, share), :], sems.at[len(copies)]
            ))
        own = pl.multiple_of(z * depth, depth)
        for j in range(tiles):
            start = pl.multiple_of(z * width + low + j * LANES, LANES)
            for g, weight in enumerate((gate_ref, up_ref)):
                copies.append(pltpu.make_async_copy(
                    weight.at[:, pl.ds(start, LANES)],
                    stack.at[pl.ds(own, depth), pl.ds((2 * j + g) * LANES, LANES)],
                    sems.at[len(copies)],
                ))
        fetch(0).start()
        run_all(copies)
        for step, shift in enumerate(order):
            fetch(step).wait()
            if step + 1 < rows:
                fetch(step + 1).start()

            def tile(j, carry, step=step, shift=shift):
                both = jnp.dot(
                    block[step % 2],
                    stack[:, pl.ds(pl.multiple_of(j * 2 * LANES, 2 * LANES), 2 * LANES)],
                    preferred_element_type=jnp.float32,
                )
                gate, up = both[:, :LANES], both[:, LANES:]
                outs[shift][:, pl.ds(pl.multiple_of(j * LANES, LANES), LANES)] = (
                    jax.nn.silu(gate) * up
                ).astype(jnp.bfloat16)
                return carry

            lax.fori_loop(0, tiles, tile, 0)

    moved = 2 * (rows * mine * features + features * 2 * wide + rows * mine * wide)
    return pl.pallas_call(
        body,
        out_shape=[jax.ShapeDtypeStruct((mine, wide), jnp.bfloat16)] * rows,
        in_specs=[ANY] * (3 + len(held) + len(after)),
        out_specs=[pl.BlockSpec(memory_space=pltpu.VMEM)] * rows,
        scratch_shapes=[
            pltpu.VMEM((features, 2 * wide), gate_weight.dtype),
            pltpu.VMEM((2, mine, features), tokens.dtype),
            pltpu.SemaphoreType.DMA((len(held) + 2 * tiles,)),
            pltpu.SemaphoreType.DMA((2,)),
        ],
        compiler_params=pltpu.CompilerParams(vmem_limit_bytes=GRANT),
        cost_estimate=pl.CostEstimate(
            flops=4 * rows * mine * features * wide, bytes_accessed=moved, transcendentals=rows * mine * wide
        ),
        name="product",
    )(tokens, gate_weight, up_weight, *[value for *_, value in held], *after)


def place(blocks, mine, ff, onto=None):
    rows = lax.axis_size("row")
    width = ff // rows
    known = [] if onto is None else [onto]

    def body(*refs):
        refs, out, slots, sems = refs[len(known):], refs[len(known) + len(blocks)], refs[-2 - len(blocks):-2], refs[-2:]
        z = lax.axis_index("row")
        loads, stores = [], []
        for n, (ref, slot, (shift, low, value)) in enumerate(zip(refs, slots, blocks)):
            came = lax.rem(z + rows - shift, rows)
            start = pl.multiple_of(came * width + low, LANES)
            loads.append(pltpu.make_async_copy(ref, slot, sems[0].at[n]))
            stores.append(pltpu.make_async_copy(slot, out.at[:, pl.ds(start, value.shape[1])], sems[1].at[n]))
        for load in loads:
            load.start()
        for load, store in zip(loads, stores):
            load.wait()
            store.start()
        for store in stores:
            store.wait()

    values = [value for _, _, value in blocks]
    return pl.pallas_call(
        body,
        out_shape=jax.ShapeDtypeStruct((mine, ff), jnp.bfloat16),
        in_specs=[ANY] * (len(known) + len(blocks)),
        out_specs=ANY,
        scratch_shapes=[pltpu.VMEM(value.shape, value.dtype) for value in values]
        + [pltpu.SemaphoreType.DMA((len(blocks),))] * 2,
        input_output_aliases={0: 0} if known else {},
        compiler_params=pltpu.CompilerParams(vmem_limit_bytes=GRANT),
        cost_estimate=pl.CostEstimate(
            flops=0, bytes_accessed=4 * sum(value.size for value in values), transcendentals=0
        ),
        name="place",
    )(*known, *values)


def in_tiles(tokens, gate_weight, up_weight):
    rows, parts = lax.axis_size("row"), lax.axis_size("parts")
    mine, ff = tokens.shape[0], gate_weight.shape[1]
    width = ff // rows
    units = width // LANES

    block_rows = lax.all_gather(tokens, "row", axis=0, tiled=True)

    edges = [0]
    for piece in range(len(PIECES)):
        edge = units * sum(PIECES[:piece + 1]) // sum(PIECES) * LANES
        if edge > edges[-1]:
            edges.append(edge)
    spans = list(zip(edges[:-1], edges[1:]))

    def weights(shift, low, high, users):
        after = sent[-1:] + arrived[:len(sent) - 2][-1:] * (len(sent) > 2) + swapped[:len(sent) - 3][-1:] * (len(sent) > 3)
        sent.append(pack(gate_weight, up_weight, shift, low, high - low, after))
        arrived.append(lax.ppermute(sent[-1], "row", around(rows, shift)))
        came = hold(arrived[-1], done) if done else arrived[-1]
        for turn in range(parts):
            if turn:
                swapped.append(lax.ppermute(came, "parts", around(parts, -turn)))
            for n in users:
                held[n].append((shift, turn, low, swapped[-1] if turn else came))

    def hidden_of(n, after):
        low, high = spans[n]
        outs = product(whole, gate_weight, up_weight, held[n], low, high - low, mine, after)
        back = [lax.ppermute(outs[shift], "row", around(rows, shift)) for shift in range(1, rows)]
        blocks.extend((shift, low, value) for shift, value in enumerate([outs[0]] + back))
        done.append(outs[0])
        returned.append(back)

    last = len(spans) - 1
    far, *near = by_distance(rows)
    plan = [(far, 0, spans[max(last - 1, 0)][1], range(max(last, 1)))]
    for n, (low, high) in enumerate(spans):
        plan += [(shift, low, high, [n]) for shift in near]
        if n == 0 < last:
            plan.append((far, *spans[last], [last]))
    sent, arrived, swapped, done, returned, blocks = [], [], [], [], [], []
    held = [[] for _ in spans]
    for step in plan:
        if last and len(sent) == max(len(plan) - 3, 3):
            hidden_of(0, [])
        weights(*step)
        if len(sent) == min(3, len(plan)):
            whole = lax.all_gather(hold(block_rows, arrived[:1] + sent[1:3]), "col", axis=1, tiled=True)
    for n in range(min(last, 1), last + 1):
        hidden_of(n, done[-1:] + (returned[n - 2] if n > 1 else []))
    early = len(blocks) - rows if last else len(blocks)
    out = place(blocks[:early], mine, ff)
    return place(blocks[early:], mine, ff, out) if last else out


def at_once(tokens, gate_weight, up_weight):
    rows, parts = lax.axis_size("row"), lax.axis_size("parts")
    y = lax.axis_index("parts")
    mine, ff = tokens.shape[0], gate_weight.shape[1]
    depth = gate_weight.shape[0]
    share, width = depth // parts, ff // rows

    whole = lax.all_gather(lax.all_gather(tokens, "row", axis=0, tiled=True), "col", axis=1, tiled=True)
    everyone = whole.shape[0]
    by_share = whole.reshape(everyone, rows, parts, share)
    sent = jnp.stack([
        lax.dynamic_slice(w, (y * share, 0), (share, ff)).reshape(share, rows, width).transpose(1, 0, 2)
        for w in (gate_weight, up_weight)
    ])
    held = lax.all_to_all(sent, "row", 1, 1, tiled=True)
    gate = up = 0.0
    for turn in range(parts):
        features = lax.dynamic_index_in_dim(by_share, (y + turn) % parts, 2, keepdims=False)
        features = features.reshape(everyone, rows * share)
        block = lax.ppermute(held, "parts", around(parts, -turn)) if turn else held
        block = block.reshape(2, rows * share, width)
        gate += jnp.dot(features, block[0], preferred_element_type=jnp.float32)
        up += jnp.dot(features, block[1], preferred_element_type=jnp.float32)
    done = (jax.nn.silu(gate) * up).astype(jnp.bfloat16)
    back = lax.all_to_all(done.reshape(rows, mine, width), "row", 0, 0, tiled=True)
    return back.transpose(1, 0, 2).reshape(mine, ff)


def on_device(tokens, gate_weight, up_weight):
    rows, parts = lax.axis_size("row"), lax.axis_size("parts")
    aligned = (
        gate_weight.shape[1] % (rows * LANES) == 0
        and gate_weight.shape[0] % (parts * 16) == 0
        and tokens.shape[0] % 16 == 0
    )
    return (in_tiles if aligned else at_once)(tokens, gate_weight, up_weight)


def solution(mesh):
    placed = (P(("parts", "row"), "col"), P("row", "col"), P("row", "col"))
    return jax.shard_map(
        on_device, mesh=mesh, in_specs=placed, out_specs=P(("parts", "row"), "col"), check_vma=False
    )
```

```python
import jax
import jax.numpy as jnp
from jax import lax
from jax.experimental import pallas as pl
from jax.experimental.pallas import tpu as pltpu
from jax.sharding import PartitionSpec as P

PIECES = (3, 2, 2)
GRANT = 60 * 2**20
LANES = 128
ANY = pl.BlockSpec(memory_space=pl.ANY)


def around(size, shift):
    return [(i, (i + shift) % size) for i in range(size)]


def by_distance(size):
    return sorted(range(1, size), key=lambda shift: -min(shift, size - shift))


def run_all(copies):
    for copy in copies:
        copy.start()
    for copy in copies:
        copy.wait()


def pack(gate_weight, up_weight, shift, low, wide, after):
    depth, ff = gate_weight.shape
    rows, parts = lax.axis_size("row"), lax.axis_size("parts")
    share, width, tiles = depth // parts, ff // rows, wide // LANES

    def body(*refs):
        weights, sent, sems = refs[:2], refs[-2], refs[-1]
        to = lax.rem(lax.axis_index("row") + shift, rows)
        first = pl.multiple_of(lax.axis_index("parts") * share, share)
        copies = []
        for j in range(tiles):
            start = pl.multiple_of(to * width + low + j * LANES, LANES)
            for g, weight in enumerate(weights):
                copies.append(pltpu.make_async_copy(
                    weight.at[pl.ds(first, share), pl.ds(start, LANES)],
                    sent.at[:, pl.ds((2 * j + g) * LANES, LANES)],
                    sems.at[2 * j + g],
                ))
        run_all(copies)

    size = share * 2 * wide * 2
    return pl.pallas_call(
        body,
        out_shape=jax.ShapeDtypeStruct((share, 2 * wide), gate_weight.dtype),
        in_specs=[ANY] * (2 + len(after)),
        out_specs=pl.BlockSpec(memory_space=pltpu.VMEM),
        scratch_shapes=[pltpu.SemaphoreType.DMA((2 * tiles,))],
        compiler_params=pltpu.CompilerParams(vmem_limit_bytes=GRANT),
        cost_estimate=pl.CostEstimate(flops=0, bytes_accessed=2 * size, transcendentals=0),
        name="pack",
    )(gate_weight, up_weight, *after)


def hold(value, after):
    def body(*refs):
        pass

    return pl.pallas_call(
        body,
        out_shape=jax.ShapeDtypeStruct(value.shape, value.dtype),
        in_specs=[ANY] * (1 + len(after)),
        out_specs=ANY,
        input_output_aliases={0: 0},
        name="hold",
    )(value, *after)


def product(tokens, gate_weight, up_weight, held, low, wide, mine, after):
    depth, ff = gate_weight.shape
    rows, parts = lax.axis_size("row"), lax.axis_size("parts")
    share, width, tiles = depth // parts, ff // rows, wide // LANES
    features = rows * depth
    order = by_distance(rows) + [0]

    def body(tokens_ref, gate_ref, up_ref, *refs):
        held_refs = refs[:len(held)]
        outs = refs[len(held) + len(after):][:rows]
        stack, block, sems, block_sems = refs[-4:]
        z, y = lax.axis_index("row"), lax.axis_index("parts")

        def fetch(step):
            to = lax.rem(z + order[step], rows)
            return pltpu.make_async_copy(
                tokens_ref.at[pl.ds(pl.multiple_of(to * mine, mine), mine), :],
                block.at[step % 2],
                block_sems.at[step % 2],
            )

        copies = []
        for ref, (shift, turn, begin, _) in zip(held_refs, held):
            came = lax.rem(z + rows - shift, rows)
            half = lax.rem(y + turn, parts)
            start = pl.multiple_of(came * depth + half * share, share)
            copies.append(pltpu.make_async_copy(
                ref.at[:, pl.ds(2 * (low - begin), 2 * wide)], stack.at[pl.ds(start, share), :], sems.at[len(copies)]
            ))
        own = pl.multiple_of(z * depth, depth)
        for j in range(tiles):
            start = pl.multiple_of(z * width + low + j * LANES, LANES)
            for g, weight in enumerate((gate_ref, up_ref)):
                copies.append(pltpu.make_async_copy(
                    weight.at[:, pl.ds(start, LANES)],
                    stack.at[pl.ds(own, depth), pl.ds((2 * j + g) * LANES, LANES)],
                    sems.at[len(copies)],
                ))
        fetch(0).start()
        run_all(copies)
        for step, shift in enumerate(order):
            fetch(step).wait()
            if step + 1 < rows:
                fetch(step + 1).start()

            def tile(j, carry, step=step, shift=shift):
                both = jnp.dot(
                    block[step % 2],
                    stack[:, pl.ds(pl.multiple_of(j * 2 * LANES, 2 * LANES), 2 * LANES)],
                    preferred_element_type=jnp.float32,
                )
                gate, up = both[:, :LANES], both[:, LANES:]
                outs[shift][:, pl.ds(pl.multiple_of(j * LANES, LANES), LANES)] = (
                    jax.nn.silu(gate) * up
                ).astype(jnp.bfloat16)
                return carry

            lax.fori_loop(0, tiles, tile, 0)

    moved = 2 * (rows * mine * features + features * 2 * wide + rows * mine * wide)
    return pl.pallas_call(
        body,
        out_shape=[jax.ShapeDtypeStruct((mine, wide), jnp.bfloat16)] * rows,
        in_specs=[ANY] * (3 + len(held) + len(after)),
        out_specs=[pl.BlockSpec(memory_space=pltpu.VMEM)] * rows,
        scratch_shapes=[
            pltpu.VMEM((features, 2 * wide), gate_weight.dtype),
            pltpu.VMEM((2, mine, features), tokens.dtype),
            pltpu.SemaphoreType.DMA((len(held) + 2 * tiles,)),
            pltpu.SemaphoreType.DMA((2,)),
        ],
        compiler_params=pltpu.CompilerParams(vmem_limit_bytes=GRANT),
        cost_estimate=pl.CostEstimate(
            flops=4 * rows * mine * features * wide, bytes_accessed=moved, transcendentals=rows * mine * wide
        ),
        name="product",
    )(tokens, gate_weight, up_weight, *[value for *_, value in held], *after)


def place(blocks, mine, ff, onto=None):
    rows = lax.axis_size("row")
    width = ff // rows
    known = [] if onto is None else [onto]

    def body(*refs):
        refs, out, slots, sems = refs[len(known):], refs[len(known) + len(blocks)], refs[-2 - len(blocks):-2], refs[-2:]
        z = lax.axis_index("row")
        loads, stores = [], []
        for n, (ref, slot, (shift, low, value)) in enumerate(zip(refs, slots, blocks)):
            came = lax.rem(z + rows - shift, rows)
            start = pl.multiple_of(came * width + low, LANES)
            loads.append(pltpu.make_async_copy(ref, slot, sems[0].at[n]))
            stores.append(pltpu.make_async_copy(slot, out.at[:, pl.ds(start, value.shape[1])], sems[1].at[n]))
        for load in loads:
            load.start()
        for load, store in zip(loads, stores):
            load.wait()
            store.start()
        for store in stores:
            store.wait()

    values = [value for _, _, value in blocks]
    return pl.pallas_call(
        body,
        out_shape=jax.ShapeDtypeStruct((mine, ff), jnp.bfloat16),
        in_specs=[ANY] * (len(known) + len(blocks)),
        out_specs=ANY,
        scratch_shapes=[pltpu.VMEM(value.shape, value.dtype) for value in values]
        + [pltpu.SemaphoreType.DMA((len(blocks),))] * 2,
        input_output_aliases={0: 0} if known else {},
        compiler_params=pltpu.CompilerParams(vmem_limit_bytes=GRANT),
        cost_estimate=pl.CostEstimate(
            flops=0, bytes_accessed=4 * sum(value.size for value in values), transcendentals=0
        ),
        name="place",
    )(*known, *values)


def in_tiles(tokens, gate_weight, up_weight):
    rows, parts = lax.axis_size("row"), lax.axis_size("parts")
    mine, ff = tokens.shape[0], gate_weight.shape[1]
    width = ff // rows
    units = width // LANES

    block_rows = lax.all_gather(tokens, "row", axis=0, tiled=True)

    edges = [0]
    for piece in range(len(PIECES)):
        edge = units * sum(PIECES[:piece + 1]) // sum(PIECES) * LANES
        if edge > edges[-1]:
            edges.append(edge)
    spans = list(zip(edges[:-1], edges[1:]))

    def weights(shift, low, high, users):
        after = sent[-1:] + arrived[:len(sent) - 2][-1:] * (len(sent) > 2) + swapped[:len(sent) - 3][-1:] * (len(sent) > 3)
        sent.append(pack(gate_weight, up_weight, shift, low, high - low, after))
        arrived.append(lax.ppermute(sent[-1], "row", around(rows, shift)))
        came = hold(arrived[-1], done) if done else arrived[-1]
        for turn in range(parts):
            if turn:
                swapped.append(lax.ppermute(came, "parts", around(parts, -turn)))
            for n in users:
                held[n].append((shift, turn, low, swapped[-1] if turn else came))

    def hidden_of(n, after):
        low, high = spans[n]
        outs = product(whole, gate_weight, up_weight, held[n], low, high - low, mine, after)
        back = [lax.ppermute(outs[shift], "row", around(rows, shift)) for shift in range(1, rows)]
        blocks.extend((shift, low, value) for shift, value in enumerate([outs[0]] + back))
        done.append(outs[0])
        returned.append(back)

    last = len(spans) - 1
    far, *near = by_distance(rows)
    plan = [(far, 0, spans[max(last - 1, 0)][1], range(max(last, 1)))]
    for n, (low, high) in enumerate(spans):
        plan += [(shift, low, high, [n]) for shift in near]
        if n == 0 < last:
            plan.append((far, *spans[last], [last]))
    sent, arrived, swapped, done, returned, blocks = [], [], [], [], [], []
    held = [[] for _ in spans]
    for step in plan:
        if last and len(sent) == max(len(plan) - 3, 3):
            hidden_of(0, [])
        weights(*step)
        if len(sent) == min(3, len(plan)):
            whole = lax.all_gather(hold(block_rows, arrived[:1] + sent[1:3]), "col", axis=1, tiled=True)
    for n in range(min(last, 1), last + 1):
        hidden_of(n, done[-1:] + (returned[n - 2][:1] if n > 1 else []))
    early = len(blocks) - rows if last else len(blocks)
    out = place(blocks[:early], mine, ff)
    return place(blocks[early:], mine, ff, out) if last else out


def at_once(tokens, gate_weight, up_weight):
    rows, parts = lax.axis_size("row"), lax.axis_size("parts")
    y = lax.axis_index("parts")
    mine, ff = tokens.shape[0], gate_weight.shape[1]
    depth = gate_weight.shape[0]
    share, width = depth // parts, ff // rows

    whole = lax.all_gather(lax.all_gather(tokens, "row", axis=0, tiled=True), "col", axis=1, tiled=True)
    everyone = whole.shape[0]
    by_share = whole.reshape(everyone, rows, parts, share)
    sent = jnp.stack([
        lax.dynamic_slice(w, (y * share, 0), (share, ff)).reshape(share, rows, width).transpose(1, 0, 2)
        for w in (gate_weight, up_weight)
    ])
    held = lax.all_to_all(sent, "row", 1, 1, tiled=True)
    gate = up = 0.0
    for turn in range(parts):
        features = lax.dynamic_index_in_dim(by_share, (y + turn) % parts, 2, keepdims=False)
        features = features.reshape(everyone, rows * share)
        block = lax.ppermute(held, "parts", around(parts, -turn)) if turn else held
        block = block.reshape(2, rows * share, width)
        gate += jnp.dot(features, block[0], preferred_element_type=jnp.float32)
        up += jnp.dot(features, block[1], preferred_element_type=jnp.float32)
    done = (jax.nn.silu(gate) * up).astype(jnp.bfloat16)
    back = lax.all_to_all(done.reshape(rows, mine, width), "row", 0, 0, tiled=True)
    return back.transpose(1, 0, 2).reshape(mine, ff)


def on_device(tokens, gate_weight, up_weight):
    rows, parts = lax.axis_size("row"), lax.axis_size("parts")
    aligned = (
        gate_weight.shape[1] % (rows * LANES) == 0
        and gate_weight.shape[0] % (parts * 16) == 0
        and tokens.shape[0] % 16 == 0
    )
    return (in_tiles if aligned else at_once)(tokens, gate_weight, up_weight)


def solution(mesh):
    placed = (P(("parts", "row"), "col"), P("row", "col"), P("row", "col"))
    return jax.shard_map(
        on_device, mesh=mesh, in_specs=placed, out_specs=P(("parts", "row"), "col"), check_vma=False
    )
```

```python
import jax
import jax.numpy as jnp
from jax import lax
from jax.experimental import pallas as pl
from jax.experimental.pallas import tpu as pltpu
from jax.sharding import PartitionSpec as P

PIECES = (3, 2, 2)
GRANT = 60 * 2**20
LANES = 128
ANY = pl.BlockSpec(memory_space=pl.ANY)


def around(size, shift):
    return [(i, (i + shift) % size) for i in range(size)]


def by_distance(size):
    return sorted(range(1, size), key=lambda shift: -min(shift, size - shift))


def run_all(copies):
    for copy in copies:
        copy.start()
    for copy in copies:
        copy.wait()


def pack(gate_weight, up_weight, shift, low, wide, after):
    depth, ff = gate_weight.shape
    rows, parts = lax.axis_size("row"), lax.axis_size("parts")
    share, width, tiles = depth // parts, ff // rows, wide // LANES

    def body(*refs):
        weights, sent, sems = refs[:2], refs[-2], refs[-1]
        to = lax.rem(lax.axis_index("row") + shift, rows)
        first = pl.multiple_of(lax.axis_index("parts") * share, share)
        copies = []
        for j in range(tiles):
            start = pl.multiple_of(to * width + low + j * LANES, LANES)
            for g, weight in enumerate(weights):
                copies.append(pltpu.make_async_copy(
                    weight.at[pl.ds(first, share), pl.ds(start, LANES)],
                    sent.at[:, pl.ds((2 * j + g) * LANES, LANES)],
                    sems.at[2 * j + g],
                ))
        run_all(copies)

    size = share * 2 * wide * 2
    return pl.pallas_call(
        body,
        out_shape=jax.ShapeDtypeStruct((share, 2 * wide), gate_weight.dtype),
        in_specs=[ANY] * (2 + len(after)),
        out_specs=pl.BlockSpec(memory_space=pltpu.VMEM),
        scratch_shapes=[pltpu.SemaphoreType.DMA((2 * tiles,))],
        compiler_params=pltpu.CompilerParams(vmem_limit_bytes=GRANT),
        cost_estimate=pl.CostEstimate(flops=0, bytes_accessed=2 * size, transcendentals=0),
        name="pack",
    )(gate_weight, up_weight, *after)


def hold(value, after):
    def body(*refs):
        pass

    return pl.pallas_call(
        body,
        out_shape=jax.ShapeDtypeStruct(value.shape, value.dtype),
        in_specs=[ANY] * (1 + len(after)),
        out_specs=ANY,
        input_output_aliases={0: 0},
        name="hold",
    )(value, *after)


def product(tokens, gate_weight, up_weight, held, low, wide, mine, after):
    depth, ff = gate_weight.shape
    rows, parts = lax.axis_size("row"), lax.axis_size("parts")
    share, width, tiles = depth // parts, ff // rows, wide // LANES
    features = rows * depth
    order = by_distance(rows) + [0]
    group = 2 if rows % 2 == 0 else 1

    def body(tokens_ref, gate_ref, up_ref, *refs):
        held_refs = refs[:len(held)]
        outs = refs[len(held) + len(after):][:rows]
        stack, block, sems, block_sems = refs[-4:]
        z, y = lax.axis_index("row"), lax.axis_index("parts")

        fetches = []
        for step, shift in enumerate(order):
            first = pl.multiple_of(lax.rem(z + shift, rows) * mine, mine)
            fetches.append(pltpu.make_async_copy(
                tokens_ref.at[pl.ds(first, mine), :], block.at[pl.ds(step * mine, mine), :], block_sems.at[step]
            ))

        copies = []
        for ref, (shift, turn, begin, _) in zip(held_refs, held):
            came = lax.rem(z + rows - shift, rows)
            half = lax.rem(y + turn, parts)
            start = pl.multiple_of(came * depth + half * share, share)
            copies.append(pltpu.make_async_copy(
                ref.at[:, pl.ds(2 * (low - begin), 2 * wide)], stack.at[pl.ds(start, share), :], sems.at[len(copies)]
            ))
        own = pl.multiple_of(z * depth, depth)
        for j in range(tiles):
            start = pl.multiple_of(z * width + low + j * LANES, LANES)
            for g, weight in enumerate((gate_ref, up_ref)):
                copies.append(pltpu.make_async_copy(
                    weight.at[:, pl.ds(start, LANES)],
                    stack.at[pl.ds(own, depth), pl.ds((2 * j + g) * LANES, LANES)],
                    sems.at[len(copies)],
                ))
        for fetch in fetches[:group]:
            fetch.start()
        for copy in copies + fetches[group:]:
            copy.start()
        for copy in copies:
            copy.wait()
        for first in range(0, rows, group):
            for fetch in fetches[first:first + group]:
                fetch.wait()

            def tile(j, carry, first=first):
                both = jnp.dot(
                    block[first * mine:(first + group) * mine],
                    stack[:, pl.ds(pl.multiple_of(j * 2 * LANES, 2 * LANES), 2 * LANES)],
                    preferred_element_type=jnp.float32,
                )
                gate, up = both[:, :LANES], both[:, LANES:]
                value = (jax.nn.silu(gate) * up).astype(jnp.bfloat16)
                for n in range(group):
                    outs[order[first + n]][:, pl.ds(pl.multiple_of(j * LANES, LANES), LANES)] = (
                        value[n * mine:(n + 1) * mine]
                    )
                return carry

            lax.fori_loop(0, tiles, tile, 0)

    moved = 2 * (rows * mine * features + features * 2 * wide + rows * mine * wide)
    return pl.pallas_call(
        body,
        out_shape=[jax.ShapeDtypeStruct((mine, wide), jnp.bfloat16)] * rows,
        in_specs=[ANY] * (3 + len(held) + len(after)),
        out_specs=[pl.BlockSpec(memory_space=pltpu.VMEM)] * rows,
        scratch_shapes=[
            pltpu.VMEM((features, 2 * wide), gate_weight.dtype),
            pltpu.VMEM((rows * mine, features), tokens.dtype),
            pltpu.SemaphoreType.DMA((len(held) + 2 * tiles,)),
            pltpu.SemaphoreType.DMA((rows,)),
        ],
        compiler_params=pltpu.CompilerParams(vmem_limit_bytes=GRANT),
        cost_estimate=pl.CostEstimate(
            flops=4 * rows * mine * features * wide, bytes_accessed=moved, transcendentals=rows * mine * wide
        ),
        name="product",
    )(tokens, gate_weight, up_weight, *[value for *_, value in held], *after)


def place(blocks, mine, ff, onto=None):
    rows = lax.axis_size("row")
    width = ff // rows
    known = [] if onto is None else [onto]

    def body(*refs):
        refs, out, slots, sems = refs[len(known):], refs[len(known) + len(blocks)], refs[-2 - len(blocks):-2], refs[-2:]
        z = lax.axis_index("row")
        loads, stores = [], []
        for n, (ref, slot, (shift, low, value)) in enumerate(zip(refs, slots, blocks)):
            came = lax.rem(z + rows - shift, rows)
            start = pl.multiple_of(came * width + low, LANES)
            loads.append(pltpu.make_async_copy(ref, slot, sems[0].at[n]))
            stores.append(pltpu.make_async_copy(slot, out.at[:, pl.ds(start, value.shape[1])], sems[1].at[n]))
        for load in loads:
            load.start()
        for load, store in zip(loads, stores):
            load.wait()
            store.start()
        for store in stores:
            store.wait()

    values = [value for _, _, value in blocks]
    return pl.pallas_call(
        body,
        out_shape=jax.ShapeDtypeStruct((mine, ff), jnp.bfloat16),
        in_specs=[ANY] * (len(known) + len(blocks)),
        out_specs=ANY,
        scratch_shapes=[pltpu.VMEM(value.shape, value.dtype) for value in values]
        + [pltpu.SemaphoreType.DMA((len(blocks),))] * 2,
        input_output_aliases={0: 0} if known else {},
        compiler_params=pltpu.CompilerParams(vmem_limit_bytes=GRANT),
        cost_estimate=pl.CostEstimate(
            flops=0, bytes_accessed=4 * sum(value.size for value in values), transcendentals=0
        ),
        name="place",
    )(*known, *values)


def in_tiles(tokens, gate_weight, up_weight):
    rows, parts = lax.axis_size("row"), lax.axis_size("parts")
    mine, ff = tokens.shape[0], gate_weight.shape[1]
    width = ff // rows
    units = width // LANES

    block_rows = lax.all_gather(tokens, "row", axis=0, tiled=True)

    edges = [0]
    for piece in range(len(PIECES)):
        edge = units * sum(PIECES[:piece + 1]) // sum(PIECES) * LANES
        if edge > edges[-1]:
            edges.append(edge)
    spans = list(zip(edges[:-1], edges[1:]))

    def weights(shift, low, high, users):
        after = sent[-1:] + arrived[:len(sent) - 2][-1:] * (len(sent) > 2) + swapped[:len(sent) - 3][-1:] * (len(sent) > 3)
        sent.append(pack(gate_weight, up_weight, shift, low, high - low, after))
        arrived.append(lax.ppermute(sent[-1], "row", around(rows, shift)))
        came = hold(arrived[-1], done) if done else arrived[-1]
        for turn in range(parts):
            if turn:
                swapped.append(lax.ppermute(came, "parts", around(parts, -turn)))
            for n in users:
                held[n].append((shift, turn, low, swapped[-1] if turn else came))

    def hidden_of(n, after):
        low, high = spans[n]
        outs = product(whole, gate_weight, up_weight, held[n], low, high - low, mine, after)
        back = [lax.ppermute(outs[shift], "row", around(rows, shift)) for shift in range(1, rows)]
        blocks.extend((shift, low, value) for shift, value in enumerate([outs[0]] + back))
        done.append(outs[0])
        returned.append(back)

    last = len(spans) - 1
    far, *near = by_distance(rows)
    plan = [(far, 0, spans[max(last - 1, 0)][1], range(max(last, 1)))]
    for n, (low, high) in enumerate(spans):
        plan += [(shift, low, high, [n]) for shift in near]
        if n == 0 < last:
            plan.append((far, *spans[last], [last]))
    sent, arrived, swapped, done, returned, blocks = [], [], [], [], [], []
    held = [[] for _ in spans]
    for step in plan:
        if last and len(sent) == max(len(plan) - 2, 3):
            hidden_of(0, [])
        weights(*step)
        if len(sent) == min(3, len(plan)):
            whole = lax.all_gather(hold(block_rows, arrived[:1] + sent[1:3]), "col", axis=1, tiled=True)
    for n in range(min(last, 1), last + 1):
        hidden_of(n, done[-1:] + (returned[n - 2][:1] if n > 1 else []))
    early = len(blocks) - rows if last else len(blocks)
    out = place(blocks[:early], mine, ff)
    return place(blocks[early:], mine, ff, out) if last else out


def at_once(tokens, gate_weight, up_weight):
    rows, parts = lax.axis_size("row"), lax.axis_size("parts")
    y = lax.axis_index("parts")
    mine, ff = tokens.shape[0], gate_weight.shape[1]
    depth = gate_weight.shape[0]
    share, width = depth // parts, ff // rows

    whole = lax.all_gather(lax.all_gather(tokens, "row", axis=0, tiled=True), "col", axis=1, tiled=True)
    everyone = whole.shape[0]
    by_share = whole.reshape(everyone, rows, parts, share)
    sent = jnp.stack([
        lax.dynamic_slice(w, (y * share, 0), (share, ff)).reshape(share, rows, width).transpose(1, 0, 2)
        for w in (gate_weight, up_weight)
    ])
    held = lax.all_to_all(sent, "row", 1, 1, tiled=True)
    gate = up = 0.0
    for turn in range(parts):
        features = lax.dynamic_index_in_dim(by_share, (y + turn) % parts, 2, keepdims=False)
        features = features.reshape(everyone, rows * share)
        block = lax.ppermute(held, "parts", around(parts, -turn)) if turn else held
        block = block.reshape(2, rows * share, width)
        gate += jnp.dot(features, block[0], preferred_element_type=jnp.float32)
        up += jnp.dot(features, block[1], preferred_element_type=jnp.float32)
    done = (jax.nn.silu(gate) * up).astype(jnp.bfloat16)
    back = lax.all_to_all(done.reshape(rows, mine, width), "row", 0, 0, tiled=True)
    return back.transpose(1, 0, 2).reshape(mine, ff)


def on_device(tokens, gate_weight, up_weight):
    rows, parts = lax.axis_size("row"), lax.axis_size("parts")
    aligned = (
        gate_weight.shape[1] % (rows * LANES) == 0
        and gate_weight.shape[0] % (parts * 16) == 0
        and tokens.shape[0] % 16 == 0
    )
    return (in_tiles if aligned else at_once)(tokens, gate_weight, up_weight)


def solution(mesh):
    placed = (P(("parts", "row"), "col"), P("row", "col"), P("row", "col"))
    return jax.shard_map(
        on_device, mesh=mesh, in_specs=placed, out_specs=P(("parts", "row"), "col"), check_vma=False
    )
```

```python
import jax
import jax.numpy as jnp
from jax import lax
from jax.experimental import pallas as pl
from jax.experimental.pallas import tpu as pltpu
from jax.sharding import PartitionSpec as P

PIECES = (3, 2, 2)
GRANT = 60 * 2**20
LANES = 128
ANY = pl.BlockSpec(memory_space=pl.ANY)


def around(size, shift):
    return [(i, (i + shift) % size) for i in range(size)]


def by_distance(size):
    return sorted(range(1, size), key=lambda shift: -min(shift, size - shift))


def run_all(copies):
    for copy in copies:
        copy.start()
    for copy in copies:
        copy.wait()


def pack(gate_weight, up_weight, shift, low, wide, after):
    depth, ff = gate_weight.shape
    rows, parts = lax.axis_size("row"), lax.axis_size("parts")
    share, width, tiles = depth // parts, ff // rows, wide // LANES

    def body(*refs):
        weights, sent, sems = refs[:2], refs[-2], refs[-1]
        to = lax.rem(lax.axis_index("row") + shift, rows)
        first = pl.multiple_of(lax.axis_index("parts") * share, share)
        copies = []
        for j in range(tiles):
            start = pl.multiple_of(to * width + low + j * LANES, LANES)
            for g, weight in enumerate(weights):
                copies.append(pltpu.make_async_copy(
                    weight.at[pl.ds(first, share), pl.ds(start, LANES)],
                    sent.at[:, pl.ds((2 * j + g) * LANES, LANES)],
                    sems.at[2 * j + g],
                ))
        run_all(copies)

    size = share * 2 * wide * 2
    return pl.pallas_call(
        body,
        out_shape=jax.ShapeDtypeStruct((share, 2 * wide), gate_weight.dtype),
        in_specs=[ANY] * (2 + len(after)),
        out_specs=pl.BlockSpec(memory_space=pltpu.VMEM),
        scratch_shapes=[pltpu.SemaphoreType.DMA((2 * tiles,))],
        compiler_params=pltpu.CompilerParams(vmem_limit_bytes=GRANT),
        cost_estimate=pl.CostEstimate(flops=0, bytes_accessed=2 * size, transcendentals=0),
        name="pack",
    )(gate_weight, up_weight, *after)


def hold(value, after):
    def body(*refs):
        pass

    return pl.pallas_call(
        body,
        out_shape=jax.ShapeDtypeStruct(value.shape, value.dtype),
        in_specs=[ANY] * (1 + len(after)),
        out_specs=ANY,
        input_output_aliases={0: 0},
        name="hold",
    )(value, *after)


def product(tokens, gate_weight, up_weight, held, low, wide, mine, after):
    depth, ff = gate_weight.shape
    rows, parts = lax.axis_size("row"), lax.axis_size("parts")
    share, width, tiles = depth // parts, ff // rows, wide // LANES
    features = rows * depth
    sources = by_step(rows)
    order = by_distance(rows) + [0]

    def body(*refs):
        token_refs, (gate_ref, up_ref), refs = refs[:rows], refs[rows:rows + 2], refs[rows + 2:]
        held_refs = refs[:len(held)]
        outs = refs[len(held) + len(after):][:rows]
        stack, block, sems, block_sems = refs[-4:]
        z, y = lax.axis_index("row"), lax.axis_index("parts")

        def fetched(step, slot=0):
            return pltpu.make_async_copy(token_refs[slot], block.at[step % 2], block_sems.at[step % 2])

        def fetch(step):
            for here in range(rows):
                slot = sources[here].index((here + order[step]) % rows)
                pl.when(z == here)(lambda slot=slot: fetched(step, slot).start())

        copies = []
        for ref, (shift, turn, begin, _) in zip(held_refs, held):
            came = lax.rem(z + rows - shift, rows)
            half = lax.rem(y + turn, parts)
            start = pl.multiple_of(came * depth + half * share, share)
            copies.append(pltpu.make_async_copy(
                ref.at[:, pl.ds(2 * (low - begin), 2 * wide)], stack.at[pl.ds(start, share), :], sems.at[len(copies)]
            ))
        own = pl.multiple_of(z * depth, depth)
        for j in range(tiles):
            start = pl.multiple_of(z * width + low + j * LANES, LANES)
            for g, weight in enumerate((gate_ref, up_ref)):
                copies.append(pltpu.make_async_copy(
                    weight.at[:, pl.ds(start, LANES)],
                    stack.at[pl.ds(own, depth), pl.ds((2 * j + g) * LANES, LANES)],
                    sems.at[len(copies)],
                ))
        fetch(0)
        run_all(copies)
        for step, shift in enumerate(order):
            fetched(step).wait()
            if step + 1 < rows:
                fetch(step + 1)

            def tile(j, carry, step=step, shift=shift):
                both = jnp.dot(
                    block[step % 2],
                    stack[:, pl.ds(pl.multiple_of(j * 2 * LANES, 2 * LANES), 2 * LANES)],
                    preferred_element_type=jnp.float32,
                )
                gate, up = both[:, :LANES], both[:, LANES:]
                outs[shift][:, pl.ds(pl.multiple_of(j * LANES, LANES), LANES)] = (
                    jax.nn.silu(gate) * up
                ).astype(jnp.bfloat16)
                return carry

            lax.fori_loop(0, tiles, tile, 0)

    moved = 2 * (rows * mine * features + features * 2 * wide + rows * mine * wide)
    return pl.pallas_call(
        body,
        out_shape=[jax.ShapeDtypeStruct((mine, wide), jnp.bfloat16)] * rows,
        in_specs=[ANY] * (rows + 2 + len(held) + len(after)),
        out_specs=[pl.BlockSpec(memory_space=pltpu.VMEM)] * rows,
        scratch_shapes=[
            pltpu.VMEM((features, 2 * wide), gate_weight.dtype),
            pltpu.VMEM((2, mine, features), tokens[0].dtype),
            pltpu.SemaphoreType.DMA((len(held) + 2 * tiles,)),
            pltpu.SemaphoreType.DMA((2,)),
        ],
        compiler_params=pltpu.CompilerParams(vmem_limit_bytes=GRANT),
        cost_estimate=pl.CostEstimate(
            flops=4 * rows * mine * features * wide, bytes_accessed=moved, transcendentals=rows * mine * wide
        ),
        name="product",
    )(*tokens, gate_weight, up_weight, *[value for *_, value in held], *after)


def by_step(rows):
    sources = []
    for z in range(rows):
        above = [z + step for step in range(1, rows - z)]
        below = [z - step for step in range(1, z + 1)]
        sources.append([z] + (above + below if 2 * z < rows else below + above))
    return sources


def pick(choices, after):
    rows, like = lax.axis_size("row"), choices[0][1]

    def body(*refs):
        out, sem = refs[-2:]
        z = lax.axis_index("row")
        copies = [pltpu.make_async_copy(ref, out, sem) for ref, _ in zip(refs, choices)]
        for copy, (places, _) in zip(copies, choices):
            for place in places:
                pl.when(z == place)(copy.start)
        copies[0].wait()

    return pl.pallas_call(
        body,
        out_shape=jax.ShapeDtypeStruct(like.shape, like.dtype),
        in_specs=[ANY] * (len(choices) + len(after)),
        out_specs=pl.BlockSpec(memory_space=pltpu.VMEM),
        scratch_shapes=[pltpu.SemaphoreType.DMA],
        compiler_params=pltpu.CompilerParams(vmem_limit_bytes=GRANT),
        cost_estimate=pl.CostEstimate(flops=0, bytes_accessed=4 * like.size, transcendentals=0),
        name="pick",
    )(*[value for _, value in choices], *after)


def place(blocks, mine, ff, onto=None):
    rows = lax.axis_size("row")
    width = ff // rows
    known = [] if onto is None else [onto]

    def body(*refs):
        refs, out, slots, sems = refs[len(known):], refs[len(known) + len(blocks)], refs[-2 - len(blocks):-2], refs[-2:]
        z = lax.axis_index("row")
        loads, stores = [], []
        for n, (ref, slot, (shift, low, value)) in enumerate(zip(refs, slots, blocks)):
            came = lax.rem(z + rows - shift, rows)
            start = pl.multiple_of(came * width + low, LANES)
            loads.append(pltpu.make_async_copy(ref, slot, sems[0].at[n]))
            stores.append(pltpu.make_async_copy(slot, out.at[:, pl.ds(start, value.shape[1])], sems[1].at[n]))
        for load in loads:
            load.start()
        for load, store in zip(loads, stores):
            load.wait()
            store.start()
        for store in stores:
            store.wait()

    values = [value for _, _, value in blocks]
    return pl.pallas_call(
        body,
        out_shape=jax.ShapeDtypeStruct((mine, ff), jnp.bfloat16),
        in_specs=[ANY] * (len(known) + len(blocks)),
        out_specs=ANY,
        scratch_shapes=[pltpu.VMEM(value.shape, value.dtype) for value in values]
        + [pltpu.SemaphoreType.DMA((len(blocks),))] * 2,
        input_output_aliases={0: 0} if known else {},
        compiler_params=pltpu.CompilerParams(vmem_limit_bytes=GRANT),
        cost_estimate=pl.CostEstimate(
            flops=0, bytes_accessed=4 * sum(value.size for value in values), transcendentals=0
        ),
        name="place",
    )(*known, *values)


def in_tiles(tokens, gate_weight, up_weight):
    rows, parts = lax.axis_size("row"), lax.axis_size("parts")
    mine, ff = tokens.shape[0], gate_weight.shape[1]
    width = ff // rows
    units = width // LANES

    edges = [0]
    for piece in range(len(PIECES)):
        edge = units * sum(PIECES[:piece + 1]) // sum(PIECES) * LANES
        if edge > edges[-1]:
            edges.append(edge)
    spans = list(zip(edges[:-1], edges[1:]))

    def tokens_of():
        lower, upper = [tokens], [tokens]
        for step in range(1, rows):
            lower.append(lax.ppermute(lower[-1], "row", [(i, i + 1) for i in range(step - 1, rows - 1)]))
            upper.append(lax.ppermute(upper[-1], "row", [(i, i - 1) for i in range(1, rows - step + 1)]))
        before = [[], sent[:1]] + [[]] * (rows - 3) + [arrived[:1] + sent[1:4]]
        for slot in range(rows):
            chosen = {}
            for here, sources in enumerate(by_step(rows)):
                chosen.setdefault(sources[slot] - here, []).append(here)
            choices = [
                (places, upper[offset] if offset > 0 else lower[-offset]) for offset, places in chosen.items()
            ]
            value = pick(choices, before[slot]) if slot else tokens
            whole.append(lax.all_gather(value, "col", axis=1, tiled=True))

    def weights(shift, low, high, users):
        after = sent[-1:] + arrived[:len(sent) - 2][-1:] * (len(sent) > 2) + swapped[:len(sent) - 3][-1:] * (len(sent) > 3)
        sent.append(pack(gate_weight, up_weight, shift, low, high - low, after))
        arrived.append(lax.ppermute(sent[-1], "row", around(rows, shift)))
        came = hold(arrived[-1], done) if done else arrived[-1]
        for turn in range(parts):
            if turn:
                swapped.append(lax.ppermute(came, "parts", around(parts, -turn)))
            for n in users:
                held[n].append((shift, turn, low, swapped[-1] if turn else came))

    def hidden_of(n, after):
        low, high = spans[n]
        outs = product(whole, gate_weight, up_weight, held[n], low, high - low, mine, after)
        back = [lax.ppermute(outs[shift], "row", around(rows, shift)) for shift in range(1, rows)]
        blocks.extend((shift, low, value) for shift, value in enumerate([outs[0]] + back))
        done.append(outs[0])
        returned.append(back)

    last = len(spans) - 1
    far, *near = by_distance(rows)
    plan = [(far, 0, spans[max(last - 1, 0)][1], range(max(last, 1)))]
    for n, (low, high) in enumerate(spans):
        plan += [(shift, low, high, [n]) for shift in near]
        if n == 0 < last:
            plan.append((far, *spans[last], [last]))
    sent, arrived, swapped, done, returned, blocks = [], [], [], [], [], []
    held = [[] for _ in spans]
    whole = []
    for step in plan:
        if last and len(sent) == max(len(plan) - 2, 3):
            hidden_of(0, [])
        weights(*step)
        if len(sent) == min(4, max(len(plan) - 2, 3)):
            tokens_of()
    for n in range(min(last, 1), last + 1):
        hidden_of(n, done[-1:] + (returned[n - 2][:1] if n > 1 else []))
    early = len(blocks) - rows if last else len(blocks)
    out = place(blocks[:early], mine, ff)
    return place(blocks[early:], mine, ff, out) if last else out


def at_once(tokens, gate_weight, up_weight):
    rows, parts = lax.axis_size("row"), lax.axis_size("parts")
    y = lax.axis_index("parts")
    mine, ff = tokens.shape[0], gate_weight.shape[1]
    depth = gate_weight.shape[0]
    share, width = depth // parts, ff // rows

    whole = lax.all_gather(lax.all_gather(tokens, "row", axis=0, tiled=True), "col", axis=1, tiled=True)
    everyone = whole.shape[0]
    by_share = whole.reshape(everyone, rows, parts, share)
    sent = jnp.stack([
        lax.dynamic_slice(w, (y * share, 0), (share, ff)).reshape(share, rows, width).transpose(1, 0, 2)
        for w in (gate_weight, up_weight)
    ])
    held = lax.all_to_all(sent, "row", 1, 1, tiled=True)
    gate = up = 0.0
    for turn in range(parts):
        features = lax.dynamic_index_in_dim(by_share, (y + turn) % parts, 2, keepdims=False)
        features = features.reshape(everyone, rows * share)
        block = lax.ppermute(held, "parts", around(parts, -turn)) if turn else held
        block = block.reshape(2, rows * share, width)
        gate += jnp.dot(features, block[0], preferred_element_type=jnp.float32)
        up += jnp.dot(features, block[1], preferred_element_type=jnp.float32)
    done = (jax.nn.silu(gate) * up).astype(jnp.bfloat16)
    back = lax.all_to_all(done.reshape(rows, mine, width), "row", 0, 0, tiled=True)
    return back.transpose(1, 0, 2).reshape(mine, ff)


def on_device(tokens, gate_weight, up_weight):
    rows, parts = lax.axis_size("row"), lax.axis_size("parts")
    aligned = (
        gate_weight.shape[1] % (rows * LANES) == 0
        and gate_weight.shape[0] % (parts * 16) == 0
        and tokens.shape[0] % 16 == 0
    )
    return (in_tiles if aligned else at_once)(tokens, gate_weight, up_weight)


def solution(mesh):
    placed = (P(("parts", "row"), "col"), P("row", "col"), P("row", "col"))
    return jax.shard_map(
        on_device, mesh=mesh, in_specs=placed, out_specs=P(("parts", "row"), "col"), check_vma=False
    )
```

```python
import jax
import jax.numpy as jnp
from jax import lax
from jax.experimental import pallas as pl
from jax.experimental.pallas import tpu as pltpu
from jax.sharding import PartitionSpec as P

PIECES = (3, 2, 2)
GRANT = 60 * 2**20
LANES = 128
ANY = pl.BlockSpec(memory_space=pl.ANY)


def around(size, shift):
    return [(i, (i + shift) % size) for i in range(size)]


def by_distance(size):
    return sorted(range(1, size), key=lambda shift: -min(shift, size - shift))


def run_all(copies):
    for copy in copies:
        copy.start()
    for copy in copies:
        copy.wait()


def pack(gate_weight, up_weight, shift, low, wide, after):
    depth, ff = gate_weight.shape
    rows, parts = lax.axis_size("row"), lax.axis_size("parts")
    share, width, tiles = depth // parts, ff // rows, wide // LANES

    def body(*refs):
        weights, sent, sems = refs[:2], refs[-2], refs[-1]
        to = lax.rem(lax.axis_index("row") + shift, rows)
        first = pl.multiple_of(lax.axis_index("parts") * share, share)
        copies = []
        for j in range(tiles):
            start = pl.multiple_of(to * width + low + j * LANES, LANES)
            for g, weight in enumerate(weights):
                copies.append(pltpu.make_async_copy(
                    weight.at[pl.ds(first, share), pl.ds(start, LANES)],
                    sent.at[:, pl.ds((2 * j + g) * LANES, LANES)],
                    sems.at[2 * j + g],
                ))
        run_all(copies)

    size = share * 2 * wide * 2
    return pl.pallas_call(
        body,
        out_shape=jax.ShapeDtypeStruct((share, 2 * wide), gate_weight.dtype),
        in_specs=[ANY] * (2 + len(after)),
        out_specs=pl.BlockSpec(memory_space=pltpu.VMEM),
        scratch_shapes=[pltpu.SemaphoreType.DMA((2 * tiles,))],
        compiler_params=pltpu.CompilerParams(vmem_limit_bytes=GRANT),
        cost_estimate=pl.CostEstimate(flops=0, bytes_accessed=2 * size, transcendentals=0),
        name="pack",
    )(gate_weight, up_weight, *after)


def hold(value, after):
    def body(*refs):
        pass

    return pl.pallas_call(
        body,
        out_shape=jax.ShapeDtypeStruct(value.shape, value.dtype),
        in_specs=[ANY] * (1 + len(after)),
        out_specs=ANY,
        input_output_aliases={0: 0},
        name="hold",
    )(value, *after)


def product(tokens, gate_weight, up_weight, held, low, wide, mine, after):
    depth, ff = gate_weight.shape
    rows, parts = lax.axis_size("row"), lax.axis_size("parts")
    share, width, tiles = depth // parts, ff // rows, wide // LANES
    features = rows * depth
    sources = by_step(rows)
    order = by_distance(rows) + [0]

    def body(*refs):
        token_refs, (gate_ref, up_ref), refs = refs[:rows], refs[rows:rows + 2], refs[rows + 2:]
        held_refs = refs[:len(held)]
        outs = refs[len(held) + len(after):][:rows]
        stack, block, sems, block_sems = refs[-4:]
        z, y = lax.axis_index("row"), lax.axis_index("parts")

        def fetched(step, slot=0):
            return pltpu.make_async_copy(token_refs[slot], block.at[step % 2], block_sems.at[step % 2])

        def fetch(step):
            for here in range(rows):
                slot = sources[here].index((here + order[step]) % rows)
                pl.when(z == here)(lambda slot=slot: fetched(step, slot).start())

        copies = []
        for ref, (shift, turn, begin, _) in zip(held_refs, held):
            came = lax.rem(z + rows - shift, rows)
            half = lax.rem(y + turn, parts)
            start = pl.multiple_of(came * depth + half * share, share)
            copies.append(pltpu.make_async_copy(
                ref.at[:, pl.ds(2 * (low - begin), 2 * wide)], stack.at[pl.ds(start, share), :], sems.at[len(copies)]
            ))
        own = pl.multiple_of(z * depth, depth)
        for j in range(tiles):
            start = pl.multiple_of(z * width + low + j * LANES, LANES)
            for g, weight in enumerate((gate_ref, up_ref)):
                copies.append(pltpu.make_async_copy(
                    weight.at[:, pl.ds(start, LANES)],
                    stack.at[pl.ds(own, depth), pl.ds((2 * j + g) * LANES, LANES)],
                    sems.at[len(copies)],
                ))
        fetch(0)
        run_all(copies)
        for step, shift in enumerate(order):
            fetched(step).wait()
            if step + 1 < rows:
                fetch(step + 1)

            def tile(j, carry, step=step, shift=shift):
                both = jnp.dot(
                    block[step % 2],
                    stack[:, pl.ds(pl.multiple_of(j * 2 * LANES, 2 * LANES), 2 * LANES)],
                    preferred_element_type=jnp.float32,
                )
                gate, up = both[:, :LANES], both[:, LANES:]
                outs[shift][:, pl.ds(pl.multiple_of(j * LANES, LANES), LANES)] = (
                    jax.nn.silu(gate) * up
                ).astype(jnp.bfloat16)
                return carry

            lax.fori_loop(0, tiles, tile, 0)

    moved = 2 * (rows * mine * features + features * 2 * wide + rows * mine * wide)
    return pl.pallas_call(
        body,
        out_shape=[jax.ShapeDtypeStruct((mine, wide), jnp.bfloat16)] * rows,
        in_specs=[ANY] * (rows + 2 + len(held) + len(after)),
        out_specs=[pl.BlockSpec(memory_space=pltpu.VMEM)] * rows,
        scratch_shapes=[
            pltpu.VMEM((features, 2 * wide), gate_weight.dtype),
            pltpu.VMEM((2, mine, features), tokens[0].dtype),
            pltpu.SemaphoreType.DMA((len(held) + 2 * tiles,)),
            pltpu.SemaphoreType.DMA((2,)),
        ],
        compiler_params=pltpu.CompilerParams(vmem_limit_bytes=GRANT),
        cost_estimate=pl.CostEstimate(
            flops=4 * rows * mine * features * wide, bytes_accessed=moved, transcendentals=rows * mine * wide
        ),
        name="product",
    )(*tokens, gate_weight, up_weight, *[value for *_, value in held], *after)


def by_step(rows):
    sources = []
    for z in range(rows):
        above = [z + step for step in range(1, rows - z)]
        below = [z - step for step in range(1, z + 1)]
        sources.append([z] + (above + below if 2 * z < rows else below + above))
    return sources


def pick(choices, after):
    rows, like = lax.axis_size("row"), choices[0][1]

    def body(*refs):
        out, sem = refs[-2:]
        z = lax.axis_index("row")
        copies = [pltpu.make_async_copy(ref, out, sem) for ref, _ in zip(refs, choices)]
        for copy, (places, _) in zip(copies, choices):
            for place in places:
                pl.when(z == place)(copy.start)
        copies[0].wait()

    return pl.pallas_call(
        body,
        out_shape=jax.ShapeDtypeStruct(like.shape, like.dtype),
        in_specs=[ANY] * (len(choices) + len(after)),
        out_specs=pl.BlockSpec(memory_space=pltpu.VMEM),
        scratch_shapes=[pltpu.SemaphoreType.DMA],
        compiler_params=pltpu.CompilerParams(vmem_limit_bytes=GRANT),
        cost_estimate=pl.CostEstimate(flops=0, bytes_accessed=4 * like.size, transcendentals=0),
        name="pick",
    )(*[value for _, value in choices], *after)


def place(blocks, mine, ff, onto=None):
    rows = lax.axis_size("row")
    width = ff // rows
    known = [] if onto is None else [onto]

    def body(*refs):
        refs, out, slots, sems = refs[len(known):], refs[len(known) + len(blocks)], refs[-2 - len(blocks):-2], refs[-2:]
        z = lax.axis_index("row")
        loads, stores = [], []
        for n, (ref, slot, (shift, low, value)) in enumerate(zip(refs, slots, blocks)):
            came = lax.rem(z + rows - shift, rows)
            start = pl.multiple_of(came * width + low, LANES)
            loads.append(pltpu.make_async_copy(ref, slot, sems[0].at[n]))
            stores.append(pltpu.make_async_copy(slot, out.at[:, pl.ds(start, value.shape[1])], sems[1].at[n]))
        for load in loads:
            load.start()
        for load, store in zip(loads, stores):
            load.wait()
            store.start()
        for store in stores:
            store.wait()

    values = [value for _, _, value in blocks]
    return pl.pallas_call(
        body,
        out_shape=jax.ShapeDtypeStruct((mine, ff), jnp.bfloat16),
        in_specs=[ANY] * (len(known) + len(blocks)),
        out_specs=ANY,
        scratch_shapes=[pltpu.VMEM(value.shape, value.dtype) for value in values]
        + [pltpu.SemaphoreType.DMA((len(blocks),))] * 2,
        input_output_aliases={0: 0} if known else {},
        compiler_params=pltpu.CompilerParams(vmem_limit_bytes=GRANT),
        cost_estimate=pl.CostEstimate(
            flops=0, bytes_accessed=4 * sum(value.size for value in values), transcendentals=0
        ),
        name="place",
    )(*known, *values)


def in_tiles(tokens, gate_weight, up_weight):
    rows, parts = lax.axis_size("row"), lax.axis_size("parts")
    mine, ff = tokens.shape[0], gate_weight.shape[1]
    width = ff // rows
    units = width // LANES

    edges = [0]
    for piece in range(len(PIECES)):
        edge = units * sum(PIECES[:piece + 1]) // sum(PIECES) * LANES
        if edge > edges[-1]:
            edges.append(edge)
    spans = list(zip(edges[:-1], edges[1:]))

    def tokens_of():
        lower, upper = [tokens], [tokens]
        for step in range(1, rows):
            lower.append(lax.ppermute(lower[-1], "row", [(i, i + 1) for i in range(step - 1, rows - 1)]))
            upper.append(lax.ppermute(upper[-1], "row", [(i, i - 1) for i in range(1, rows - step + 1)]))
        z = lax.axis_index("row")
        before = {1: sent[:1], rows - 1: arrived[:1] + sent[1:3]}
        for slot in range(rows):
            chosen = {}
            for here, sources in enumerate(by_step(rows)):
                chosen.setdefault(sources[slot] - here, []).append(here)
            choices = [
                (places, upper[offset] if offset > 0 else lower[-offset]) for offset, places in chosen.items()
            ]
            if len(choices) == 2:
                (places, first), (_, second) = choices
                here = sum([z == place for place in places[1:]], start=z == places[0])
                value = jnp.where(here, first, second)
            else:
                value = pick(choices, []) if slot else tokens
            if slot in before:
                value = hold(value, before[slot])
            whole.append(lax.all_gather(value, "col", axis=1, tiled=True))

    def weights(shift, low, high, users):
        after = sent[-1:] + arrived[:len(sent) - 2][-1:] * (len(sent) > 2) + swapped[:len(sent) - 3][-1:] * (len(sent) > 3)
        sent.append(pack(gate_weight, up_weight, shift, low, high - low, after))
        arrived.append(lax.ppermute(sent[-1], "row", around(rows, shift)))
        came = hold(arrived[-1], done) if done else arrived[-1]
        for turn in range(parts):
            if turn:
                swapped.append(lax.ppermute(came, "parts", around(parts, -turn)))
            for n in users:
                held[n].append((shift, turn, low, swapped[-1] if turn else came))

    def hidden_of(n, after):
        low, high = spans[n]
        outs = product(whole, gate_weight, up_weight, held[n], low, high - low, mine, after)
        back = [lax.ppermute(outs[shift], "row", around(rows, shift)) for shift in by_distance(rows)]
        blocks.extend((shift, low, value) for shift, value in zip([0] + by_distance(rows), [outs[0]] + back))
        done.append(outs[0])
        returned.append(back)

    last = len(spans) - 1
    far, *near = by_distance(rows)
    plan = [(far, 0, spans[max(last - 1, 0)][1], range(max(last, 1)))]
    for n, (low, high) in enumerate(spans):
        plan += [(shift, low, high, [n]) for shift in near]
        if n == 0 < last:
            plan.append((far, *spans[last], [last]))
    sent, arrived, swapped, done, returned, blocks = [], [], [], [], [], []
    held = [[] for _ in spans]
    whole = []
    for step in plan:
        if last and len(sent) == max(len(plan) - 2, 3):
            hidden_of(0, [])
        weights(*step)
        if len(sent) == min(3, max(len(plan) - 2, 3)):
            tokens_of()
    for n in range(min(last, 1), last + 1):
        hidden_of(n, done[-1:] + (returned[n - 2][:1] if n > 1 else []))
    early = len(blocks) - rows if last else len(blocks)
    out = place(blocks[:early], mine, ff)
    return place(blocks[early:], mine, ff, out) if last else out


def at_once(tokens, gate_weight, up_weight):
    rows, parts = lax.axis_size("row"), lax.axis_size("parts")
    y = lax.axis_index("parts")
    mine, ff = tokens.shape[0], gate_weight.shape[1]
    depth = gate_weight.shape[0]
    share, width = depth // parts, ff // rows

    whole = lax.all_gather(lax.all_gather(tokens, "row", axis=0, tiled=True), "col", axis=1, tiled=True)
    everyone = whole.shape[0]
    by_share = whole.reshape(everyone, rows, parts, share)
    sent = jnp.stack([
        lax.dynamic_slice(w, (y * share, 0), (share, ff)).reshape(share, rows, width).transpose(1, 0, 2)
        for w in (gate_weight, up_weight)
    ])
    held = lax.all_to_all(sent, "row", 1, 1, tiled=True)
    gate = up = 0.0
    for turn in range(parts):
        features = lax.dynamic_index_in_dim(by_share, (y + turn) % parts, 2, keepdims=False)
        features = features.reshape(everyone, rows * share)
        block = lax.ppermute(held, "parts", around(parts, -turn)) if turn else held
        block = block.reshape(2, rows * share, width)
        gate += jnp.dot(features, block[0], preferred_element_type=jnp.float32)
        up += jnp.dot(features, block[1], preferred_element_type=jnp.float32)
    done = (jax.nn.silu(gate) * up).astype(jnp.bfloat16)
    back = lax.all_to_all(done.reshape(rows, mine, width), "row", 0, 0, tiled=True)
    return back.transpose(1, 0, 2).reshape(mine, ff)


def on_device(tokens, gate_weight, up_weight):
    rows, parts = lax.axis_size("row"), lax.axis_size("parts")
    aligned = (
        gate_weight.shape[1] % (rows * LANES) == 0
        and gate_weight.shape[0] % (parts * 16) == 0
        and tokens.shape[0] % 16 == 0
    )
    return (in_tiles if aligned else at_once)(tokens, gate_weight, up_weight)


def solution(mesh):
    placed = (P(("parts", "row"), "col"), P("row", "col"), P("row", "col"))
    return jax.shard_map(
        on_device, mesh=mesh, in_specs=placed, out_specs=P(("parts", "row"), "col"), check_vma=False
    )
```

```python
import jax
import jax.numpy as jnp
from jax import lax
from jax.experimental import pallas as pl
from jax.experimental.pallas import tpu as pltpu
from jax.sharding import PartitionSpec as P

PIECES = (3, 2, 2)
GRANT = 60 * 2**20
LANES = 128
ANY = pl.BlockSpec(memory_space=pl.ANY)


def around(size, shift):
    return [(i, (i + shift) % size) for i in range(size)]


def by_distance(size):
    return sorted(range(1, size), key=lambda shift: -min(shift, size - shift))


def run_all(copies):
    for copy in copies:
        copy.start()
    for copy in copies:
        copy.wait()


def pack(gate_weight, up_weight, shift, low, wide, after):
    depth, ff = gate_weight.shape
    rows, parts = lax.axis_size("row"), lax.axis_size("parts")
    share, width, tiles = depth // parts, ff // rows, wide // LANES

    def body(*refs):
        weights, sent, sems = refs[:2], refs[-2], refs[-1]
        to = lax.rem(lax.axis_index("row") + shift, rows)
        first = pl.multiple_of(lax.axis_index("parts") * share, share)
        copies = []
        for j in range(tiles):
            start = pl.multiple_of(to * width + low + j * LANES, LANES)
            for g, weight in enumerate(weights):
                copies.append(pltpu.make_async_copy(
                    weight.at[pl.ds(first, share), pl.ds(start, LANES)],
                    sent.at[:, pl.ds((2 * j + g) * LANES, LANES)],
                    sems.at[2 * j + g],
                ))
        run_all(copies)

    size = share * 2 * wide * 2
    return pl.pallas_call(
        body,
        out_shape=jax.ShapeDtypeStruct((share, 2 * wide), gate_weight.dtype),
        in_specs=[ANY] * (2 + len(after)),
        out_specs=pl.BlockSpec(memory_space=pltpu.VMEM),
        scratch_shapes=[pltpu.SemaphoreType.DMA((2 * tiles,))],
        compiler_params=pltpu.CompilerParams(vmem_limit_bytes=GRANT),
        cost_estimate=pl.CostEstimate(flops=0, bytes_accessed=2 * size, transcendentals=0),
        name="pack",
    )(gate_weight, up_weight, *after)


def hold(value, after):
    def body(*refs):
        pass

    return pl.pallas_call(
        body,
        out_shape=jax.ShapeDtypeStruct(value.shape, value.dtype),
        in_specs=[ANY] * (1 + len(after)),
        out_specs=ANY,
        input_output_aliases={0: 0},
        name="hold",
    )(value, *after)


def product(tokens, gate_weight, up_weight, held, low, wide, mine, after):
    depth, ff = gate_weight.shape
    rows, parts = lax.axis_size("row"), lax.axis_size("parts")
    share, width, tiles = depth // parts, ff // rows, wide // LANES
    features = rows * depth
    sources = by_step(rows)
    order = by_distance(rows) + [0]

    def body(*refs):
        token_refs, (gate_ref, up_ref), refs = refs[:rows], refs[rows:rows + 2], refs[rows + 2:]
        held_refs = refs[:len(held)]
        outs = refs[len(held) + len(after):][:rows]
        stack, block, sems, block_sems = refs[-4:]
        z, y = lax.axis_index("row"), lax.axis_index("parts")

        def fetched(step, slot=0):
            return pltpu.make_async_copy(token_refs[slot], block.at[step % 2], block_sems.at[step % 2])

        def fetch(step):
            for here in range(rows):
                slot = sources[here].index((here + order[step]) % rows)
                pl.when(z == here)(lambda slot=slot: fetched(step, slot).start())

        copies = []
        for ref, (shift, turn, begin, _) in zip(held_refs, held):
            came = lax.rem(z + rows - shift, rows)
            half = lax.rem(y + turn, parts)
            start = pl.multiple_of(came * depth + half * share, share)
            copies.append(pltpu.make_async_copy(
                ref.at[:, pl.ds(2 * (low - begin), 2 * wide)], stack.at[pl.ds(start, share), :], sems.at[len(copies)]
            ))
        own = pl.multiple_of(z * depth, depth)
        for j in range(tiles):
            start = pl.multiple_of(z * width + low + j * LANES, LANES)
            for g, weight in enumerate((gate_ref, up_ref)):
                copies.append(pltpu.make_async_copy(
                    weight.at[:, pl.ds(start, LANES)],
                    stack.at[pl.ds(own, depth), pl.ds((2 * j + g) * LANES, LANES)],
                    sems.at[len(copies)],
                ))
        fetch(0)
        run_all(copies)
        for step, shift in enumerate(order):
            fetched(step).wait()
            if step + 1 < rows:
                fetch(step + 1)

            def tile(j, carry, step=step, shift=shift):
                both = jnp.dot(
                    block[step % 2],
                    stack[:, pl.ds(pl.multiple_of(j * 2 * LANES, 2 * LANES), 2 * LANES)],
                    preferred_element_type=jnp.float32,
                )
                gate, up = both[:, :LANES], both[:, LANES:]
                outs[shift][:, pl.ds(pl.multiple_of(j * LANES, LANES), LANES)] = (
                    jax.nn.silu(gate) * up
                ).astype(jnp.bfloat16)
                return carry

            lax.fori_loop(0, tiles, tile, 0)

    moved = 2 * (rows * mine * features + features * 2 * wide + rows * mine * wide)
    return pl.pallas_call(
        body,
        out_shape=[jax.ShapeDtypeStruct((mine, wide), jnp.bfloat16)] * rows,
        in_specs=[ANY] * (rows + 2 + len(held) + len(after)),
        out_specs=[pl.BlockSpec(memory_space=pltpu.VMEM)] * rows,
        scratch_shapes=[
            pltpu.VMEM((features, 2 * wide), gate_weight.dtype),
            pltpu.VMEM((2, mine, features), tokens[0].dtype),
            pltpu.SemaphoreType.DMA((len(held) + 2 * tiles,)),
            pltpu.SemaphoreType.DMA((2,)),
        ],
        compiler_params=pltpu.CompilerParams(vmem_limit_bytes=GRANT),
        cost_estimate=pl.CostEstimate(
            flops=4 * rows * mine * features * wide, bytes_accessed=moved, transcendentals=rows * mine * wide
        ),
        name="product",
    )(*tokens, gate_weight, up_weight, *[value for *_, value in held], *after)


def by_step(rows):
    sources = []
    for z in range(rows):
        above = [z + step for step in range(1, rows - z)]
        below = [z - step for step in range(1, z + 1)]
        sources.append([z] + (above + below if 2 * z < rows else below + above))
    return sources


def pick(choices, after):
    rows, like = lax.axis_size("row"), choices[0][1]

    def body(*refs):
        out, sem = refs[-2:]
        z = lax.axis_index("row")
        copies = [pltpu.make_async_copy(ref, out, sem) for ref, _ in zip(refs, choices)]
        for copy, (places, _) in zip(copies, choices):
            for place in places:
                pl.when(z == place)(copy.start)
        copies[0].wait()

    return pl.pallas_call(
        body,
        out_shape=jax.ShapeDtypeStruct(like.shape, like.dtype),
        in_specs=[ANY] * (len(choices) + len(after)),
        out_specs=pl.BlockSpec(memory_space=pltpu.VMEM),
        scratch_shapes=[pltpu.SemaphoreType.DMA],
        compiler_params=pltpu.CompilerParams(vmem_limit_bytes=GRANT),
        cost_estimate=pl.CostEstimate(flops=0, bytes_accessed=4 * like.size, transcendentals=0),
        name="pick",
    )(*[value for _, value in choices], *after)


def place(blocks, mine, ff, onto=None):
    rows = lax.axis_size("row")
    width = ff // rows
    known = [] if onto is None else [onto]

    def body(*refs):
        refs, out, slots, sems = refs[len(known):], refs[len(known) + len(blocks)], refs[-2 - len(blocks):-2], refs[-2:]
        z = lax.axis_index("row")
        loads, stores = [], []
        for n, (ref, slot, (shift, low, value)) in enumerate(zip(refs, slots, blocks)):
            came = lax.rem(z + rows - shift, rows)
            start = pl.multiple_of(came * width + low, LANES)
            loads.append(pltpu.make_async_copy(ref, slot, sems[0].at[n]))
            stores.append(pltpu.make_async_copy(slot, out.at[:, pl.ds(start, value.shape[1])], sems[1].at[n]))
        for load in loads:
            load.start()
        for load, store in zip(loads, stores):
            load.wait()
            store.start()
        for store in stores:
            store.wait()

    values = [value for _, _, value in blocks]
    return pl.pallas_call(
        body,
        out_shape=jax.ShapeDtypeStruct((mine, ff), jnp.bfloat16),
        in_specs=[ANY] * (len(known) + len(blocks)),
        out_specs=ANY,
        scratch_shapes=[pltpu.VMEM(value.shape, value.dtype) for value in values]
        + [pltpu.SemaphoreType.DMA((len(blocks),))] * 2,
        input_output_aliases={0: 0} if known else {},
        compiler_params=pltpu.CompilerParams(vmem_limit_bytes=GRANT),
        cost_estimate=pl.CostEstimate(
            flops=0, bytes_accessed=4 * sum(value.size for value in values), transcendentals=0
        ),
        name="place",
    )(*known, *values)


def in_tiles(tokens, gate_weight, up_weight):
    rows, parts = lax.axis_size("row"), lax.axis_size("parts")
    mine, ff = tokens.shape[0], gate_weight.shape[1]
    width = ff // rows
    units = width // LANES

    edges = [0]
    for piece in range(len(PIECES)):
        edge = units * sum(PIECES[:piece + 1]) // sum(PIECES) * LANES
        if edge > edges[-1]:
            edges.append(edge)
    spans = list(zip(edges[:-1], edges[1:]))

    def tokens_of():
        lower, upper = [tokens], [tokens]
        for step in range(1, rows):
            lower.append(lax.ppermute(lower[-1], "row", [(i, i + 1) for i in range(step - 1, rows - 1)]))
            upper.append(lax.ppermute(upper[-1], "row", [(i, i - 1) for i in range(1, rows - step + 1)]))
        z = lax.axis_index("row")
        before = {1: sent[:1], rows - 1: arrived[:1] + sent[1:3]}
        for slot in range(rows):
            chosen = {}
            for here, sources in enumerate(by_step(rows)):
                chosen.setdefault(sources[slot] - here, []).append(here)
            choices = [
                (places, upper[offset] if offset > 0 else lower[-offset]) for offset, places in chosen.items()
            ]
            if len(choices) == 2:
                (places, first), (_, second) = choices
                here = sum([z == place for place in places[1:]], start=z == places[0])
                value = jnp.where(here, first, second)
            else:
                value = pick(choices, []) if slot else tokens
            if slot in before:
                value = hold(value, before[slot])
            whole.append(lax.all_gather(value, "col", axis=1, tiled=True))

    def weights(shift, low, high, users):
        after = sent[-1:] + arrived[:len(sent) - 2][-1:] * (len(sent) > 2) + swapped[:len(sent) - 3][-1:] * (len(sent) > 4)
        sent.append(pack(gate_weight, up_weight, shift, low, high - low, after))
        arrived.append(lax.ppermute(sent[-1], "row", around(rows, shift)))
        came = hold(arrived[-1], done) if done else arrived[-1]
        for turn in range(parts):
            if turn:
                swapped.append(lax.ppermute(came, "parts", around(parts, -turn)))
            for n in users:
                held[n].append((shift, turn, low, swapped[-1] if turn else came))

    def hidden_of(n, after):
        low, high = spans[n]
        outs = product(whole, gate_weight, up_weight, held[n], low, high - low, mine, after)
        back = [lax.ppermute(outs[shift], "row", around(rows, shift)) for shift in by_distance(rows)]
        blocks.extend((shift, low, value) for shift, value in zip([0] + by_distance(rows), [outs[0]] + back))
        done.append(outs[0])
        returned.append(back)

    last = len(spans) - 1
    far, *near = by_distance(rows)
    plan = [(far, 0, spans[max(last - 1, 0)][1], range(max(last, 1)))]
    for n, (low, high) in enumerate(spans):
        plan += [(shift, low, high, [n]) for shift in near]
        if n == 0 < last:
            plan.append((far, *spans[last], [last]))
    sent, arrived, swapped, done, returned, blocks = [], [], [], [], [], []
    held = [[] for _ in spans]
    whole = []
    for step in plan:
        if last and len(sent) == max(len(plan) - 2, 3):
            hidden_of(0, [])
        weights(*step)
        if len(sent) == min(3, max(len(plan) - 2, 3)):
            tokens_of()
    for n in range(min(last, 1), last + 1):
        hidden_of(n, done[-1:] + (returned[n - 2][:1] if n > 1 else []))
    early = len(blocks) - rows if last else len(blocks)
    out = place(blocks[:early], mine, ff)
    return place(blocks[early:], mine, ff, out) if last else out


def at_once(tokens, gate_weight, up_weight):
    rows, parts = lax.axis_size("row"), lax.axis_size("parts")
    y = lax.axis_index("parts")
    mine, ff = tokens.shape[0], gate_weight.shape[1]
    depth = gate_weight.shape[0]
    share, width = depth // parts, ff // rows

    whole = lax.all_gather(lax.all_gather(tokens, "row", axis=0, tiled=True), "col", axis=1, tiled=True)
    everyone = whole.shape[0]
    by_share = whole.reshape(everyone, rows, parts, share)
    sent = jnp.stack([
        lax.dynamic_slice(w, (y * share, 0), (share, ff)).reshape(share, rows, width).transpose(1, 0, 2)
        for w in (gate_weight, up_weight)
    ])
    held = lax.all_to_all(sent, "row", 1, 1, tiled=True)
    gate = up = 0.0
    for turn in range(parts):
        features = lax.dynamic_index_in_dim(by_share, (y + turn) % parts, 2, keepdims=False)
        features = features.reshape(everyone, rows * share)
        block = lax.ppermute(held, "parts", around(parts, -turn)) if turn else held
        block = block.reshape(2, rows * share, width)
        gate += jnp.dot(features, block[0], preferred_element_type=jnp.float32)
        up += jnp.dot(features, block[1], preferred_element_type=jnp.float32)
    done = (jax.nn.silu(gate) * up).astype(jnp.bfloat16)
    back = lax.all_to_all(done.reshape(rows, mine, width), "row", 0, 0, tiled=True)
    return back.transpose(1, 0, 2).reshape(mine, ff)


def on_device(tokens, gate_weight, up_weight):
    rows, parts = lax.axis_size("row"), lax.axis_size("parts")
    aligned = (
        gate_weight.shape[1] % (rows * LANES) == 0
        and gate_weight.shape[0] % (parts * 16) == 0
        and tokens.shape[0] % 16 == 0
    )
    return (in_tiles if aligned else at_once)(tokens, gate_weight, up_weight)


def solution(mesh):
    placed = (P(("parts", "row"), "col"), P("row", "col"), P("row", "col"))
    return jax.shard_map(
        on_device, mesh=mesh, in_specs=placed, out_specs=P(("parts", "row"), "col"), check_vma=False
    )
```

```python
import jax
import jax.numpy as jnp
from jax import lax
from jax.experimental import pallas as pl
from jax.experimental.pallas import tpu as pltpu
from jax.sharding import PartitionSpec as P

PIECES = (4, 2, 1)
GRANT = 60 * 2**20
LANES = 128
ANY = pl.BlockSpec(memory_space=pl.ANY)


def around(size, shift):
    return [(i, (i + shift) % size) for i in range(size)]


def by_distance(size):
    return sorted(range(1, size), key=lambda shift: -min(shift, size - shift))


def run_all(copies):
    for copy in copies:
        copy.start()
    for copy in copies:
        copy.wait()


def pack(gate_weight, up_weight, shift, low, wide, after):
    depth, ff = gate_weight.shape
    rows, parts = lax.axis_size("row"), lax.axis_size("parts")
    share, width, tiles = depth // parts, ff // rows, wide // LANES

    def body(*refs):
        weights, sent, sems = refs[:2], refs[-2], refs[-1]
        to = lax.rem(lax.axis_index("row") + shift, rows)
        first = pl.multiple_of(lax.axis_index("parts") * share, share)
        copies = []
        for j in range(tiles):
            start = pl.multiple_of(to * width + low + j * LANES, LANES)
            for g, weight in enumerate(weights):
                copies.append(pltpu.make_async_copy(
                    weight.at[pl.ds(first, share), pl.ds(start, LANES)],
                    sent.at[:, pl.ds((2 * j + g) * LANES, LANES)],
                    sems.at[2 * j + g],
                ))
        run_all(copies)

    size = share * 2 * wide * 2
    return pl.pallas_call(
        body,
        out_shape=jax.ShapeDtypeStruct((share, 2 * wide), gate_weight.dtype),
        in_specs=[ANY] * (2 + len(after)),
        out_specs=pl.BlockSpec(memory_space=pltpu.VMEM),
        scratch_shapes=[pltpu.SemaphoreType.DMA((2 * tiles,))],
        compiler_params=pltpu.CompilerParams(vmem_limit_bytes=GRANT),
        cost_estimate=pl.CostEstimate(flops=0, bytes_accessed=2 * size, transcendentals=0),
        name="pack",
    )(gate_weight, up_weight, *after)


def hold(value, after):
    def body(*refs):
        pass

    return pl.pallas_call(
        body,
        out_shape=jax.ShapeDtypeStruct(value.shape, value.dtype),
        in_specs=[ANY] * (1 + len(after)),
        out_specs=ANY,
        input_output_aliases={0: 0},
        name="hold",
    )(value, *after)


def product(tokens, gate_weight, up_weight, held, low, wide, mine, after):
    depth, ff = gate_weight.shape
    rows, parts = lax.axis_size("row"), lax.axis_size("parts")
    share, width, tiles = depth // parts, ff // rows, wide // LANES
    features = rows * depth
    sources = by_step(rows)
    order = by_distance(rows) + [0]

    def body(*refs):
        token_refs, (gate_ref, up_ref), refs = refs[:rows], refs[rows:rows + 2], refs[rows + 2:]
        held_refs = refs[:len(held)]
        outs = refs[len(held) + len(after):][:rows]
        stack, block, sems, block_sems = refs[-4:]
        z, y = lax.axis_index("row"), lax.axis_index("parts")

        def fetched(step, slot=0):
            return pltpu.make_async_copy(token_refs[slot], block.at[step % 2], block_sems.at[step % 2])

        def fetch(step):
            for here in range(rows):
                slot = sources[here].index((here + order[step]) % rows)
                pl.when(z == here)(lambda slot=slot: fetched(step, slot).start())

        copies = []
        for ref, (shift, turn, begin, _) in zip(held_refs, held):
            came = lax.rem(z + rows - shift, rows)
            half = lax.rem(y + turn, parts)
            start = pl.multiple_of(came * depth + half * share, share)
            copies.append(pltpu.make_async_copy(
                ref.at[:, pl.ds(2 * (low - begin), 2 * wide)], stack.at[pl.ds(start, share), :], sems.at[len(copies)]
            ))
        own = pl.multiple_of(z * depth, depth)
        for j in range(tiles):
            start = pl.multiple_of(z * width + low + j * LANES, LANES)
            for g, weight in enumerate((gate_ref, up_ref)):
                copies.append(pltpu.make_async_copy(
                    weight.at[:, pl.ds(start, LANES)],
                    stack.at[pl.ds(own, depth), pl.ds((2 * j + g) * LANES, LANES)],
                    sems.at[len(copies)],
                ))
        fetch(0)
        run_all(copies)
        for step, shift in enumerate(order):
            fetched(step).wait()
            if step + 1 < rows:
                fetch(step + 1)

            def tile(j, carry, step=step, shift=shift):
                both = jnp.dot(
                    block[step % 2],
                    stack[:, pl.ds(pl.multiple_of(j * 2 * LANES, 2 * LANES), 2 * LANES)],
                    preferred_element_type=jnp.float32,
                )
                gate, up = both[:, :LANES], both[:, LANES:]
                outs[shift][:, pl.ds(pl.multiple_of(j * LANES, LANES), LANES)] = (
                    jax.nn.silu(gate) * up
                ).astype(jnp.bfloat16)
                return carry

            lax.fori_loop(0, tiles, tile, 0)

    moved = 2 * (rows * mine * features + features * 2 * wide + rows * mine * wide)
    return pl.pallas_call(
        body,
        out_shape=[jax.ShapeDtypeStruct((mine, wide), jnp.bfloat16)] * rows,
        in_specs=[ANY] * (rows + 2 + len(held) + len(after)),
        out_specs=[pl.BlockSpec(memory_space=pltpu.VMEM)] * rows,
        scratch_shapes=[
            pltpu.VMEM((features, 2 * wide), gate_weight.dtype),
            pltpu.VMEM((2, mine, features), tokens[0].dtype),
            pltpu.SemaphoreType.DMA((len(held) + 2 * tiles,)),
            pltpu.SemaphoreType.DMA((2,)),
        ],
        compiler_params=pltpu.CompilerParams(vmem_limit_bytes=GRANT),
        cost_estimate=pl.CostEstimate(
            flops=4 * rows * mine * features * wide, bytes_accessed=moved, transcendentals=rows * mine * wide
        ),
        name="product",
    )(*tokens, gate_weight, up_weight, *[value for *_, value in held], *after)


def by_step(rows):
    sources = []
    for z in range(rows):
        above = [z + step for step in range(1, rows - z)]
        below = [z - step for step in range(1, z + 1)]
        sources.append([z] + (above + below if 2 * z < rows else below + above))
    return sources


def pick(choices, after):
    rows, like = lax.axis_size("row"), choices[0][1]

    def body(*refs):
        out, sem = refs[-2:]
        z = lax.axis_index("row")
        copies = [pltpu.make_async_copy(ref, out, sem) for ref, _ in zip(refs, choices)]
        for copy, (places, _) in zip(copies, choices):
            for place in places:
                pl.when(z == place)(copy.start)
        copies[0].wait()

    return pl.pallas_call(
        body,
        out_shape=jax.ShapeDtypeStruct(like.shape, like.dtype),
        in_specs=[ANY] * (len(choices) + len(after)),
        out_specs=pl.BlockSpec(memory_space=pltpu.VMEM),
        scratch_shapes=[pltpu.SemaphoreType.DMA],
        compiler_params=pltpu.CompilerParams(vmem_limit_bytes=GRANT),
        cost_estimate=pl.CostEstimate(flops=0, bytes_accessed=4 * like.size, transcendentals=0),
        name="pick",
    )(*[value for _, value in choices], *after)


def place(blocks, mine, ff, onto=None):
    rows = lax.axis_size("row")
    width = ff // rows
    known = [] if onto is None else [onto]

    def body(*refs):
        refs, out, slots, sems = refs[len(known):], refs[len(known) + len(blocks)], refs[-2 - len(blocks):-2], refs[-2:]
        z = lax.axis_index("row")
        loads, stores = [], []
        for n, (ref, slot, (shift, low, value)) in enumerate(zip(refs, slots, blocks)):
            came = lax.rem(z + rows - shift, rows)
            start = pl.multiple_of(came * width + low, LANES)
            loads.append(pltpu.make_async_copy(ref, slot, sems[0].at[n]))
            stores.append(pltpu.make_async_copy(slot, out.at[:, pl.ds(start, value.shape[1])], sems[1].at[n]))
        for load in loads:
            load.start()
        for load, store in zip(loads, stores):
            load.wait()
            store.start()
        for store in stores:
            store.wait()

    values = [value for _, _, value in blocks]
    return pl.pallas_call(
        body,
        out_shape=jax.ShapeDtypeStruct((mine, ff), jnp.bfloat16),
        in_specs=[ANY] * (len(known) + len(blocks)),
        out_specs=ANY,
        scratch_shapes=[pltpu.VMEM(value.shape, value.dtype) for value in values]
        + [pltpu.SemaphoreType.DMA((len(blocks),))] * 2,
        input_output_aliases={0: 0} if known else {},
        compiler_params=pltpu.CompilerParams(vmem_limit_bytes=GRANT),
        cost_estimate=pl.CostEstimate(
            flops=0, bytes_accessed=4 * sum(value.size for value in values), transcendentals=0
        ),
        name="place",
    )(*known, *values)


def in_tiles(tokens, gate_weight, up_weight):
    rows, parts = lax.axis_size("row"), lax.axis_size("parts")
    mine, ff = tokens.shape[0], gate_weight.shape[1]
    width = ff // rows
    units = width // LANES

    edges = [0]
    for piece in range(len(PIECES)):
        edge = units * sum(PIECES[:piece + 1]) // sum(PIECES) * LANES
        if edge > edges[-1]:
            edges.append(edge)
    spans = list(zip(edges[:-1], edges[1:]))

    def tokens_of():
        lower, upper = [tokens], [tokens]
        for step in range(1, rows):
            lower.append(lax.ppermute(lower[-1], "row", [(i, i + 1) for i in range(step - 1, rows - 1)]))
            upper.append(lax.ppermute(upper[-1], "row", [(i, i - 1) for i in range(1, rows - step + 1)]))
        z = lax.axis_index("row")
        before = {1: sent[:1], rows - 1: arrived[:1] + sent[1:3]}
        for slot in range(rows):
            chosen = {}
            for here, sources in enumerate(by_step(rows)):
                chosen.setdefault(sources[slot] - here, []).append(here)
            choices = [
                (places, upper[offset] if offset > 0 else lower[-offset]) for offset, places in chosen.items()
            ]
            if len(choices) == 2:
                (places, first), (_, second) = choices
                here = sum([z == place for place in places[1:]], start=z == places[0])
                value = jnp.where(here, first, second)
            else:
                value = pick(choices, []) if slot else tokens
            if slot in before:
                value = hold(value, before[slot])
            whole.append(lax.all_gather(value, "col", axis=1, tiled=True))

    def weights(shift, low, high, users):
        after = sent[-1:] + arrived[:len(sent) - 2][-1:] * (len(sent) > 2) + swapped[:len(sent) - 3][-1:] * (len(sent) > 3)
        sent.append(pack(gate_weight, up_weight, shift, low, high - low, after))
        arrived.append(lax.ppermute(sent[-1], "row", around(rows, shift)))
        came = hold(arrived[-1], done) if done else arrived[-1]
        for turn in range(parts):
            if turn:
                swapped.append(lax.ppermute(came, "parts", around(parts, -turn)))
            for n in users:
                held[n].append((shift, turn, low, swapped[-1] if turn else came))

    def hidden_of(n, after):
        low, high = spans[n]
        outs = product(whole, gate_weight, up_weight, held[n], low, high - low, mine, after)
        back = [lax.ppermute(outs[shift], "row", around(rows, shift)) for shift in by_distance(rows)]
        blocks.extend((shift, low, value) for shift, value in zip([0] + by_distance(rows), [outs[0]] + back))
        done.append(outs[0])
        returned.append(back)

    last = len(spans) - 1
    far, *near = by_distance(rows)
    plan = [(far, 0, spans[max(last - 1, 0)][1], range(max(last, 1)))]
    for n, (low, high) in enumerate(spans):
        plan += [(shift, low, high, [n]) for shift in near]
        if n == 0 < last:
            plan.append((far, *spans[last], [last]))
    sent, arrived, swapped, done, returned, blocks = [], [], [], [], [], []
    held = [[] for _ in spans]
    whole = []
    for step in plan:
        if last and len(sent) == max(len(plan) - 2, 3):
            hidden_of(0, [])
        weights(*step)
        if len(sent) == min(3, max(len(plan) - 2, 3)):
            tokens_of()
    for n in range(min(last, 1), last + 1):
        hidden_of(n, done[-1:] + (returned[n - 2][:1] if n > 1 else []))
    early = len(blocks) - rows if last else len(blocks)
    out = place(blocks[:early], mine, ff)
    return place(blocks[early:], mine, ff, out) if last else out


def at_once(tokens, gate_weight, up_weight):
    rows, parts = lax.axis_size("row"), lax.axis_size("parts")
    y = lax.axis_index("parts")
    mine, ff = tokens.shape[0], gate_weight.shape[1]
    depth = gate_weight.shape[0]
    share, width = depth // parts, ff // rows

    whole = lax.all_gather(lax.all_gather(tokens, "row", axis=0, tiled=True), "col", axis=1, tiled=True)
    everyone = whole.shape[0]
    by_share = whole.reshape(everyone, rows, parts, share)
    sent = jnp.stack([
        lax.dynamic_slice(w, (y * share, 0), (share, ff)).reshape(share, rows, width).transpose(1, 0, 2)
        for w in (gate_weight, up_weight)
    ])
    held = lax.all_to_all(sent, "row", 1, 1, tiled=True)
    gate = up = 0.0
    for turn in range(parts):
        features = lax.dynamic_index_in_dim(by_share, (y + turn) % parts, 2, keepdims=False)
        features = features.reshape(everyone, rows * share)
        block = lax.ppermute(held, "parts", around(parts, -turn)) if turn else held
        block = block.reshape(2, rows * share, width)
        gate += jnp.dot(features, block[0], preferred_element_type=jnp.float32)
        up += jnp.dot(features, block[1], preferred_element_type=jnp.float32)
    done = (jax.nn.silu(gate) * up).astype(jnp.bfloat16)
    back = lax.all_to_all(done.reshape(rows, mine, width), "row", 0, 0, tiled=True)
    return back.transpose(1, 0, 2).reshape(mine, ff)


def on_device(tokens, gate_weight, up_weight):
    rows, parts = lax.axis_size("row"), lax.axis_size("parts")
    aligned = (
        gate_weight.shape[1] % (rows * LANES) == 0
        and gate_weight.shape[0] % (parts * 16) == 0
        and tokens.shape[0] % 16 == 0
    )
    return (in_tiles if aligned else at_once)(tokens, gate_weight, up_weight)


def solution(mesh):
    placed = (P(("parts", "row"), "col"), P("row", "col"), P("row", "col"))
    return jax.shard_map(
        on_device, mesh=mesh, in_specs=placed, out_specs=P(("parts", "row"), "col"), check_vma=False
    )
```

```python
import jax
import jax.numpy as jnp
from jax import lax
from jax.experimental import pallas as pl
from jax.experimental.pallas import tpu as pltpu
from jax.sharding import PartitionSpec as P

PIECES = (3, 2, 2)
GRANT = 60 * 2**20
LANES = 128
ANY = pl.BlockSpec(memory_space=pl.ANY)


def around(size, shift):
    return [(i, (i + shift) % size) for i in range(size)]


def by_distance(size):
    return sorted(range(1, size), key=lambda shift: -min(shift, size - shift))


def run_all(copies):
    for copy in copies:
        copy.start()
    for copy in copies:
        copy.wait()


def pack(gate_weight, up_weight, shift, low, wide, after):
    depth, ff = gate_weight.shape
    rows, parts = lax.axis_size("row"), lax.axis_size("parts")
    share, width, tiles = depth // parts, ff // rows, wide // LANES

    def body(*refs):
        weights, sent, sems = refs[:2], refs[-2], refs[-1]
        to = lax.rem(lax.axis_index("row") + shift, rows)
        first = pl.multiple_of(lax.axis_index("parts") * share, share)
        copies = []
        for j in range(tiles):
            start = pl.multiple_of(to * width + low + j * LANES, LANES)
            for g, weight in enumerate(weights):
                copies.append(pltpu.make_async_copy(
                    weight.at[pl.ds(first, share), pl.ds(start, LANES)],
                    sent.at[:, pl.ds((2 * j + g) * LANES, LANES)],
                    sems.at[2 * j + g],
                ))
        run_all(copies)

    size = share * 2 * wide * 2
    return pl.pallas_call(
        body,
        out_shape=jax.ShapeDtypeStruct((share, 2 * wide), gate_weight.dtype),
        in_specs=[ANY] * (2 + len(after)),
        out_specs=pl.BlockSpec(memory_space=pltpu.VMEM),
        scratch_shapes=[pltpu.SemaphoreType.DMA((2 * tiles,))],
        compiler_params=pltpu.CompilerParams(vmem_limit_bytes=GRANT),
        cost_estimate=pl.CostEstimate(flops=0, bytes_accessed=2 * size, transcendentals=0),
        name="pack",
    )(gate_weight, up_weight, *after)


def hold(value, after):
    def body(*refs):
        pass

    return pl.pallas_call(
        body,
        out_shape=jax.ShapeDtypeStruct(value.shape, value.dtype),
        in_specs=[ANY] * (1 + len(after)),
        out_specs=ANY,
        input_output_aliases={0: 0},
        name="hold",
    )(value, *after)


def product(tokens, gate_weight, up_weight, held, low, wide, mine, after):
    depth, ff = gate_weight.shape
    rows, parts = lax.axis_size("row"), lax.axis_size("parts")
    share, width, tiles = depth // parts, ff // rows, wide // LANES
    features = rows * depth
    sources = by_step(rows)
    order = by_distance(rows) + [0]

    def body(*refs):
        token_refs, (gate_ref, up_ref), refs = refs[:rows], refs[rows:rows + 2], refs[rows + 2:]
        held_refs = refs[:len(held)]
        outs = refs[len(held) + len(after):][:rows]
        stack, block, sems, block_sems = refs[-4:]
        z, y = lax.axis_index("row"), lax.axis_index("parts")

        def fetched(step, slot=0):
            return pltpu.make_async_copy(token_refs[slot], block.at[step % 2], block_sems.at[step % 2])

        def fetch(step):
            for here in range(rows):
                slot = sources[here].index((here + order[step]) % rows)
                pl.when(z == here)(lambda slot=slot: fetched(step, slot).start())

        copies = []
        for ref, (shift, turn, begin, _) in zip(held_refs, held):
            came = lax.rem(z + rows - shift, rows)
            half = lax.rem(y + turn, parts)
            start = pl.multiple_of(came * depth + half * share, share)
            copies.append(pltpu.make_async_copy(
                ref.at[:, pl.ds(2 * (low - begin), 2 * wide)], stack.at[pl.ds(start, share), :], sems.at[len(copies)]
            ))
        own = pl.multiple_of(z * depth, depth)
        for j in range(tiles):
            start = pl.multiple_of(z * width + low + j * LANES, LANES)
            for g, weight in enumerate((gate_ref, up_ref)):
                copies.append(pltpu.make_async_copy(
                    weight.at[:, pl.ds(start, LANES)],
                    stack.at[pl.ds(own, depth), pl.ds((2 * j + g) * LANES, LANES)],
                    sems.at[len(copies)],
                ))
        fetch(0)
        run_all(copies)
        for step, shift in enumerate(order):
            fetched(step).wait()
            if step + 1 < rows:
                fetch(step + 1)

            def tile(j, carry, step=step, shift=shift):
                both = jnp.dot(
                    block[step % 2],
                    stack[:, pl.ds(pl.multiple_of(j * 2 * LANES, 2 * LANES), 2 * LANES)],
                    preferred_element_type=jnp.float32,
                )
                gate, up = both[:, :LANES], both[:, LANES:]
                outs[shift][:, pl.ds(pl.multiple_of(j * LANES, LANES), LANES)] = (
                    jax.nn.silu(gate) * up
                ).astype(jnp.bfloat16)
                return carry

            lax.fori_loop(0, tiles, tile, 0)

    moved = 2 * (rows * mine * features + features * 2 * wide + rows * mine * wide)
    return pl.pallas_call(
        body,
        out_shape=[jax.ShapeDtypeStruct((mine, wide), jnp.bfloat16)] * rows,
        in_specs=[ANY] * (rows + 2 + len(held) + len(after)),
        out_specs=[pl.BlockSpec(memory_space=pltpu.VMEM)] * rows,
        scratch_shapes=[
            pltpu.VMEM((features, 2 * wide), gate_weight.dtype),
            pltpu.VMEM((2, mine, features), tokens[0].dtype),
            pltpu.SemaphoreType.DMA((len(held) + 2 * tiles,)),
            pltpu.SemaphoreType.DMA((2,)),
        ],
        compiler_params=pltpu.CompilerParams(vmem_limit_bytes=GRANT),
        cost_estimate=pl.CostEstimate(
            flops=4 * rows * mine * features * wide, bytes_accessed=moved, transcendentals=rows * mine * wide
        ),
        name="product",
    )(*tokens, gate_weight, up_weight, *[value for *_, value in held], *after)


def by_step(rows):
    sources = []
    for z in range(rows):
        above = [z + step for step in range(1, rows - z)]
        below = [z - step for step in range(1, z + 1)]
        sources.append([z] + (above + below if 2 * z < rows else below + above))
    return sources


def pick(choices, after):
    rows, like = lax.axis_size("row"), choices[0][1]

    def body(*refs):
        out, sem = refs[-2:]
        z = lax.axis_index("row")
        copies = [pltpu.make_async_copy(ref, out, sem) for ref, _ in zip(refs, choices)]
        for copy, (places, _) in zip(copies, choices):
            for place in places:
                pl.when(z == place)(copy.start)
        copies[0].wait()

    return pl.pallas_call(
        body,
        out_shape=jax.ShapeDtypeStruct(like.shape, like.dtype),
        in_specs=[ANY] * (len(choices) + len(after)),
        out_specs=pl.BlockSpec(memory_space=pltpu.VMEM),
        scratch_shapes=[pltpu.SemaphoreType.DMA],
        compiler_params=pltpu.CompilerParams(vmem_limit_bytes=GRANT),
        cost_estimate=pl.CostEstimate(flops=0, bytes_accessed=4 * like.size, transcendentals=0),
        name="pick",
    )(*[value for _, value in choices], *after)


def place(blocks, mine, ff, onto=None):
    rows = lax.axis_size("row")
    width = ff // rows
    known = [] if onto is None else [onto]

    def body(*refs):
        refs, out, slots, sems = refs[len(known):], refs[len(known) + len(blocks)], refs[-2 - len(blocks):-2], refs[-2:]
        z = lax.axis_index("row")
        loads, stores = [], []
        for n, (ref, slot, (shift, low, value)) in enumerate(zip(refs, slots, blocks)):
            came = lax.rem(z + rows - shift, rows)
            start = pl.multiple_of(came * width + low, LANES)
            loads.append(pltpu.make_async_copy(ref, slot, sems[0].at[n]))
            stores.append(pltpu.make_async_copy(slot, out.at[:, pl.ds(start, value.shape[1])], sems[1].at[n]))
        for load in loads:
            load.start()
        for load, store in zip(loads, stores):
            load.wait()
            store.start()
        for store in stores:
            store.wait()

    values = [value for _, _, value in blocks]
    return pl.pallas_call(
        body,
        out_shape=jax.ShapeDtypeStruct((mine, ff), jnp.bfloat16),
        in_specs=[ANY] * (len(known) + len(blocks)),
        out_specs=ANY,
        scratch_shapes=[pltpu.VMEM(value.shape, value.dtype) for value in values]
        + [pltpu.SemaphoreType.DMA((len(blocks),))] * 2,
        input_output_aliases={0: 0} if known else {},
        compiler_params=pltpu.CompilerParams(vmem_limit_bytes=GRANT),
        cost_estimate=pl.CostEstimate(
            flops=0, bytes_accessed=4 * sum(value.size for value in values), transcendentals=0
        ),
        name="place",
    )(*known, *values)


def in_tiles(tokens, gate_weight, up_weight):
    rows, parts = lax.axis_size("row"), lax.axis_size("parts")
    mine, ff = tokens.shape[0], gate_weight.shape[1]
    width = ff // rows
    units = width // LANES

    edges = [0]
    for piece in range(len(PIECES)):
        edge = units * sum(PIECES[:piece + 1]) // sum(PIECES) * LANES
        if edge > edges[-1]:
            edges.append(edge)
    spans = list(zip(edges[:-1], edges[1:]))

    def tokens_of():
        lower, upper = [tokens], [tokens]
        for step in range(1, rows):
            lower.append(lax.ppermute(lower[-1], "row", [(i, i + 1) for i in range(step - 1, rows - 1)]))
            upper.append(lax.ppermute(upper[-1], "row", [(i, i - 1) for i in range(1, rows - step + 1)]))
        z = lax.axis_index("row")
        before = {1: sent[:1], rows - 1: arrived[:1] + sent[1:3]}
        for slot in range(rows):
            chosen = {}
            for here, sources in enumerate(by_step(rows)):
                chosen.setdefault(sources[slot] - here, []).append(here)
            choices = [
                (places, upper[offset] if offset > 0 else lower[-offset]) for offset, places in chosen.items()
            ]
            if len(choices) == 2:
                (places, first), (_, second) = choices
                here = sum([z == place for place in places[1:]], start=z == places[0])
                value = jnp.where(here, first, second)
            else:
                value = pick(choices, []) if slot else tokens
            if slot in before:
                value = hold(value, before[slot])
            whole.append(lax.all_gather(value, "col", axis=1, tiled=True))

    def weights(shift, low, high, users):
        after = sent[-1:] + arrived[:len(sent) - 2][-1:] * (len(sent) > 2) + swapped[:len(sent) - 3][-1:] * (len(sent) > 3)
        sent.append(pack(gate_weight, up_weight, shift, low, high - low, after))
        arrived.append(lax.ppermute(sent[-1], "row", around(rows, shift)))
        came = hold(arrived[-1], done) if done else arrived[-1]
        for turn in range(parts):
            if turn:
                swapped.append(lax.ppermute(came, "parts", around(parts, -turn)))
            for n in users:
                held[n].append((shift, turn, low, swapped[-1] if turn else came))

    def hidden_of(n, after):
        low, high = spans[n]
        outs = product(whole, gate_weight, up_weight, held[n], low, high - low, mine, after)
        back = [lax.ppermute(outs[shift], "row", around(rows, shift)) for shift in by_distance(rows)]
        blocks.extend((shift, low, value) for shift, value in zip([0] + by_distance(rows), [outs[0]] + back))
        done.append(outs[0])
        returned.append(back)

    last = len(spans) - 1
    far, *near = by_distance(rows)
    plan = [(far, 0, spans[max(last - 1, 0)][1], range(max(last, 1)))]
    for n, (low, high) in enumerate(spans):
        plan += [(shift, low, high, [n]) for shift in near]
        if n == 0 < last:
            plan.append((far, *spans[last], [last]))
    sent, arrived, swapped, done, returned, blocks = [], [], [], [], [], []
    held = [[] for _ in spans]
    whole = []
    for step in plan:
        if last and len(sent) == max(len(plan) - 3, 3):
            hidden_of(0, [])
        weights(*step)
        if len(sent) == min(3, max(len(plan) - 3, 3)):
            tokens_of()
    for n in range(min(last, 1), last + 1):
        hidden_of(n, done[-1:] + (returned[n - 2][:1] if n > 1 else []))
    early = len(blocks) - rows if last else len(blocks)
    out = place(blocks[:early], mine, ff)
    return place(blocks[early:], mine, ff, out) if last else out


def at_once(tokens, gate_weight, up_weight):
    rows, parts = lax.axis_size("row"), lax.axis_size("parts")
    y = lax.axis_index("parts")
    mine, ff = tokens.shape[0], gate_weight.shape[1]
    depth = gate_weight.shape[0]
    share, width = depth // parts, ff // rows

    whole = lax.all_gather(lax.all_gather(tokens, "row", axis=0, tiled=True), "col", axis=1, tiled=True)
    everyone = whole.shape[0]
    by_share = whole.reshape(everyone, rows, parts, share)
    sent = jnp.stack([
        lax.dynamic_slice(w, (y * share, 0), (share, ff)).reshape(share, rows, width).transpose(1, 0, 2)
        for w in (gate_weight, up_weight)
    ])
    held = lax.all_to_all(sent, "row", 1, 1, tiled=True)
    gate = up = 0.0
    for turn in range(parts):
        features = lax.dynamic_index_in_dim(by_share, (y + turn) % parts, 2, keepdims=False)
        features = features.reshape(everyone, rows * share)
        block = lax.ppermute(held, "parts", around(parts, -turn)) if turn else held
        block = block.reshape(2, rows * share, width)
        gate += jnp.dot(features, block[0], preferred_element_type=jnp.float32)
        up += jnp.dot(features, block[1], preferred_element_type=jnp.float32)
    done = (jax.nn.silu(gate) * up).astype(jnp.bfloat16)
    back = lax.all_to_all(done.reshape(rows, mine, width), "row", 0, 0, tiled=True)
    return back.transpose(1, 0, 2).reshape(mine, ff)


def on_device(tokens, gate_weight, up_weight):
    rows, parts = lax.axis_size("row"), lax.axis_size("parts")
    aligned = (
        gate_weight.shape[1] % (rows * LANES) == 0
        and gate_weight.shape[0] % (parts * 16) == 0
        and tokens.shape[0] % 16 == 0
    )
    return (in_tiles if aligned else at_once)(tokens, gate_weight, up_weight)


def solution(mesh):
    placed = (P(("parts", "row"), "col"), P("row", "col"), P("row", "col"))
    return jax.shard_map(
        on_device, mesh=mesh, in_specs=placed, out_specs=P(("parts", "row"), "col"), check_vma=False
    )
```
